32 devices in a mesh: src: 4 (over z), row: 8 (over y, x, core).
Axes of the slice: x: 2, y: 2, z: 4, core: 2. Of those that a mesh axis runs over, the one named last changes fastest.
Arguments:
- spec_re: bfloat16 [1024, 1024], P('row'), may hold values from -18 to 18
- spec_im: bfloat16 [1024, 1024], P('row'), may hold values from -18 to 18
- target: float32 [1024, 1024], P('row'), may hold values from 0.3 to 1.5
- weights: float32 [32], P('src'), may hold values from 0.25 to 2.5
- cent_row: int32 [32], P('src'), may hold values from 128 to 895
- cent_col: int32 [32], P('src'), may hold values from 128 to 895
Outputs:
- grad_re: float32 [1024, 1024], P('row')
- grad_im: float32 [1024, 1024], P('row')
The draws below stay inside these ranges and needn't reach their ends.
Inputs may be any that keep to these rules, and one draw needn't show every extreme that they name: Every pupil disk of radius 128 about (cent_row, cent_col) lies inside the band.
All inputs are finite; a program needn't handle non-finite values.
Results may differ from the reference program's by a relative error of at most 0.0072.
Values may be sent and summed in bfloat16 or wider, within the bound.
A program may use at most 128 MiB of HBM per device.

```python
import math
import jax
import jax.numpy as jnp
from jax import lax

BAND = 1024
RAD = 128
POINTS = 32


def with_ends(drawn, key, least, high):
    dims = drawn.shape
    place = [jax.random.randint(jax.random.fold_in(key, axis), (), 0, dims[axis]) for axis in range(len(dims))]
    drawn = drawn.at[tuple(place)].set(least)
    longest = dims.index(max(dims))
    place[longest] = (place[longest] + 1) % dims[longest]
    return drawn.at[tuple(place)].set(high)


def levels(stream_key, dims, pieces, least, high):
    level = 1.0
    for dim, shards_of in pieces:
        steps = jax.random.uniform(jax.random.fold_in(jax.random.fold_in(stream_key, 6), dim), (shards_of,), jnp.float32, least / len(pieces), high / len(pieces))
        level = level * jnp.repeat(jnp.exp(steps), dims[dim] // shards_of).reshape((-1,) + (1,) * (len(dims) - 1 - dim))
    return level


def normal_values(own_key, shape, deviation, limit, cuts=(), kind=jnp.bfloat16):
    level = levels(own_key, shape, cuts, -0.22, 0.18) if cuts else 1.0
    result = jax.random.normal(own_key, shape, jnp.float32) * deviation * level
    return jnp.minimum(jnp.maximum(result, -limit), limit).astype(kind)


def setup_inputs(seed: int = 0) -> dict:
    keys = jax.random.split(jax.random.key(seed), 7)
    spec_re = normal_values(keys[0], (BAND, BAND), 3.0, 18.0, ((0, 8),))
    spec_im = normal_values(keys[1], (BAND, BAND), 3.0, 18.0, ((0, 8),))
    target = jnp.clip(0.3 + 1.2 * jax.random.uniform(keys[2], (BAND, BAND), jnp.float32) ** levels(keys[2], (BAND, BAND), ((0, 8),), -0.2, 0.2), 0.3, 1.5)
    weights = jnp.clip(jnp.exp(math.log(2.5) - 2.3025851 * jax.random.uniform(keys[3], (POINTS,), jnp.float32) ** levels(keys[3], (POINTS,), ((0, 4),), -0.2, 0.2)), 0.25, 2.5)
    cent_row = with_ends(jax.random.randint(keys[4], (POINTS,), RAD, BAND - RAD), jax.random.fold_in(keys[4], 1), RAD, (BAND - RAD) - 1).astype(jnp.int32)
    cent_col = with_ends(jax.random.randint(keys[5], (POINTS,), RAD, BAND - RAD), jax.random.fold_in(keys[5], 1), RAD, (BAND - RAD) - 1).astype(jnp.int32)
    return {"spec_re": spec_re, "spec_im": spec_im, "target": target, "weights": weights, "cent_row": cent_row, "cent_col": cent_col}


def make_tables(band):
    position = jnp.arange(band, dtype=jnp.int32)
    phase = position[:, None] * position[None, :] % band
    angle = phase.astype(jnp.float32) * (2.0 * math.pi / band)
    factor = 1.0 / math.sqrt(band)
    return ((jnp.cos(angle) * factor).astype(jnp.bfloat16), (jnp.sin(angle) * factor).astype(jnp.bfloat16))

def reference(spec_re, spec_im, target, weights, cent_row, cent_col):
    band = spec_re.shape[0]
    window = 2 * RAD + 1
    cosine, sine = make_tables(band)
    offsets = jnp.arange(window, dtype=jnp.int32) - RAD
    inside_disk = offsets[:, None] ** 2 + offsets[None, :] ** 2 <= RAD * RAD
    zero_value = jnp.zeros((), jnp.bfloat16)

    def point_field(point):
        first_row = (cent_row[point] - RAD).astype(jnp.int32)
        first_col = (cent_col[point] - RAD).astype(jnp.int32)
        masked_re = jnp.where(inside_disk, lax.dynamic_slice(spec_re, (first_row, first_col), (window, window)), zero_value)
        masked_im = jnp.where(inside_disk, lax.dynamic_slice(spec_im, (first_row, first_col), (window, window)), zero_value)
        cos_col = lax.dynamic_slice_in_dim(cosine, first_col, window, 0)
        sin_col = lax.dynamic_slice_in_dim(sine, first_col, window, 0)
        cos_row = lax.dynamic_slice_in_dim(cosine, first_row, window, 0)
        sin_row = lax.dynamic_slice_in_dim(sine, first_row, window, 0)
        col_re = (jnp.dot(masked_re, cos_col, preferred_element_type=jnp.float32) - jnp.dot(masked_im, sin_col, preferred_element_type=jnp.float32)).astype(jnp.bfloat16)
        col_im = (jnp.dot(masked_re, sin_col, preferred_element_type=jnp.float32) + jnp.dot(masked_im, cos_col, preferred_element_type=jnp.float32)).astype(jnp.bfloat16)
        field_re = jnp.dot(col_re.T, cos_row, preferred_element_type=jnp.float32) - jnp.dot(col_im.T, sin_row, preferred_element_type=jnp.float32)
        field_im = jnp.dot(col_re.T, sin_row, preferred_element_type=jnp.float32) + jnp.dot(col_im.T, cos_row, preferred_element_type=jnp.float32)
        return (field_re, field_im, first_row, first_col, cos_col, sin_col, cos_row, sin_row)

    def add_power(accumulated, point):
        field_re, field_im = point_field(point)[:2]
        return (accumulated + weights[point] * (field_re * field_re + field_im * field_im), None)
    points_all = jnp.arange(POINTS, dtype=jnp.int32)
    power_sum, _ = lax.scan(add_power, jnp.zeros((band, band), jnp.float32), points_all)
    intensity = power_sum / POINTS
    mismatch = intensity - target

    def add_gradient(carry, point):
        total_re, total_im = carry
        field_re, field_im, first_row, first_col, cos_col, sin_col, cos_row, sin_row = point_field(point)
        grad_fre = (2.0 * weights[point] * mismatch * field_re).astype(jnp.bfloat16)
        grad_fim = (2.0 * weights[point] * mismatch * field_im).astype(jnp.bfloat16)
        adj_re = (jnp.dot(grad_fre, cos_row.T, preferred_element_type=jnp.float32) + jnp.dot(grad_fim, sin_row.T, preferred_element_type=jnp.float32)).astype(jnp.bfloat16)
        adj_im = (jnp.dot(grad_fim, cos_row.T, preferred_element_type=jnp.float32) - jnp.dot(grad_fre, sin_row.T, preferred_element_type=jnp.float32)).astype(jnp.bfloat16)
        term_re = jnp.dot(adj_re.T, cos_col.T, preferred_element_type=jnp.float32) + jnp.dot(adj_im.T, sin_col.T, preferred_element_type=jnp.float32)
        term_im = jnp.dot(adj_im.T, cos_col.T, preferred_element_type=jnp.float32) - jnp.dot(adj_re.T, sin_col.T, preferred_element_type=jnp.float32)
        term_re = jnp.where(inside_disk, term_re, jnp.zeros((), jnp.float32))
        term_im = jnp.where(inside_disk, term_im, jnp.zeros((), jnp.float32))
        old_re = lax.dynamic_slice(total_re, (first_row, first_col), (window, window))
        old_im = lax.dynamic_slice(total_im, (first_row, first_col), (window, window))
        total_re = lax.dynamic_update_slice(total_re, old_re + term_re, (first_row, first_col))
        total_im = lax.dynamic_update_slice(total_im, old_im + term_im, (first_row, first_col))
        return ((total_re, total_im), None)
    empty_grid = jnp.zeros((band, band), jnp.float32)
    (grad_re, grad_im), _ = lax.scan(add_gradient, (empty_grid, empty_grid), points_all)
    return (grad_re, grad_im)
```

```python
import functools
import math

import jax
import jax.numpy as jnp
import numpy as np
from jax import lax
from jax.experimental import pallas as pl
from jax.experimental.pallas import tpu as pltpu
from jax.sharding import PartitionSpec as P

RAD = 128
LANES = 128
RADIX = 4
WIN_Q = 80
WIN_L = 384


def host_tables(band):
    position = np.arange(band, dtype=np.int64)
    phase = position[:, None] * position[None, :] % band
    angle = phase.astype(np.float32) * np.float32(2.0 * math.pi / band)
    factor = np.float32(1.0 / math.sqrt(band))
    return (
        (np.cos(angle) * factor).astype(jnp.bfloat16),
        (np.sin(angle) * factor).astype(jnp.bfloat16),
    )


def times_i(value):
    return -value[1], value[0]


def add(a, b):
    return a[0] + b[0], a[1] + b[1]


def sub(a, b):
    return a[0] - b[0], a[1] - b[1]


def main_kernel(
    total_points,
    own_rows,
    cent_row_ref,
    cent_col_ref,
    weight_ref,
    spec_ref,
    narrow_ref,
    wide_ref,
    back_ref,
    target_ref,
    out_ref,
    band_ref,
    field_ref,
    adj_ref,
    power_ref,
    grad_ref,
):
    slots = LANES // own_rows
    quarter = spec_ref.shape[2]
    groups = total_points // slots
    wide_rows = RADIX * WIN_Q

    def window(point):
        centre_row = cent_row_ref[point]
        centre_col = cent_col_ref[point]
        first_q = pl.multiple_of((centre_row - RAD) // (RADIX * 16) * 16, 16)
        first_l = pl.multiple_of((centre_col - RAD) // LANES * LANES, LANES)
        shape = (RADIX, WIN_Q, LANES)
        row_gap = (
            lax.broadcasted_iota(jnp.int32, shape, 1) * RADIX
            + lax.broadcasted_iota(jnp.int32, shape, 0)
            + (first_q * RADIX - centre_row)
        ).astype(jnp.float32)
        room = float(RAD * RAD) - row_gap * row_gap
        lane = lax.broadcasted_iota(jnp.int32, (1, 1, LANES), 2)
        masks = []
        for block in range(WIN_L // LANES):
            gap = (lane + (first_l + block * LANES - centre_col)).astype(jnp.float32)
            masks.append(gap * gap <= room)
        return first_q, first_l, masks

    def slot_lanes(slot):
        lane = lax.broadcasted_iota(jnp.int32, (1, 1, LANES), 2)
        return (lane // own_rows == slot).astype(jnp.float32).astype(jnp.bfloat16)

    band_ref[...] = jnp.zeros_like(band_ref)
    grad_ref[...] = jnp.zeros_like(grad_ref)

    def spread(point, carry):
        first_q, first_l, masks = window(point)
        inside = jnp.concatenate(
            [mask.astype(jnp.float32).astype(jnp.bfloat16) for mask in masks], axis=-1
        )
        rows = pl.ds(first_q, WIN_Q)
        cols = pl.ds(first_l, WIN_L)
        masked = jnp.concatenate(
            [
                (spec_ref[part, :, rows, cols] * inside).reshape(wide_rows, WIN_L)
                for part in range(2)
            ],
            axis=1,
        )
        table = jnp.concatenate([narrow_ref[0, :, cols], narrow_ref[1, :, cols]], axis=1)
        product = lax.dot_general(
            masked, table, (((1,), (1,)), ((), ())), preferred_element_type=jnp.float32
        ).astype(jnp.bfloat16)
        product = product.reshape(RADIX, WIN_Q, 2 * LANES)
        chosen = slot_lanes(point % slots)
        real = product[:, :, :LANES] * chosen
        imag = product[:, :, LANES:] * chosen
        base = pl.multiple_of(point // slots * (2 * LANES), 2 * LANES)
        low = pl.ds(base, LANES)
        high = pl.ds(base + LANES, LANES)
        rows_i = pl.ds(quarter + first_q, WIN_Q)
        band_ref[:, rows, low] += real
        band_ref[:, rows, high] += imag
        band_ref[:, rows_i, low] -= imag
        band_ref[:, rows_i, high] += real
        return carry

    lax.fori_loop(0, total_points, spread, 0)

    power_ref[...] = jnp.zeros_like(power_ref)

    def forward(group, carry):
        base = pl.multiple_of(group * (2 * LANES), 2 * LANES)
        cols = pl.ds(base, 2 * LANES)
        parts = []
        for residue in range(RADIX):
            product = jnp.dot(
                wide_ref[residue], band_ref[residue, :, cols], preferred_element_type=jnp.float32
            )
            parts.append((product[:, :LANES], product[:, LANES:]))
        even, odd = add(parts[0], parts[2]), add(parts[1], parts[3])
        even_gap, odd_gap = sub(parts[0], parts[2]), times_i(sub(parts[1], parts[3]))
        fields = [add(even, odd), add(even_gap, odd_gap), sub(even, odd), sub(even_gap, odd_gap)]
        weight = weight_ref[group]
        for index, (real, imag) in enumerate(fields):
            field_ref[index, :, pl.ds(base, LANES)] = real
            field_ref[index, :, pl.ds(base + LANES, LANES)] = imag
            power_ref[index] += weight * (real * real + imag * imag)
        return carry

    lax.fori_loop(0, groups, forward, 0)

    for index in range(RADIX):
        power = power_ref[index]
        shift = own_rows
        while shift < LANES:
            power = power + pltpu.roll(power, shift, 1)
            shift *= 2
        power_ref[index] = power * (2.0 / total_points) - 2.0 * target_ref[index]

    def backward(group, carry):
        base = pl.multiple_of(group * (2 * LANES), 2 * LANES)
        weight = weight_ref[group]
        grads = []
        for index in range(RADIX):
            scale = weight * power_ref[index]
            grads.append(
                (
                    scale * field_ref[index, :, pl.ds(base, LANES)],
                    scale * field_ref[index, :, pl.ds(base + LANES, LANES)],
                )
            )
        even, odd = add(grads[0], grads[2]), add(grads[1], grads[3])
        even_gap, odd_gap = sub(grads[0], grads[2]), times_i(sub(grads[1], grads[3]))
        folded = [add(even, odd), sub(even_gap, odd_gap), sub(even, odd), add(even_gap, odd_gap)]
        for residue, (real, imag) in enumerate(folded):
            real = real.astype(jnp.bfloat16)
            imag = imag.astype(jnp.bfloat16)
            operand = jnp.concatenate(
                [jnp.concatenate([real, imag], axis=1), jnp.concatenate([imag, -real], axis=1)],
                axis=0,
            )
            adj_ref[residue, :, pl.ds(base, 2 * LANES)] = jnp.dot(
                back_ref[residue], operand, preferred_element_type=jnp.float32
            ).astype(jnp.bfloat16)
        return carry

    lax.fori_loop(0, groups, backward, 0)

    def collect(point, carry):
        first_q, first_l, masks = window(point)
        rows = pl.ds(first_q, WIN_Q)
        cols = pl.ds(first_l, WIN_L)
        base = pl.multiple_of(point // slots * (2 * LANES), 2 * LANES)
        chosen = slot_lanes(point % slots)
        adjoint = adj_ref[:, rows, pl.ds(base, 2 * LANES)]
        adjoint = adjoint * jnp.concatenate([chosen, chosen], axis=-1)
        adjoint = adjoint.reshape(wide_rows, 2 * LANES)
        for part in range(2):
            term = jnp.dot(
                adjoint, narrow_ref[part, :, cols], preferred_element_type=jnp.float32
            ).reshape(RADIX, WIN_Q, WIN_L)
            for block, mask in enumerate(masks):
                where = (part, slice(None), rows, pl.ds(first_l + block * LANES, LANES))
                piece = term[:, :, block * LANES : (block + 1) * LANES]
                grad_ref[where] += jnp.where(mask, piece, 0.0)
        return carry

    lax.fori_loop(0, total_points, collect, 0)
    out_ref[...] = grad_ref[...].astype(out_ref.dtype)


def local(spec_re, spec_im, target, weights, cent_row, cent_col):
    rows_dev, band = spec_re.shape
    groups_src = lax.axis_size("src")
    points_dev = weights.shape[0]
    total_points = points_dev * groups_src
    own_rows = target.shape[0] // groups_src
    slots = LANES // own_rows
    groups = total_points // slots
    quarter = band // RADIX
    cosine, sine = host_tables(band)

    stacked = jnp.stack([spec_re, spec_im], axis=0).reshape(2, rows_dev // RADIX, RADIX, band)
    stacked = stacked.transpose(0, 2, 1, 3)
    spectrum = lax.all_gather(stacked, "row", axis=2, tiled=True)
    points = jnp.stack(
        [weights, cent_row.astype(jnp.float32), cent_col.astype(jnp.float32)], axis=0
    )
    points = lax.all_gather(points, "src", axis=1, tiled=True)
    weights_all = points[0]
    rows_all = points[1].astype(jnp.int32)
    cols_all = points[2].astype(jnp.int32)

    first_own = lax.axis_index("src") * own_rows
    first_row = lax.axis_index("row") * target.shape[0] + first_own
    cos_own = lax.dynamic_slice_in_dim(jnp.asarray(cosine), first_row, own_rows, 0)
    sin_own = lax.dynamic_slice_in_dim(jnp.asarray(sine), first_row, own_rows, 0)
    cos_many = jnp.tile(cos_own, (slots, 1))
    sin_many = jnp.tile(sin_own, (slots, 1))
    narrow = jnp.stack(
        [
            jnp.concatenate([cos_many, sin_many], axis=0),
            jnp.concatenate([-sin_many, cos_many], axis=0),
        ],
        axis=0,
    )
    cos_split = cosine[:quarter].reshape(quarter, quarter, RADIX).transpose(2, 0, 1)
    sin_split = sine[:quarter].reshape(quarter, quarter, RADIX).transpose(2, 0, 1)
    wide = jnp.asarray(np.concatenate([cos_split, sin_split], axis=2))
    back = jnp.asarray(
        np.concatenate([cos_split.transpose(0, 2, 1), sin_split.transpose(0, 2, 1)], axis=2)
    )
    target_own = lax.dynamic_slice_in_dim(target, first_own, own_rows, 0)
    target_own = jnp.tile(target_own, (slots, 1)).T.reshape(RADIX, quarter, LANES)
    weight_rows = jnp.repeat(weights_all, own_rows).reshape(groups, 1, LANES)

    vmem = pl.BlockSpec(memory_space=pltpu.VMEM)
    smem = pl.BlockSpec(memory_space=pltpu.SMEM)
    lanes_all = 2 * own_rows * total_points
    partial = pl.pallas_call(
        functools.partial(main_kernel, total_points, own_rows),
        out_shape=jax.ShapeDtypeStruct((2, RADIX, quarter, band), jnp.bfloat16),
        in_specs=[smem, smem] + [vmem] * 6,
        out_specs=vmem,
        scratch_shapes=[
            pltpu.VMEM((RADIX, 2 * quarter, lanes_all), jnp.bfloat16),
            pltpu.VMEM((RADIX, quarter, lanes_all), jnp.float32),
            pltpu.VMEM((RADIX, quarter, lanes_all), jnp.bfloat16),
            pltpu.VMEM((RADIX, quarter, LANES), jnp.float32),
            pltpu.VMEM((2, RADIX, quarter, band), jnp.float32),
        ],
        compiler_params=pltpu.CompilerParams(vmem_limit_bytes=56 * 1024 * 1024),
    )(rows_all, cols_all, weight_rows, spectrum, narrow, wide, back, target_own)

    summed = lax.psum_scatter(partial, "row", scatter_dimension=2, tiled=True)
    summed = lax.psum(summed, "src").astype(jnp.float32)
    summed = summed.transpose(0, 2, 1, 3).reshape(2, rows_dev, band)
    return summed[0], summed[1]


def solution(mesh):
    return jax.shard_map(
        local,
        mesh=mesh,
        in_specs=(P("row", None), P("row", None), P("row", None), P("src"), P("src"), P("src")),
        out_specs=(P("row", None), P("row", None)),
        check_vma=False,
    )
```

```python
import functools
import math

import jax
import jax.numpy as jnp
import numpy as np
from jax import lax
from jax.experimental import pallas as pl
from jax.experimental.pallas import tpu as pltpu
from jax.sharding import PartitionSpec as P

RAD = 128
LANES = 128
RADIX = 4
WIN_Q = 80
WIN_L = 384


def host_tables(band):
    position = np.arange(band, dtype=np.int64)
    phase = position[:, None] * position[None, :] % band
    angle = phase.astype(np.float32) * np.float32(2.0 * math.pi / band)
    factor = np.float32(1.0 / math.sqrt(band))
    return (
        (np.cos(angle) * factor).astype(jnp.bfloat16),
        (np.sin(angle) * factor).astype(jnp.bfloat16),
    )


def times_i(value):
    return -value[1], value[0]


def add(a, b):
    return a[0] + b[0], a[1] + b[1]


def sub(a, b):
    return a[0] - b[0], a[1] - b[1]


def main_kernel(
    total_points,
    own_rows,
    cent_ref,
    weight_ref,
    spec_ref,
    narrow_ref,
    wide_ref,
    back_ref,
    target_ref,
    out_ref,
    band_ref,
    field_ref,
    adj_ref,
    power_ref,
    grad_ref,
    product_ref,
    scale_ref,
):
    slots = LANES // own_rows
    quarter = spec_ref.shape[1] // RADIX
    points_dev = total_points // cent_ref.shape[0]
    groups = total_points // slots
    wide_rows = RADIX * WIN_Q

    def window(point, split):
        centre_row = cent_ref[point // points_dev, 0, point % points_dev]
        centre_col = cent_ref[point // points_dev, 1, point % points_dev]
        first_q = pl.multiple_of((centre_row - RAD) // (RADIX * 16) * 16, 16)
        first_l = pl.multiple_of((centre_col - RAD) // LANES * LANES, LANES)
        if split:
            shape = (RADIX, WIN_Q, LANES)
            offset = lax.broadcasted_iota(jnp.int32, shape, 1) * RADIX
            offset = offset + lax.broadcasted_iota(jnp.int32, shape, 0)
        else:
            shape = (wide_rows, LANES)
            offset = lax.broadcasted_iota(jnp.int32, shape, 0)
        row_gap = (offset + (first_q * RADIX - centre_row)).astype(jnp.float32)
        room = float(RAD * RAD) - row_gap * row_gap
        flat = (1,) * (len(shape) - 1) + (LANES,)
        lane = lax.broadcasted_iota(jnp.int32, flat, len(shape) - 1)
        masks = []
        for block in range(WIN_L // LANES):
            gap = (lane + (first_l + block * LANES - centre_col)).astype(jnp.float32)
            masks.append(gap * gap <= room)
        return first_q, first_l, masks

    def slot_lanes(slot):
        lane = lax.broadcasted_iota(jnp.int32, (1, LANES), 1)
        return (lane // own_rows == slot).astype(jnp.float32)

    scale_ref[...] = jnp.zeros_like(scale_ref)

    def place_weight(point, carry):
        weight = weight_ref[point // points_dev, 0, point % points_dev]
        scale_ref[point // slots] += weight * slot_lanes(point % slots)
        return carry

    lax.fori_loop(0, total_points, place_weight, 0)

    band_ref[...] = jnp.zeros_like(band_ref)
    grad_ref[...] = jnp.zeros_like(grad_ref)

    def spread(point, carry):
        first_q, first_l, masks = window(point, False)
        inside = jnp.concatenate(
            [mask.astype(jnp.float32).astype(jnp.bfloat16) for mask in masks], axis=-1
        )
        rows_all = pl.ds(pl.multiple_of(first_q * RADIX, 16 * RADIX), wide_rows)
        rows = pl.ds(first_q, WIN_Q)
        cols = pl.ds(first_l, WIN_L)
        masked = jnp.concatenate(
            [spec_ref[part, rows_all, cols] * inside for part in range(2)], axis=1
        )
        table = jnp.concatenate([narrow_ref[0, :, cols], narrow_ref[1, :, cols]], axis=1)
        product = lax.dot_general(
            masked, table, (((1,), (1,)), ((), ())), preferred_element_type=jnp.float32
        )
        product_ref[0] = product[:, :LANES]
        product_ref[1] = product[:, LANES:]
        chosen = slot_lanes(point % slots)
        base = pl.multiple_of(point // slots * (2 * LANES), 2 * LANES)
        low = pl.ds(base, LANES)
        high = pl.ds(base + LANES, LANES)
        rows_i = pl.ds(quarter + first_q, WIN_Q)
        for residue in range(RADIX):
            picked = pl.ds(residue, WIN_Q, stride=RADIX)
            real = (product_ref[0, picked, :] * chosen).astype(jnp.bfloat16)
            imag = (product_ref[1, picked, :] * chosen).astype(jnp.bfloat16)
            band_ref[residue, rows, low] += real
            band_ref[residue, rows, high] += imag
            band_ref[residue, rows_i, low] -= imag
            band_ref[residue, rows_i, high] += real
        return carry

    lax.fori_loop(0, total_points, spread, 0)

    power_ref[...] = jnp.zeros_like(power_ref)

    def forward(group, carry):
        base = pl.multiple_of(group * (2 * LANES), 2 * LANES)
        cols = pl.ds(base, 2 * LANES)
        parts = []
        for residue in range(RADIX):
            product = jnp.dot(
                wide_ref[residue], band_ref[residue, :, cols], preferred_element_type=jnp.float32
            )
            parts.append((product[:, :LANES], product[:, LANES:]))
        even, odd = add(parts[0], parts[2]), add(parts[1], parts[3])
        even_gap, odd_gap = sub(parts[0], parts[2]), times_i(sub(parts[1], parts[3]))
        fields = [add(even, odd), add(even_gap, odd_gap), sub(even, odd), sub(even_gap, odd_gap)]
        weight = scale_ref[group]
        for index, (real, imag) in enumerate(fields):
            field_ref[index, :, pl.ds(base, LANES)] = real
            field_ref[index, :, pl.ds(base + LANES, LANES)] = imag
            power_ref[index] += weight * (real * real + imag * imag)
        return carry

    lax.fori_loop(0, groups, forward, 0)

    for index in range(RADIX):
        power = power_ref[index]
        shift = own_rows
        while shift < LANES:
            power = power + pltpu.roll(power, shift, 1)
            shift *= 2
        power_ref[index] = power * (2.0 / total_points) - 2.0 * target_ref[index]

    def backward(group, carry):
        base = pl.multiple_of(group * (2 * LANES), 2 * LANES)
        weight = scale_ref[group]
        grads = []
        for index in range(RADIX):
            scale = weight * power_ref[index]
            grads.append(
                (
                    scale * field_ref[index, :, pl.ds(base, LANES)],
                    scale * field_ref[index, :, pl.ds(base + LANES, LANES)],
                )
            )
        even, odd = add(grads[0], grads[2]), add(grads[1], grads[3])
        even_gap, odd_gap = sub(grads[0], grads[2]), times_i(sub(grads[1], grads[3]))
        folded = [add(even, odd), sub(even_gap, odd_gap), sub(even, odd), add(even_gap, odd_gap)]
        for residue, (real, imag) in enumerate(folded):
            real = real.astype(jnp.bfloat16)
            imag = imag.astype(jnp.bfloat16)
            operand = jnp.concatenate(
                [jnp.concatenate([real, imag], axis=1), jnp.concatenate([imag, -real], axis=1)],
                axis=0,
            )
            adj_ref[residue, :, pl.ds(base, 2 * LANES)] = jnp.dot(
                back_ref[residue], operand, preferred_element_type=jnp.float32
            ).astype(jnp.bfloat16)
        return carry

    lax.fori_loop(0, groups, backward, 0)

    def collect(point, carry):
        first_q, first_l, masks = window(point, True)
        rows = pl.ds(first_q, WIN_Q)
        cols = pl.ds(first_l, WIN_L)
        base = pl.multiple_of(point // slots * (2 * LANES), 2 * LANES)
        chosen = slot_lanes(point % slots).astype(jnp.bfloat16)
        adjoint = adj_ref[:, rows, pl.ds(base, 2 * LANES)]
        adjoint = adjoint * jnp.concatenate([chosen, chosen], axis=-1)[None]
        adjoint = adjoint.reshape(wide_rows, 2 * LANES)
        for part in range(2):
            term = jnp.dot(
                adjoint, narrow_ref[part, :, cols], preferred_element_type=jnp.float32
            ).reshape(RADIX, WIN_Q, WIN_L)
            for block, mask in enumerate(masks):
                where = (part, slice(None), rows, pl.ds(first_l + block * LANES, LANES))
                piece = term[:, :, block * LANES : (block + 1) * LANES]
                grad_ref[where] += jnp.where(mask, piece, 0.0)
        return carry

    lax.fori_loop(0, total_points, collect, 0)
    out_ref[...] = grad_ref[...].astype(out_ref.dtype)


def row_place():
    row = lax.axis_index("row")
    core, x, y = row % 2, row // 2 % 2, row // 4
    mate = row + 1 - 2 * core
    across_x = row + 2 - 4 * x
    across_y = row + 4 - 8 * y
    return row, core, x, y, mate, across_x, across_y


def enter(rows, sources):
    barrier = pltpu.get_barrier_semaphore()
    for row in rows:
        pl.semaphore_signal(
            barrier, inc=1, device_id={"row": row}, device_id_type=pl.DeviceIdType.MESH
        )
    for source in sources:
        pl.semaphore_signal(
            barrier, inc=1, device_id={"src": source}, device_id_type=pl.DeviceIdType.MESH
        )
    pl.semaphore_wait(barrier, len(rows) + len(sources))


def gather_kernel(
    sources,
    re_ref,
    im_ref,
    cent_ref,
    weight_ref,
    spec_ref,
    cents_ref,
    weights_ref,
    local_sem,
    send_sem,
    recv_sem,
    point_send_sem,
    point_recv_sem,
):
    row, core, x, y, mate, across_x, across_y = row_place()
    corner = across_x + across_y - row
    mate_step = mate - row
    rows_dev = re_ref.shape[0]
    own = lax.axis_index("src")
    peers = [(own + step) % sources for step in range(1, sources)]
    enter([mate, across_x, across_y], peers)

    def rows_of(device):
        return pl.ds(pl.multiple_of(device * rows_dev, rows_dev), rows_dev)

    keep = [
        pltpu.make_async_copy(re_ref, spec_ref.at[0, rows_of(row), :], local_sem.at[0]),
        pltpu.make_async_copy(im_ref, spec_ref.at[1, rows_of(row), :], local_sem.at[1]),
        pltpu.make_async_copy(cent_ref, cents_ref.at[own], local_sem.at[2]),
        pltpu.make_async_copy(weight_ref, weights_ref.at[own], local_sem.at[3]),
    ]
    for copy in keep:
        copy.start()
    small = []
    for index, peer in enumerate(peers):
        for kind, (source, target) in enumerate(
            [(cent_ref, cents_ref.at[own]), (weight_ref, weights_ref.at[own])]
        ):
            small.append(
                pltpu.make_async_remote_copy(
                    src_ref=source,
                    dst_ref=target,
                    send_sem=point_send_sem.at[kind, index],
                    recv_sem=point_recv_sem.at[kind, index],
                    device_id={"src": peer},
                    device_id_type=pl.DeviceIdType.MESH,
                )
            )
    for copy in small:
        copy.start()

    sent = []

    def send(part, holder, to):
        first = holder is None
        target = spec_ref.at[part, rows_of(row if first else holder), :]
        index = len(sent)
        copy = pltpu.make_async_remote_copy(
            src_ref=(re_ref, im_ref)[part] if first else target,
            dst_ref=target,
            send_sem=send_sem.at[index],
            recv_sem=recv_sem.at[index],
            device_id={"row": to},
            device_id_type=pl.DeviceIdType.MESH,
        )
        copy.start()
        sent.append(copy)
        return copy

    re_x = send(0, None, across_x)
    im_y = send(1, None, across_y)
    im_x = send(1, None, across_x)
    re_y = send(0, None, across_y)
    send(0, None, mate)
    send(1, None, mate)
    re_x.wait_recv()
    re_corner = send(0, across_x, across_y)
    send(0, across_x, mate)
    im_y.wait_recv()
    im_corner = send(1, across_y, across_x)
    send(1, across_y, mate)
    im_x.wait_recv()
    send(1, across_x, mate)
    re_y.wait_recv()
    send(0, across_y, mate)
    re_corner.wait_recv()
    send(0, corner, mate)
    im_corner.wait_recv()
    send(1, corner, mate)
    direct = (re_x, im_y, im_x, re_y, re_corner, im_corner)
    for copy in sent:
        if not any(copy is other for other in direct):
            copy.wait_recv()
    for copy in sent:
        copy.wait_send()
    for copy in small:
        copy.wait()
    for copy in keep:
        copy.wait()


def reduce_kernel(
    sources,
    part_ref,
    out_ref,
    mate_in,
    chip_sum,
    first_re_in,
    first_im_in,
    first_re,
    first_im,
    last_re_in,
    last_im_in,
    left_in,
    right_in,
    chain,
    final_in,
    send_sem,
    recv_sem,
    up_send,
    left_recv,
    right_recv,
    down_send,
    down_recv,
):
    row, core, x, y, mate, across_x, across_y = row_place()
    chunks = part_ref.shape[1]
    own = lax.axis_index("src")
    root = sources // 2
    has_left = jnp.logical_and(own > 0, own <= root)
    has_right = jnp.logical_and(own >= root, own < sources - 1)
    peers = [(own + step) % sources for step in range(1, sources)]
    enter([mate, across_x, across_y], peers)

    @pl.when(jnp.logical_not(has_left))
    def _():
        left_in[...] = jnp.zeros_like(left_in)

    @pl.when(jnp.logical_not(has_right))
    def _():
        right_in[...] = jnp.zeros_like(right_in)

    def wide(value):
        return value.astype(jnp.float32)

    def row_copy(kind, chunk, source, target, to):
        return pltpu.make_async_remote_copy(
            src_ref=source,
            dst_ref=target,
            send_sem=send_sem.at[kind, chunk],
            recv_sem=recv_sem.at[kind, chunk],
            device_id={"row": to},
            device_id_type=pl.DeviceIdType.MESH,
        )

    pair, step_re, step_im, end_re, end_im = {}, {}, {}, {}, {}
    for chunk in range(chunks):
        pair[chunk] = row_copy(
            0, chunk, part_ref.at[:, chunk, :, :, 1 - core], mate_in.at[chunk], mate
        )
        pair[chunk].start()

    def add_pair(chunk):
        pair[chunk].wait_recv()
        total = wide(part_ref[:, chunk, :, :, core]) + wide(mate_in[chunk])
        chip_sum[chunk] = total.astype(chip_sum.dtype)
        step_re[chunk] = row_copy(
            1, chunk, chip_sum.at[chunk, 0, :, 1 - x], first_re_in.at[chunk], across_x
        )
        step_im[chunk] = row_copy(
            2, chunk, chip_sum.at[chunk, 1, 1 - y], first_im_in.at[chunk], across_y
        )
        step_re[chunk].start()
        step_im[chunk].start()

    def add_first(chunk):
        step_re[chunk].wait_recv()
        total = wide(chip_sum[chunk, 0, :, x]) + wide(first_re_in[chunk])
        first_re[chunk] = total.astype(first_re.dtype)
        end_re[chunk] = row_copy(
            3, chunk, first_re.at[chunk, 1 - y], last_re_in.at[chunk], across_y
        )
        end_re[chunk].start()
        step_im[chunk].wait_recv()
        total = wide(chip_sum[chunk, 1, y]) + wide(first_im_in[chunk])
        first_im[chunk] = total.astype(first_im.dtype)
        end_im[chunk] = row_copy(
            4, chunk, first_im.at[chunk, 1 - x], last_im_in.at[chunk], across_x
        )
        end_im[chunk].start()

    def src_copy(source, target, sent, received, to):
        return pltpu.make_async_remote_copy(
            src_ref=source,
            dst_ref=target,
            send_sem=sent,
            recv_sem=received,
            device_id={"src": to},
            device_id_type=pl.DeviceIdType.MESH,
        )

    after = jnp.minimum(own + 1, sources - 1)
    before = jnp.maximum(own - 1, 0)

    def to_right(chunk):
        return src_copy(
            chain.at[chunk], left_in.at[chunk], up_send.at[chunk], left_recv.at[chunk], after
        )

    def to_left(chunk):
        return src_copy(
            chain.at[chunk], right_in.at[chunk], up_send.at[chunk], right_recv.at[chunk], before
        )

    def down_left(chunk, source):
        return src_copy(
            source.at[chunk],
            final_in.at[chunk],
            down_send.at[0, chunk],
            down_recv.at[chunk],
            before,
        )

    def down_right(chunk, source):
        return src_copy(
            source.at[chunk],
            final_in.at[chunk],
            down_send.at[1, chunk],
            down_recv.at[chunk],
            after,
        )

    def add_last(chunk):
        end_re[chunk].wait_recv()
        end_im[chunk].wait_recv()

        @pl.when(has_left)
        def _():
            to_right(chunk).wait_recv()

        @pl.when(has_right)
        def _():
            to_left(chunk).wait_recv()

        real = wide(first_re[chunk, y]) + wide(last_re_in[chunk])
        imag = wide(first_im[chunk, x]) + wide(last_im_in[chunk])
        for part, total in enumerate((real, imag)):
            total = total + wide(left_in[chunk, part]) + wide(right_in[chunk, part])
            chain[chunk, part] = total.astype(chain.dtype)

        @pl.when(own < root)
        def _():
            to_right(chunk).start()

        @pl.when(own > root)
        def _():
            to_left(chunk).start()

        @pl.when(own == root)
        def _():
            if root > 0:
                down_left(chunk, chain).start()
            if root < sources - 1:
                down_right(chunk, chain).start()
            out_ref[:, chunk] = chain[chunk]

    def spread_final(chunk):
        @pl.when(own < root)
        def _():
            down_left(chunk, final_in).wait_recv()

            @pl.when(own > 0)
            def _():
                down_left(chunk, final_in).start()

            out_ref[:, chunk] = final_in[chunk]

        @pl.when(own > root)
        def _():
            down_right(chunk, final_in).wait_recv()

            @pl.when(own < sources - 1)
            def _():
                down_right(chunk, final_in).start()

            out_ref[:, chunk] = final_in[chunk]

    stages = ((add_pair, 0), (add_first, 1), (add_last, 2), (spread_final, 4))
    for time in range(chunks + 4):
        for stage, lag in stages:
            if 0 <= time - lag < chunks:
                stage(time - lag)

    for chunk in range(chunks):
        for group in (pair, step_re, step_im, end_re, end_im):
            group[chunk].wait_send()

        @pl.when(own < root)
        def _():
            to_right(chunk).wait_send()

            @pl.when(own > 0)
            def _():
                down_left(chunk, final_in).wait_send()

        @pl.when(own > root)
        def _():
            to_left(chunk).wait_send()

            @pl.when(own < sources - 1)
            def _():
                down_right(chunk, final_in).wait_send()

        @pl.when(own == root)
        def _():
            if root > 0:
                down_left(chunk, chain).wait_send()
            if root < sources - 1:
                down_right(chunk, chain).wait_send()


def gather_all(spec_re, spec_im, cents, weights, sources, kernels):
    rows_dev, band = spec_re.shape
    if not kernels:
        spectrum = lax.all_gather(jnp.stack([spec_re, spec_im]), "row", axis=1, tiled=True)
        return spectrum, lax.all_gather(cents, "src"), lax.all_gather(weights, "src")
    hbm = pl.BlockSpec(memory_space=pl.ANY)
    vmem = pl.BlockSpec(memory_space=pltpu.VMEM)
    dma = pltpu.SemaphoreType.DMA
    return pl.pallas_call(
        functools.partial(gather_kernel, sources),
        out_shape=(
            jax.ShapeDtypeStruct((2, rows_dev * lax.axis_size("row"), band), spec_re.dtype),
            jax.ShapeDtypeStruct((sources,) + cents.shape, cents.dtype),
            jax.ShapeDtypeStruct((sources,) + weights.shape, weights.dtype),
        ),
        in_specs=[hbm, hbm, vmem, vmem],
        out_specs=(hbm, vmem, vmem),
        scratch_shapes=[
            dma((4,)),
            dma((14,)),
            dma((14,)),
            dma((2, max(sources - 1, 1))),
            dma((2, max(sources - 1, 1))),
        ],
        compiler_params=pltpu.CompilerParams(collective_id=0, has_side_effects=True),
    )(spec_re, spec_im, cents, weights)


def reduce_all(partial, sources, kernels):
    _, residues, quarter, band = partial.shape
    if not kernels:
        summed = lax.psum_scatter(partial, "row", scatter_dimension=2, tiled=True)
        return lax.psum(summed, "src")
    own = quarter // lax.axis_size("row")
    partial = partial.reshape(2, residues, 2, 2, 2, own, band)
    vmem = pl.BlockSpec(memory_space=pltpu.VMEM)
    dma = pltpu.SemaphoreType.DMA

    def buffer(*lead):
        return pltpu.VMEM((residues,) + lead + (own, band), partial.dtype)

    return pl.pallas_call(
        functools.partial(reduce_kernel, sources),
        out_shape=jax.ShapeDtypeStruct((2, residues, own, band), partial.dtype),
        in_specs=[vmem],
        out_specs=vmem,
        scratch_shapes=[
            buffer(2, 2, 2),
            buffer(2, 2, 2),
            buffer(2),
            buffer(2),
            buffer(2),
            buffer(2),
            buffer(),
            buffer(),
            buffer(2),
            buffer(2),
            buffer(2),
            buffer(2),
            dma((5, residues)),
            dma((5, residues)),
            dma((residues,)),
            dma((residues,)),
            dma((residues,)),
            dma((2, residues)),
            dma((residues,)),
        ],
        compiler_params=pltpu.CompilerParams(
            collective_id=1, has_side_effects=True, vmem_limit_bytes=40 * 1024 * 1024
        ),
    )(partial)


def local(spec_re, spec_im, target, weights, cent_row, cent_col):
    rows_dev, band = spec_re.shape
    groups_src = lax.axis_size("src")
    points_dev = weights.shape[0]
    total_points = points_dev * groups_src
    own_rows = target.shape[0] // groups_src
    slots = LANES // own_rows
    groups = total_points // slots
    quarter = band // RADIX
    cosine, sine = host_tables(band)

    kernels = lax.axis_size("row") == 8 and rows_dev % (RADIX * 16) == 0
    cents = jnp.stack([cent_row, cent_col], axis=0)
    cents = jnp.pad(cents, ((0, 6), (0, LANES - points_dev)))
    weights_wide = jnp.pad(weights[None], ((0, 7), (0, LANES - points_dev)))
    spectrum, cents_all, weights_all = gather_all(
        spec_re, spec_im, cents, weights_wide, groups_src, kernels
    )

    first_own = lax.axis_index("src") * own_rows
    first_row = lax.axis_index("row") * target.shape[0] + first_own
    cos_own = lax.dynamic_slice_in_dim(jnp.asarray(cosine), first_row, own_rows, 0)
    sin_own = lax.dynamic_slice_in_dim(jnp.asarray(sine), first_row, own_rows, 0)
    cos_many = jnp.tile(cos_own, (slots, 1))
    sin_many = jnp.tile(sin_own, (slots, 1))
    narrow = jnp.stack(
        [
            jnp.concatenate([cos_many, sin_many], axis=0),
            jnp.concatenate([-sin_many, cos_many], axis=0),
        ],
        axis=0,
    )
    cos_split = cosine[:quarter].reshape(quarter, quarter, RADIX).transpose(2, 0, 1)
    sin_split = sine[:quarter].reshape(quarter, quarter, RADIX).transpose(2, 0, 1)
    wide = jnp.asarray(np.concatenate([cos_split, sin_split], axis=2))
    back = jnp.asarray(
        np.concatenate([cos_split.transpose(0, 2, 1), sin_split.transpose(0, 2, 1)], axis=2)
    )
    target_own = lax.dynamic_slice_in_dim(target, first_own, own_rows, 0)
    target_own = jnp.tile(target_own, (slots, 1)).T.reshape(RADIX, quarter, LANES)

    vmem = pl.BlockSpec(memory_space=pltpu.VMEM)
    smem = pl.BlockSpec(memory_space=pltpu.SMEM)
    lanes_all = 2 * own_rows * total_points
    partial = pl.pallas_call(
        functools.partial(main_kernel, total_points, own_rows),
        out_shape=jax.ShapeDtypeStruct((2, RADIX, quarter, band), jnp.bfloat16),
        in_specs=[smem, smem] + [vmem] * 5,
        out_specs=vmem,
        scratch_shapes=[
            pltpu.VMEM((RADIX, 2 * quarter, lanes_all), jnp.bfloat16),
            pltpu.VMEM((RADIX, quarter, lanes_all), jnp.float32),
            pltpu.VMEM((RADIX, quarter, lanes_all), jnp.bfloat16),
            pltpu.VMEM((RADIX, quarter, LANES), jnp.float32),
            pltpu.VMEM((2, RADIX, quarter, band), jnp.float32),
            pltpu.VMEM((2, RADIX * WIN_Q, LANES), jnp.float32),
            pltpu.VMEM((groups, 1, LANES), jnp.float32),
        ],
        compiler_params=pltpu.CompilerParams(vmem_limit_bytes=56 * 1024 * 1024),
    )(cents_all, weights_all, spectrum, narrow, wide, back, target_own)

    summed = reduce_all(partial, groups_src, kernels).astype(jnp.float32)
    summed = summed.transpose(0, 2, 1, 3).reshape(2, rows_dev, band)
    return summed[0], summed[1]


def solution(mesh):
    return jax.shard_map(
        local,
        mesh=mesh,
        in_specs=(P("row", None), P("row", None), P("row", None), P("src"), P("src"), P("src")),
        out_specs=(P("row", None), P("row", None)),
        check_vma=False,
    )
```

```python
import functools
import math

import jax
import jax.numpy as jnp
import numpy as np
from jax import lax
from jax.experimental import pallas as pl
from jax.experimental.pallas import tpu as pltpu
from jax.sharding import PartitionSpec as P

RAD = 128
LANES = 128
RADIX = 4
WIN_Q = 80
WIN_L = 384


def host_tables(band):
    position = np.arange(band, dtype=np.int64)
    phase = position[:, None] * position[None, :] % band
    angle = phase.astype(np.float32) * np.float32(2.0 * math.pi / band)
    factor = np.float32(1.0 / math.sqrt(band))
    return (
        (np.cos(angle) * factor).astype(jnp.bfloat16),
        (np.sin(angle) * factor).astype(jnp.bfloat16),
    )


def times_i(value):
    return -value[1], value[0]


def add(a, b):
    return a[0] + b[0], a[1] + b[1]


def sub(a, b):
    return a[0] - b[0], a[1] - b[1]


def main_kernel(
    total_points,
    own_rows,
    cent_ref,
    weight_ref,
    spec_ref,
    cos_ref,
    sin_ref,
    wide_ref,
    back_ref,
    target_ref,
    out_ref,
    band_ref,
    field_ref,
    adj_ref,
    power_ref,
    grad_ref,
    product_ref,
    scale_ref,
    narrow_ref,
    aim_ref,
    own_ref,
    own_sem,
):
    slots = LANES // own_rows
    quarter = spec_ref.shape[1] // RADIX
    points_dev = total_points // cent_ref.shape[0]
    groups = total_points // slots
    wide_rows = RADIX * WIN_Q

    def window(point, split):
        centre_row = cent_ref[point // points_dev, 0, point % points_dev]
        centre_col = cent_ref[point // points_dev, 1, point % points_dev]
        first_q = pl.multiple_of((centre_row - RAD) // (RADIX * 16) * 16, 16)
        first_l = pl.multiple_of((centre_col - RAD) // LANES * LANES, LANES)
        if split:
            shape = (RADIX, WIN_Q, LANES)
            offset = lax.broadcasted_iota(jnp.int32, shape, 1) * RADIX
            offset = offset + lax.broadcasted_iota(jnp.int32, shape, 0)
        else:
            shape = (wide_rows, LANES)
            offset = lax.broadcasted_iota(jnp.int32, shape, 0)
        row_gap = (offset + (first_q * RADIX - centre_row)).astype(jnp.float32)
        room = float(RAD * RAD) - row_gap * row_gap
        flat = (1,) * (len(shape) - 1) + (LANES,)
        lane = lax.broadcasted_iota(jnp.int32, flat, len(shape) - 1)
        masks = []
        for block in range(WIN_L // LANES):
            gap = (lane + (first_l + block * LANES - centre_col)).astype(jnp.float32)
            masks.append(gap * gap <= room)
        return first_q, first_l, masks

    def slot_lanes(slot):
        lane = lax.broadcasted_iota(jnp.int32, (1, LANES), 1)
        return (lane // own_rows == slot).astype(jnp.float32)

    scale_ref[...] = jnp.zeros_like(scale_ref)

    def place_weight(point, carry):
        weight = weight_ref[point // points_dev, 0, point % points_dev]
        scale_ref[point // slots] += weight * slot_lanes(point % slots)
        return carry

    lax.fori_loop(0, total_points, place_weight, 0)

    if own_rows % 16 == 0:
        first_own = pl.multiple_of(lax.axis_index("src") * own_rows, own_rows)
        first_row = lax.axis_index("row") * target_ref.shape[0] + first_own
        own = pl.ds(pl.multiple_of(first_row, own_rows), own_rows)
        copies = [
            pltpu.make_async_copy(table.at[own, :], own_ref.at[part], own_sem.at[part])
            for part, table in enumerate((cos_ref, sin_ref))
        ]
        for copy in copies:
            copy.start()
        aim = jnp.concatenate([target_ref[pl.ds(first_own, own_rows), :]] * slots, axis=0).T
        for copy in copies:
            copy.wait()
        for slot in range(slots):
            low = pl.ds(slot * own_rows, own_rows)
            high = pl.ds(LANES + slot * own_rows, own_rows)
            narrow_ref[0, low, :] = own_ref[0]
            narrow_ref[0, high, :] = own_ref[1]
            narrow_ref[1, low, :] = -own_ref[1]
            narrow_ref[1, high, :] = own_ref[0]
    else:
        aim = target_ref[...]
        narrow_ref[0, :LANES, :] = cos_ref[...]
        narrow_ref[0, LANES:, :] = sin_ref[...]
        narrow_ref[1, :LANES, :] = -sin_ref[...]
        narrow_ref[1, LANES:, :] = cos_ref[...]
    aim_ref[...] = aim.reshape(aim_ref.shape)

    band_ref[...] = jnp.zeros_like(band_ref)
    grad_ref[...] = jnp.zeros_like(grad_ref)

    def spread(point, carry):
        first_q, first_l, masks = window(point, False)
        inside = jnp.concatenate(
            [mask.astype(jnp.float32).astype(jnp.bfloat16) for mask in masks], axis=-1
        )
        rows_all = pl.ds(pl.multiple_of(first_q * RADIX, 16 * RADIX), wide_rows)
        rows = pl.ds(first_q, WIN_Q)
        cols = pl.ds(first_l, WIN_L)
        masked = jnp.concatenate(
            [spec_ref[part, rows_all, cols] * inside for part in range(2)], axis=1
        )
        table = jnp.concatenate([narrow_ref[0, :, cols], narrow_ref[1, :, cols]], axis=1)
        product = lax.dot_general(
            masked, table, (((1,), (1,)), ((), ())), preferred_element_type=jnp.float32
        )
        product_ref[0] = product[:, :LANES]
        product_ref[1] = product[:, LANES:]
        chosen = slot_lanes(point % slots)
        base = pl.multiple_of(point // slots * (2 * LANES), 2 * LANES)
        low = pl.ds(base, LANES)
        high = pl.ds(base + LANES, LANES)
        rows_i = pl.ds(quarter + first_q, WIN_Q)
        for residue in range(RADIX):
            picked = pl.ds(residue, WIN_Q, stride=RADIX)
            real = (product_ref[0, picked, :] * chosen).astype(jnp.bfloat16)
            imag = (product_ref[1, picked, :] * chosen).astype(jnp.bfloat16)
            band_ref[residue, rows, low] += real
            band_ref[residue, rows, high] += imag
            band_ref[residue, rows_i, low] -= imag
            band_ref[residue, rows_i, high] += real
        return carry

    lax.fori_loop(0, total_points, spread, 0, unroll=4)

    power_ref[...] = jnp.zeros_like(power_ref)

    def forward(group, carry):
        base = pl.multiple_of(group * (2 * LANES), 2 * LANES)
        cols = pl.ds(base, 2 * LANES)
        parts = []
        for residue in range(RADIX):
            product = jnp.dot(
                wide_ref[residue], band_ref[residue, :, cols], preferred_element_type=jnp.float32
            )
            parts.append((product[:, :LANES], product[:, LANES:]))
        even, odd = add(parts[0], parts[2]), add(parts[1], parts[3])
        even_gap, odd_gap = sub(parts[0], parts[2]), times_i(sub(parts[1], parts[3]))
        fields = [add(even, odd), add(even_gap, odd_gap), sub(even, odd), sub(even_gap, odd_gap)]
        weight = scale_ref[group]
        for index, (real, imag) in enumerate(fields):
            field_ref[index, :, pl.ds(base, LANES)] = real
            field_ref[index, :, pl.ds(base + LANES, LANES)] = imag
            power_ref[index] += weight * (real * real + imag * imag)
        return carry

    lax.fori_loop(0, groups, forward, 0, unroll=2)

    for index in range(RADIX):
        power = power_ref[index]
        shift = own_rows
        while shift < LANES:
            power = power + pltpu.roll(power, shift, 1)
            shift *= 2
        power_ref[index] = power * (2.0 / total_points) - 2.0 * aim_ref[index]

    def backward(group, carry):
        base = pl.multiple_of(group * (2 * LANES), 2 * LANES)
        weight = scale_ref[group]
        grads = []
        for index in range(RADIX):
            scale = weight * power_ref[index]
            grads.append(
                (
                    scale * field_ref[index, :, pl.ds(base, LANES)],
                    scale * field_ref[index, :, pl.ds(base + LANES, LANES)],
                )
            )
        even, odd = add(grads[0], grads[2]), add(grads[1], grads[3])
        even_gap, odd_gap = sub(grads[0], grads[2]), times_i(sub(grads[1], grads[3]))
        folded = [add(even, odd), sub(even_gap, odd_gap), sub(even, odd), add(even_gap, odd_gap)]
        for residue, (real, imag) in enumerate(folded):
            real = real.astype(jnp.bfloat16)
            imag = imag.astype(jnp.bfloat16)
            operand = jnp.concatenate(
                [jnp.concatenate([real, imag], axis=1), jnp.concatenate([imag, -real], axis=1)],
                axis=0,
            )
            adj_ref[residue, :, pl.ds(base, 2 * LANES)] = jnp.dot(
                back_ref[residue], operand, preferred_element_type=jnp.float32
            ).astype(jnp.bfloat16)
        return carry

    lax.fori_loop(0, groups, backward, 0, unroll=2)

    def collect(point, carry):
        first_q, first_l, masks = window(point, True)
        rows = pl.ds(first_q, WIN_Q)
        cols = pl.ds(first_l, WIN_L)
        base = pl.multiple_of(point // slots * (2 * LANES), 2 * LANES)
        chosen = slot_lanes(point % slots).astype(jnp.bfloat16)
        adjoint = adj_ref[:, rows, pl.ds(base, 2 * LANES)]
        adjoint = adjoint * jnp.concatenate([chosen, chosen], axis=-1)[None]
        adjoint = adjoint.reshape(wide_rows, 2 * LANES)
        for part in range(2):
            term = jnp.dot(
                adjoint, narrow_ref[part, :, cols], preferred_element_type=jnp.float32
            ).reshape(RADIX, WIN_Q, WIN_L)
            for block, mask in enumerate(masks):
                where = (part, slice(None), rows, pl.ds(first_l + block * LANES, LANES))
                piece = term[:, :, block * LANES : (block + 1) * LANES]
                grad_ref[where] += jnp.where(mask, piece, 0.0)
        return carry

    lax.fori_loop(0, total_points, collect, 0, unroll=4)
    out_ref[...] = grad_ref[...].astype(out_ref.dtype)


def row_place():
    row = lax.axis_index("row")
    core, x, y = row % 2, row // 2 % 2, row // 4
    mate = row + 1 - 2 * core
    across_x = row + 2 - 4 * x
    across_y = row + 4 - 8 * y
    return row, core, x, y, mate, across_x, across_y


def enter(rows, sources):
    barrier = pltpu.get_barrier_semaphore()
    for row in rows:
        pl.semaphore_signal(
            barrier, inc=1, device_id={"row": row}, device_id_type=pl.DeviceIdType.MESH
        )
    for source in sources:
        pl.semaphore_signal(
            barrier, inc=1, device_id={"src": source}, device_id_type=pl.DeviceIdType.MESH
        )
    pl.semaphore_wait(barrier, len(rows) + len(sources))


def gather_kernel(
    sources,
    re_ref,
    im_ref,
    cent_row_ref,
    cent_col_ref,
    weight_row_ref,
    spec_ref,
    cents_ref,
    weights_ref,
    cent_ref,
    weight_ref,
    local_sem,
    send_sem,
    recv_sem,
    point_send_sem,
    point_recv_sem,
):
    row, core, x, y, mate, across_x, across_y = row_place()
    corner = across_x + across_y - row
    mate_step = mate - row
    rows_dev = re_ref.shape[0]
    own = lax.axis_index("src")
    peers = [(own + step) % sources for step in range(1, sources)]
    points_dev = weight_row_ref.shape[1]
    cent_ref[...] = jnp.zeros_like(cent_ref)
    weight_ref[...] = jnp.zeros_like(weight_ref)
    cent_ref[0:1, 0:points_dev] = cent_row_ref[...]
    cent_ref[1:2, 0:points_dev] = cent_col_ref[...]
    weight_ref[0:1, 0:points_dev] = weight_row_ref[...]
    enter([mate, across_x, across_y], peers)

    def rows_of(device):
        return pl.ds(pl.multiple_of(device * rows_dev, rows_dev), rows_dev)

    keep = [
        pltpu.make_async_copy(re_ref, spec_ref.at[0, rows_of(row), :], local_sem.at[0]),
        pltpu.make_async_copy(im_ref, spec_ref.at[1, rows_of(row), :], local_sem.at[1]),
        pltpu.make_async_copy(cent_ref, cents_ref.at[own], local_sem.at[2]),
        pltpu.make_async_copy(weight_ref, weights_ref.at[own], local_sem.at[3]),
    ]
    for copy in keep:
        copy.start()
    small = []
    for index, peer in enumerate(peers):
        for kind, (source, target) in enumerate(
            [(cent_ref, cents_ref.at[own]), (weight_ref, weights_ref.at[own])]
        ):
            small.append(
                pltpu.make_async_remote_copy(
                    src_ref=source,
                    dst_ref=target,
                    send_sem=point_send_sem.at[kind, index],
                    recv_sem=point_recv_sem.at[kind, index],
                    device_id={"src": peer},
                    device_id_type=pl.DeviceIdType.MESH,
                )
            )
    sent = []

    def send(part, holder, to):
        first = holder is None
        target = spec_ref.at[part, rows_of(row if first else holder), :]
        index = len(sent)
        copy = pltpu.make_async_remote_copy(
            src_ref=(re_ref, im_ref)[part] if first else target,
            dst_ref=target,
            send_sem=send_sem.at[index],
            recv_sem=recv_sem.at[index],
            device_id={"row": to},
            device_id_type=pl.DeviceIdType.MESH,
        )
        copy.start()
        sent.append(copy)
        return copy

    re_x = send(0, None, across_x)
    im_y = send(1, None, across_y)
    im_x = send(1, None, across_x)
    re_y = send(0, None, across_y)
    for copy in small:
        copy.start()
    send(0, None, mate)
    send(1, None, mate)
    re_x.wait_recv()
    re_corner = send(0, across_x, across_y)
    send(0, across_x, mate)
    im_y.wait_recv()
    im_corner = send(1, across_y, across_x)
    send(1, across_y, mate)
    im_x.wait_recv()
    send(1, across_x, mate)
    re_y.wait_recv()
    send(0, across_y, mate)
    re_corner.wait_recv()
    send(0, corner, mate)
    im_corner.wait_recv()
    send(1, corner, mate)
    direct = (re_x, im_y, im_x, re_y, re_corner, im_corner)
    for copy in sent:
        if not any(copy is other for other in direct):
            copy.wait_recv()
    for copy in sent:
        copy.wait_send()
    for copy in small:
        copy.wait()
    for copy in keep:
        copy.wait()


def reduce_kernel(
    sources,
    part_ref,
    out_re_ref,
    out_im_ref,
    plane,
    own_part,
    own_sem,
    mate_in,
    chip_sum,
    first_re_in,
    first_im_in,
    first_re,
    first_im,
    last_re_in,
    last_im_in,
    left_in,
    right_in,
    chain,
    final_in,
    send_sem,
    recv_sem,
    up_send,
    left_recv,
    right_recv,
    down_send,
    down_recv,
):
    row, core, x, y, mate, across_x, across_y = row_place()
    chunks = mate_in.shape[0]
    width = mate_in.shape[-1]
    halves = chunks // part_ref.shape[1]
    own = lax.axis_index("src")
    root = sources // 2
    has_left = jnp.logical_and(own > 0, own <= root)
    has_right = jnp.logical_and(own >= root, own < sources - 1)
    peers = [(own + step) % sources for step in range(1, sources)]
    enter([mate, across_x, across_y], peers)

    @pl.when(jnp.logical_not(has_left))
    def _():
        left_in[...] = jnp.zeros_like(left_in)

    @pl.when(jnp.logical_not(has_right))
    def _():
        right_in[...] = jnp.zeros_like(right_in)

    def wide(value):
        return value.astype(jnp.float32)

    def row_copy(kind, chunk, source, target, to):
        return pltpu.make_async_remote_copy(
            src_ref=source,
            dst_ref=target,
            send_sem=send_sem.at[kind, chunk],
            recv_sem=recv_sem.at[kind, chunk],
            device_id={"row": to},
            device_id_type=pl.DeviceIdType.MESH,
        )

    pair, step_re, step_im, end_re, end_im = {}, {}, {}, {}, {}
    keep = {}
    for chunk in range(chunks):
        residue = chunk // halves
        cols = pl.ds(chunk % halves * width, width)
        pair[chunk] = row_copy(
            0, chunk, part_ref.at[:, residue, :, :, 1 - core, :, cols], mate_in.at[chunk], mate
        )
        pair[chunk].start()
        keep[chunk] = pltpu.make_async_copy(
            part_ref.at[:, residue, :, :, core, :, cols], own_part.at[chunk], own_sem.at[chunk]
        )
        keep[chunk].start()

    def place(chunk, source):
        residue = chunk // halves
        blocks = width // LANES
        rows = pl.ds(residue, source.shape[2], stride=RADIX)
        for part in range(2):
            for block in range(blocks):
                plane[part, chunk % halves * blocks + block, rows, :] = wide(
                    source[chunk, part, :, block * LANES : (block + 1) * LANES]
                )

    def add_pair(chunk):
        keep[chunk].wait()
        pair[chunk].wait_recv()
        total = wide(own_part[chunk]) + wide(mate_in[chunk])
        chip_sum[chunk] = total.astype(chip_sum.dtype)
        step_re[chunk] = row_copy(
            1, chunk, chip_sum.at[chunk, 0, :, 1 - x], first_re_in.at[chunk], across_x
        )
        step_im[chunk] = row_copy(
            2, chunk, chip_sum.at[chunk, 1, 1 - y], first_im_in.at[chunk], across_y
        )
        step_re[chunk].start()
        step_im[chunk].start()

    def add_first(chunk):
        step_re[chunk].wait_recv()
        total = wide(chip_sum[chunk, 0, :, x]) + wide(first_re_in[chunk])
        first_re[chunk] = total.astype(first_re.dtype)
        end_re[chunk] = row_copy(
            3, chunk, first_re.at[chunk, 1 - y], last_re_in.at[chunk], across_y
        )
        end_re[chunk].start()
        step_im[chunk].wait_recv()
        total = wide(chip_sum[chunk, 1, y]) + wide(first_im_in[chunk])
        first_im[chunk] = total.astype(first_im.dtype)
        end_im[chunk] = row_copy(
            4, chunk, first_im.at[chunk, 1 - x], last_im_in.at[chunk], across_x
        )
        end_im[chunk].start()

    def src_copy(source, target, sent, received, to):
        return pltpu.make_async_remote_copy(
            src_ref=source,
            dst_ref=target,
            send_sem=sent,
            recv_sem=received,
            device_id={"src": to},
            device_id_type=pl.DeviceIdType.MESH,
        )

    after = jnp.minimum(own + 1, sources - 1)
    before = jnp.maximum(own - 1, 0)

    def to_right(chunk):
        return src_copy(
            chain.at[chunk], left_in.at[chunk], up_send.at[chunk], left_recv.at[chunk], after
        )

    def to_left(chunk):
        return src_copy(
            chain.at[chunk], right_in.at[chunk], up_send.at[chunk], right_recv.at[chunk], before
        )

    def down_left(chunk, source):
        return src_copy(
            source.at[chunk],
            final_in.at[chunk],
            down_send.at[0, chunk],
            down_recv.at[chunk],
            before,
        )

    def down_right(chunk, source):
        return src_copy(
            source.at[chunk],
            final_in.at[chunk],
            down_send.at[1, chunk],
            down_recv.at[chunk],
            after,
        )

    def add_last(chunk):
        end_re[chunk].wait_recv()
        end_im[chunk].wait_recv()

        @pl.when(has_left)
        def _():
            to_right(chunk).wait_recv()

        @pl.when(has_right)
        def _():
            to_left(chunk).wait_recv()

        real = wide(first_re[chunk, y]) + wide(last_re_in[chunk])
        imag = wide(first_im[chunk, x]) + wide(last_im_in[chunk])
        for part, total in enumerate((real, imag)):
            total = total + wide(left_in[chunk, part]) + wide(right_in[chunk, part])
            chain[chunk, part] = total.astype(chain.dtype)

        @pl.when(own < root)
        def _():
            to_right(chunk).start()

        @pl.when(own > root)
        def _():
            to_left(chunk).start()

        @pl.when(own == root)
        def _():
            if root > 0:
                down_left(chunk, chain).start()
            if root < sources - 1:
                down_right(chunk, chain).start()
            place(chunk, chain)

    def spread_final(chunk):
        @pl.when(own < root)
        def _():
            down_left(chunk, final_in).wait_recv()

            @pl.when(own > 0)
            def _():
                down_left(chunk, final_in).start()

            place(chunk, final_in)

        @pl.when(own > root)
        def _():
            down_right(chunk, final_in).wait_recv()

            @pl.when(own < sources - 1)
            def _():
                down_right(chunk, final_in).start()

            place(chunk, final_in)

    stages = ((add_pair, 0), (add_first, 1), (add_last, 2), (spread_final, 4))
    for time in range(chunks + 4):
        for stage, lag in stages:
            if 0 <= time - lag < chunks:
                stage(time - lag)

    for part, out_ref in enumerate((out_re_ref, out_im_ref)):
        for block in range(plane.shape[1]):
            out_ref[:, block * LANES : (block + 1) * LANES] = plane[part, block]

    for chunk in range(chunks):
        for group in (pair, step_re, step_im, end_re, end_im):
            group[chunk].wait_send()

        @pl.when(own < root)
        def _():
            to_right(chunk).wait_send()

            @pl.when(own > 0)
            def _():
                down_left(chunk, final_in).wait_send()

        @pl.when(own > root)
        def _():
            to_left(chunk).wait_send()

            @pl.when(own < sources - 1)
            def _():
                down_right(chunk, final_in).wait_send()

        @pl.when(own == root)
        def _():
            if root > 0:
                down_left(chunk, chain).wait_send()
            if root < sources - 1:
                down_right(chunk, chain).wait_send()


def gather_all(spec_re, spec_im, cent_row, cent_col, weights, sources, kernels):
    rows_dev, band = spec_re.shape
    points_dev = weights.shape[0]
    if not kernels:
        pad = ((0, 6), (0, LANES - points_dev))
        cents = jnp.pad(jnp.stack([cent_row, cent_col], axis=0), pad)
        weights = jnp.pad(jnp.stack([weights, weights], axis=0), pad)
        spectrum = lax.all_gather(jnp.stack([spec_re, spec_im]), "row", axis=1, tiled=True)
        return spectrum, lax.all_gather(cents, "src"), lax.all_gather(weights, "src")
    tile = (8, LANES)
    hbm = pl.BlockSpec(memory_space=pl.ANY)
    vmem = pl.BlockSpec(memory_space=pltpu.VMEM)
    dma = pltpu.SemaphoreType.DMA
    return pl.pallas_call(
        functools.partial(gather_kernel, sources),
        out_shape=(
            jax.ShapeDtypeStruct((2, rows_dev * lax.axis_size("row"), band), spec_re.dtype),
            jax.ShapeDtypeStruct((sources,) + tile, cent_row.dtype),
            jax.ShapeDtypeStruct((sources,) + tile, weights.dtype),
        ),
        in_specs=[hbm, hbm, vmem, vmem, vmem],
        out_specs=(hbm, vmem, vmem),
        scratch_shapes=[
            pltpu.VMEM(tile, cent_row.dtype),
            pltpu.VMEM(tile, weights.dtype),
            dma((4,)),
            dma((14,)),
            dma((14,)),
            dma((2, max(sources - 1, 1))),
            dma((2, max(sources - 1, 1))),
        ],
        compiler_params=pltpu.CompilerParams(collective_id=0, has_side_effects=True),
    )(spec_re, spec_im, cent_row[None], cent_col[None], weights[None])


def reduce_all(partial, sources, kernels):
    _, residues, quarter, band = partial.shape
    own = quarter // lax.axis_size("row")
    rows_dev = own * residues
    if not kernels:
        summed = lax.psum_scatter(partial, "row", scatter_dimension=2, tiled=True)
        summed = lax.psum(summed, "src").astype(jnp.float32)
        summed = summed.transpose(0, 2, 1, 3).reshape(2, rows_dev, band)
        return summed[0], summed[1]
    halves = 2
    chunks = residues * halves
    partial = partial.reshape(2, residues, 2, 2, 2, own, band)
    vmem = pl.BlockSpec(memory_space=pltpu.VMEM)
    dma = pltpu.SemaphoreType.DMA

    def buffer(*lead):
        return pltpu.VMEM((chunks,) + lead + (own, band // halves), partial.dtype)

    result = jax.ShapeDtypeStruct((rows_dev, band), jnp.float32)
    return pl.pallas_call(
        functools.partial(reduce_kernel, sources),
        out_shape=(result, result),
        in_specs=[pl.BlockSpec(memory_space=pl.ANY)],
        out_specs=(vmem, vmem),
        scratch_shapes=[
            pltpu.VMEM((2, band // LANES, rows_dev, LANES), jnp.float32),
            buffer(2, 2, 2),
            dma((chunks,)),
            buffer(2, 2, 2),
            buffer(2, 2, 2),
            buffer(2),
            buffer(2),
            buffer(2),
            buffer(2),
            buffer(),
            buffer(),
            buffer(2),
            buffer(2),
            buffer(2),
            buffer(2),
            dma((5, chunks)),
            dma((5, chunks)),
            dma((chunks,)),
            dma((chunks,)),
            dma((chunks,)),
            dma((2, chunks)),
            dma((chunks,)),
        ],
        compiler_params=pltpu.CompilerParams(
            collective_id=1, has_side_effects=True, vmem_limit_bytes=40 * 1024 * 1024
        ),
    )(partial)


def local(spec_re, spec_im, target, weights, cent_row, cent_col):
    rows_dev, band = spec_re.shape
    groups_src = lax.axis_size("src")
    points_dev = weights.shape[0]
    total_points = points_dev * groups_src
    own_rows = target.shape[0] // groups_src
    slots = LANES // own_rows
    groups = total_points // slots
    quarter = band // RADIX
    cosine, sine = host_tables(band)

    kernels = lax.axis_size("row") == 8 and rows_dev % (RADIX * 16) == 0
    spectrum, cents_all, weights_all = gather_all(
        spec_re, spec_im, cent_row, cent_col, weights, groups_src, kernels
    )

    cos_own, sin_own, target_own = jnp.asarray(cosine), jnp.asarray(sine), target
    if own_rows % 16:
        first_own = lax.axis_index("src") * own_rows
        first_row = lax.axis_index("row") * target.shape[0] + first_own
        cos_own = lax.dynamic_slice_in_dim(cos_own, first_row, own_rows, 0)
        sin_own = lax.dynamic_slice_in_dim(sin_own, first_row, own_rows, 0)
        cos_own = jnp.tile(cos_own, (slots, 1))
        sin_own = jnp.tile(sin_own, (slots, 1))
        target_own = lax.dynamic_slice_in_dim(target, first_own, own_rows, 0)
        target_own = jnp.tile(target_own, (slots, 1)).T
    cos_split = cosine[:quarter].reshape(quarter, quarter, RADIX).transpose(2, 0, 1)
    sin_split = sine[:quarter].reshape(quarter, quarter, RADIX).transpose(2, 0, 1)
    wide = jnp.asarray(np.concatenate([cos_split, sin_split], axis=2))
    back = jnp.asarray(
        np.concatenate([cos_split.transpose(0, 2, 1), sin_split.transpose(0, 2, 1)], axis=2)
    )

    vmem = pl.BlockSpec(memory_space=pltpu.VMEM)
    table = vmem if own_rows % 16 else pl.BlockSpec(memory_space=pl.ANY)
    smem = pl.BlockSpec(memory_space=pltpu.SMEM)
    lanes_all = 2 * own_rows * total_points
    partial = pl.pallas_call(
        functools.partial(main_kernel, total_points, own_rows),
        out_shape=jax.ShapeDtypeStruct((2, RADIX, quarter, band), jnp.bfloat16),
        in_specs=[smem, smem, vmem, table, table, vmem, vmem, vmem],
        out_specs=vmem,
        scratch_shapes=[
            pltpu.VMEM((RADIX, 2 * quarter, lanes_all), jnp.bfloat16),
            pltpu.VMEM((RADIX, quarter, lanes_all), jnp.float32),
            pltpu.VMEM((RADIX, quarter, lanes_all), jnp.bfloat16),
            pltpu.VMEM((RADIX, quarter, LANES), jnp.float32),
            pltpu.VMEM((2, RADIX, quarter, band), jnp.float32),
            pltpu.VMEM((2, RADIX * WIN_Q, LANES), jnp.float32),
            pltpu.VMEM((groups, 1, LANES), jnp.float32),
            pltpu.VMEM((2, 2 * LANES, band), jnp.bfloat16),
            pltpu.VMEM((RADIX, quarter, LANES), jnp.float32),
            pltpu.VMEM((2, max(own_rows, 16), band), jnp.bfloat16),
            pltpu.SemaphoreType.DMA((2,)),
        ],
        compiler_params=pltpu.CompilerParams(vmem_limit_bytes=56 * 1024 * 1024),
    )(cents_all, weights_all, spectrum, cos_own, sin_own, wide, back, target_own)

    return reduce_all(partial, groups_src, kernels)


def solution(mesh):
    return jax.shard_map(
        local,
        mesh=mesh,
        in_specs=(P("row", None), P("row", None), P("row", None), P("src"), P("src"), P("src")),
        out_specs=(P("row", None), P("row", None)),
        check_vma=False,
    )
```

```python
import functools
import math

import jax
import jax.numpy as jnp
import numpy as np
from jax import lax
from jax.experimental import pallas as pl
from jax.experimental.pallas import tpu as pltpu
from jax.sharding import PartitionSpec as P

RAD = 128
LANES = 128
RADIX = 4
WIN_Q = 80
WIN_L = 384


def host_tables(band):
    position = np.arange(band, dtype=np.int64)
    phase = position[:, None] * position[None, :] % band
    angle = phase.astype(np.float32) * np.float32(2.0 * math.pi / band)
    factor = np.float32(1.0 / math.sqrt(band))
    return (
        (np.cos(angle) * factor).astype(jnp.bfloat16),
        (np.sin(angle) * factor).astype(jnp.bfloat16),
    )


def times_i(value):
    return -value[1], value[0]


def add(a, b):
    return a[0] + b[0], a[1] + b[1]


def sub(a, b):
    return a[0] - b[0], a[1] - b[1]


def main_kernel(
    total_points,
    own_rows,
    cent_ref,
    weight_ref,
    spec_hbm,
    cos_ref,
    sin_ref,
    wide_hbm,
    back_hbm,
    target_ref,
    out_hbm,
    spec_ref,
    wide_ref,
    back_ref,
    out_ref,
    in_sem,
    out_sem,
    band_ref,
    field_ref,
    adj_ref,
    power_ref,
    grad_ref,
    product_ref,
    scale_ref,
    narrow_ref,
    aim_ref,
    own_ref,
    own_sem,
):
    slots = LANES // own_rows
    quarter = spec_ref.shape[1] // RADIX
    points_dev = total_points // cent_ref.shape[0]
    groups = total_points // slots
    wide_rows = RADIX * WIN_Q

    def window(point, split):
        centre_row = cent_ref[point // points_dev, 0, point % points_dev]
        centre_col = cent_ref[point // points_dev, 1, point % points_dev]
        first_q = pl.multiple_of((centre_row - RAD) // (RADIX * 16) * 16, 16)
        first_l = pl.multiple_of((centre_col - RAD) // LANES * LANES, LANES)
        if split:
            shape = (RADIX, WIN_Q, LANES)
            offset = lax.broadcasted_iota(jnp.int32, shape, 1) * RADIX
            offset = offset + lax.broadcasted_iota(jnp.int32, shape, 0)
        else:
            shape = (wide_rows, LANES)
            offset = lax.broadcasted_iota(jnp.int32, shape, 0)
        row_gap = (offset + (first_q * RADIX - centre_row)).astype(jnp.float32)
        room = float(RAD * RAD) - row_gap * row_gap
        flat = (1,) * (len(shape) - 1) + (LANES,)
        lane = lax.broadcasted_iota(jnp.int32, flat, len(shape) - 1)
        masks = []
        for block in range(WIN_L // LANES):
            gap = (lane + (first_l + block * LANES - centre_col)).astype(jnp.float32)
            masks.append(gap * gap <= room)
        return first_q, first_l, masks

    def slot_lanes(slot):
        lane = lax.broadcasted_iota(jnp.int32, (1, LANES), 1)
        return (lane // own_rows == slot).astype(jnp.float32)

    incoming = [
        pltpu.make_async_copy(source, target, in_sem.at[index])
        for index, (source, target) in enumerate(
            ((spec_hbm, spec_ref), (wide_hbm, wide_ref), (back_hbm, back_ref))
        )
    ]
    for copy in incoming:
        copy.start()
    scale_ref[...] = jnp.zeros_like(scale_ref)

    def place_weight(point, carry):
        weight = weight_ref[point // points_dev, 0, point % points_dev]
        scale_ref[point // slots] += weight * slot_lanes(point % slots)
        return carry

    lax.fori_loop(0, total_points, place_weight, 0)

    if own_rows % 16 == 0:
        first_own = pl.multiple_of(lax.axis_index("src") * own_rows, own_rows)
        first_row = lax.axis_index("row") * target_ref.shape[0] + first_own
        own = pl.ds(pl.multiple_of(first_row, own_rows), own_rows)
        copies = [
            pltpu.make_async_copy(table.at[own, :], own_ref.at[part], own_sem.at[part])
            for part, table in enumerate((cos_ref, sin_ref))
        ]
        for copy in copies:
            copy.start()
        aim = jnp.concatenate([target_ref[pl.ds(first_own, own_rows), :]] * slots, axis=0).T
        for copy in copies:
            copy.wait()
        for slot in range(slots):
            low = pl.ds(slot * own_rows, own_rows)
            high = pl.ds(LANES + slot * own_rows, own_rows)
            narrow_ref[0, low, :] = own_ref[0]
            narrow_ref[0, high, :] = own_ref[1]
            narrow_ref[1, low, :] = -own_ref[1]
            narrow_ref[1, high, :] = own_ref[0]
    else:
        aim = target_ref[...]
        narrow_ref[0, :LANES, :] = cos_ref[...]
        narrow_ref[0, LANES:, :] = sin_ref[...]
        narrow_ref[1, :LANES, :] = -sin_ref[...]
        narrow_ref[1, LANES:, :] = cos_ref[...]
    aim_ref[...] = aim.reshape(aim_ref.shape)

    band_ref[...] = jnp.zeros_like(band_ref)
    grad_ref[...] = jnp.zeros_like(grad_ref)

    incoming[0].wait()
    buffers = product_ref.shape[0]

    def spread(step, carry):
        places = []
        for buffer in range(buffers):
            point = step * buffers + buffer
            first_q, first_l, masks = window(point, False)
            inside = jnp.concatenate(
                [mask.astype(jnp.float32).astype(jnp.bfloat16) for mask in masks], axis=-1
            )
            rows_all = pl.ds(pl.multiple_of(first_q * RADIX, 16 * RADIX), wide_rows)
            cols = pl.ds(first_l, WIN_L)
            masked = jnp.concatenate(
                [spec_ref[part, rows_all, cols] * inside for part in range(2)], axis=1
            )
            table = jnp.concatenate([narrow_ref[0, :, cols], narrow_ref[1, :, cols]], axis=1)
            product = lax.dot_general(
                masked, table, (((1,), (1,)), ((), ())), preferred_element_type=jnp.float32
            )
            product_ref[buffer, 0] = product[:, :LANES]
            product_ref[buffer, 1] = product[:, LANES:]
            places.append((point, first_q))
        for buffer, (point, first_q) in enumerate(places):
            chosen = slot_lanes(point % slots)
            base = pl.multiple_of(point // slots * (2 * LANES), 2 * LANES)
            low = pl.ds(base, LANES)
            high = pl.ds(base + LANES, LANES)
            rows = pl.ds(first_q, WIN_Q)
            rows_i = pl.ds(quarter + first_q, WIN_Q)
            for residue in range(RADIX):
                picked = pl.ds(residue, WIN_Q, stride=RADIX)
                real = (product_ref[buffer, 0, picked, :] * chosen).astype(jnp.bfloat16)
                imag = (product_ref[buffer, 1, picked, :] * chosen).astype(jnp.bfloat16)
                band_ref[residue, rows, low] += real
                band_ref[residue, rows, high] += imag
                band_ref[residue, rows_i, low] -= imag
                band_ref[residue, rows_i, high] += real
        return carry

    lax.fori_loop(0, total_points // buffers, spread, 0)
    incoming[1].wait()

    power_ref[...] = jnp.zeros_like(power_ref)

    def forward(group, carry):
        base = pl.multiple_of(group * (2 * LANES), 2 * LANES)
        cols = pl.ds(base, 2 * LANES)
        parts = []
        for residue in range(RADIX):
            product = jnp.dot(
                wide_ref[residue], band_ref[residue, :, cols], preferred_element_type=jnp.float32
            )
            parts.append((product[:, :LANES], product[:, LANES:]))
        even, odd = add(parts[0], parts[2]), add(parts[1], parts[3])
        even_gap, odd_gap = sub(parts[0], parts[2]), times_i(sub(parts[1], parts[3]))
        fields = [add(even, odd), add(even_gap, odd_gap), sub(even, odd), sub(even_gap, odd_gap)]
        weight = scale_ref[group]
        for index, (real, imag) in enumerate(fields):
            field_ref[index, :, pl.ds(base, LANES)] = real
            field_ref[index, :, pl.ds(base + LANES, LANES)] = imag
            power_ref[index] += weight * (real * real + imag * imag)
        return carry

    lax.fori_loop(0, groups, forward, 0, unroll=2)

    for index in range(RADIX):
        power = power_ref[index]
        shift = own_rows
        while shift < LANES:
            power = power + pltpu.roll(power, shift, 1)
            shift *= 2
        power_ref[index] = power * (2.0 / total_points) - 2.0 * aim_ref[index]

    incoming[2].wait()

    def backward(group, carry):
        base = pl.multiple_of(group * (2 * LANES), 2 * LANES)
        weight = scale_ref[group]
        grads = []
        for index in range(RADIX):
            scale = weight * power_ref[index]
            grads.append(
                (
                    scale * field_ref[index, :, pl.ds(base, LANES)],
                    scale * field_ref[index, :, pl.ds(base + LANES, LANES)],
                )
            )
        even, odd = add(grads[0], grads[2]), add(grads[1], grads[3])
        even_gap, odd_gap = sub(grads[0], grads[2]), times_i(sub(grads[1], grads[3]))
        folded = [add(even, odd), sub(even_gap, odd_gap), sub(even, odd), add(even_gap, odd_gap)]
        for residue, (real, imag) in enumerate(folded):
            real = real.astype(jnp.bfloat16)
            imag = imag.astype(jnp.bfloat16)
            operand = jnp.concatenate(
                [jnp.concatenate([real, imag], axis=1), jnp.concatenate([imag, -real], axis=1)],
                axis=0,
            )
            adj_ref[residue, :, pl.ds(base, 2 * LANES)] = jnp.dot(
                back_ref[residue], operand, preferred_element_type=jnp.float32
            ).astype(jnp.bfloat16)
        return carry

    lax.fori_loop(0, groups, backward, 0, unroll=2)

    def collect(point, carry):
        first_q, first_l, masks = window(point, True)
        rows = pl.ds(first_q, WIN_Q)
        cols = pl.ds(first_l, WIN_L)
        base = pl.multiple_of(point // slots * (2 * LANES), 2 * LANES)
        chosen = slot_lanes(point % slots).astype(jnp.bfloat16)
        adjoint = adj_ref[:, rows, pl.ds(base, 2 * LANES)]
        adjoint = adjoint * jnp.concatenate([chosen, chosen], axis=-1)[None]
        adjoint = adjoint.reshape(wide_rows, 2 * LANES)
        for part in range(2):
            term = jnp.dot(
                adjoint, narrow_ref[part, :, cols], preferred_element_type=jnp.float32
            ).reshape(RADIX, WIN_Q, WIN_L)
            for block, mask in enumerate(masks):
                where = (part, slice(None), rows, pl.ds(first_l + block * LANES, LANES))
                piece = term[:, :, block * LANES : (block + 1) * LANES]
                grad_ref[where] += jnp.where(mask, piece, 0.0)
        return carry

    lax.fori_loop(0, total_points, collect, 0, unroll=4)
    leaving = []
    for part in range(2):
        for residue in range(RADIX):
            out_ref[part, residue] = grad_ref[part, residue].astype(out_ref.dtype)
            copy = pltpu.make_async_copy(
                out_ref.at[part, residue], out_hbm.at[part, residue], out_sem.at[part, residue]
            )
            copy.start()
            leaving.append(copy)
    for copy in leaving:
        copy.wait()


def row_place():
    row = lax.axis_index("row")
    core, x, y = row % 2, row // 2 % 2, row // 4
    mate = row + 1 - 2 * core
    across_x = row + 2 - 4 * x
    across_y = row + 4 - 8 * y
    return row, core, x, y, mate, across_x, across_y


def enter(rows, sources):
    barrier = pltpu.get_barrier_semaphore()
    for row in rows:
        pl.semaphore_signal(
            barrier, inc=1, device_id={"row": row}, device_id_type=pl.DeviceIdType.MESH
        )
    for source in sources:
        pl.semaphore_signal(
            barrier, inc=1, device_id={"src": source}, device_id_type=pl.DeviceIdType.MESH
        )
    pl.semaphore_wait(barrier, len(rows) + len(sources))


def gather_kernel(
    sources,
    re_ref,
    im_ref,
    cent_row_ref,
    cent_col_ref,
    weight_row_ref,
    spec_ref,
    cents_ref,
    weights_ref,
    cent_ref,
    weight_ref,
    local_sem,
    send_sem,
    recv_sem,
    point_send_sem,
    point_recv_sem,
):
    row, core, x, y, mate, across_x, across_y = row_place()
    corner = across_x + across_y - row
    mate_step = mate - row
    rows_dev = re_ref.shape[0]
    own = lax.axis_index("src")
    peers = [(own + step) % sources for step in range(1, sources)]
    points_dev = weight_row_ref.shape[1]
    cent_ref[...] = jnp.zeros_like(cent_ref)
    weight_ref[...] = jnp.zeros_like(weight_ref)
    cent_ref[0:1, 0:points_dev] = cent_row_ref[...]
    cent_ref[1:2, 0:points_dev] = cent_col_ref[...]
    weight_ref[0:1, 0:points_dev] = weight_row_ref[...]
    enter([mate, across_x, across_y], peers)

    parity = own % 2
    partner = own + 1 - 2 * parity
    few = rows_dev * 3 // 8
    most = rows_dev - few
    fetched = (few * parity, most)
    passed = (most * parity, few)
    missing = (most * (1 - parity), few)
    whole = (0, rows_dev)

    def rows_of(device, piece=whole):
        return pl.ds(pl.multiple_of(device * rows_dev + piece[0], 16), piece[1])

    keep = [
        pltpu.make_async_copy(re_ref, spec_ref.at[0, rows_of(row), :], local_sem.at[0]),
        pltpu.make_async_copy(im_ref, spec_ref.at[1, rows_of(row), :], local_sem.at[1]),
        pltpu.make_async_copy(cent_ref, cents_ref.at[own], local_sem.at[2]),
        pltpu.make_async_copy(weight_ref, weights_ref.at[own], local_sem.at[3]),
    ]
    for copy in keep:
        copy.start()
    small = []
    for index, peer in enumerate(peers):
        for kind, (source, target) in enumerate(
            [(cent_ref, cents_ref.at[own]), (weight_ref, weights_ref.at[own])]
        ):
            small.append(
                pltpu.make_async_remote_copy(
                    src_ref=source,
                    dst_ref=target,
                    send_sem=point_send_sem.at[kind, index],
                    recv_sem=point_recv_sem.at[kind, index],
                    device_id={"src": peer},
                    device_id_type=pl.DeviceIdType.MESH,
                )
            )
    sent = []

    def send(part, holder, piece, axis, to):
        target = spec_ref.at[part, rows_of(row if holder is None else holder, piece), :]
        source = target
        if holder is None:
            first = pl.multiple_of(piece[0], 16)
            source = (re_ref, im_ref)[part].at[pl.ds(first, piece[1]), :]
        index = len(sent)
        copy = pltpu.make_async_remote_copy(
            src_ref=source,
            dst_ref=target,
            send_sem=send_sem.at[index],
            recv_sem=recv_sem.at[index],
            device_id={axis: to},
            device_id_type=pl.DeviceIdType.MESH,
        )
        copy.start()
        sent.append(copy)
        return copy

    re_x = send(0, None, fetched, "row", across_x)
    im_y = send(1, None, fetched, "row", across_y)
    im_x = send(1, None, fetched, "row", across_x)
    re_y = send(0, None, fetched, "row", across_y)
    for copy in small:
        copy.start()
    late = [send(part, None, whole, "row", mate) for part in range(2)]
    partner_copies = []

    def pass_on(part, holder):
        partner_copies.append((send(part, holder, passed, "src", partner), part, holder))
        late.append(send(part, holder, fetched, "row", mate))

    re_x.wait_recv()
    re_corner = send(0, across_x, fetched, "row", across_y)
    pass_on(0, across_x)
    im_y.wait_recv()
    im_corner = send(1, across_y, fetched, "row", across_x)
    pass_on(1, across_y)
    im_x.wait_recv()
    pass_on(1, across_x)
    re_y.wait_recv()
    pass_on(0, across_y)
    re_corner.wait_recv()
    pass_on(0, corner)
    im_corner.wait_recv()
    pass_on(1, corner)
    for copy, part, holder in partner_copies:
        copy.wait_recv()
        late.append(send(part, holder, missing, "row", mate))
    for copy in late:
        copy.wait_recv()
    for copy in sent:
        copy.wait_send()
    for copy in small:
        copy.wait()
    for copy in keep:
        copy.wait()


def reduce_kernel(
    sources,
    part_ref,
    out_re_ref,
    out_im_ref,
    plane,
    own_part,
    own_sem,
    mate_in,
    chip_sum,
    first_re_in,
    first_im_in,
    first_re,
    first_im,
    last_re_in,
    last_im_in,
    left_in,
    right_in,
    chain,
    final_in,
    send_sem,
    recv_sem,
    up_send,
    left_recv,
    right_recv,
    down_send,
    down_recv,
):
    row, core, x, y, mate, across_x, across_y = row_place()
    chunks = mate_in.shape[0]
    depth = mate_in.shape[-2]
    halves = chunks // part_ref.shape[1]
    own = lax.axis_index("src")
    root = sources // 2
    leaf = jnp.logical_or(own == 0, own == sources - 1)
    has_left = jnp.logical_and(own > 0, own <= root)
    has_right = jnp.logical_and(own >= root, own < sources - 1)
    peers = [(own + step) % sources for step in range(1, sources)]
    enter([mate, across_x, across_y], peers)

    @pl.when(jnp.logical_not(has_left))
    def _():
        left_in[...] = jnp.zeros_like(left_in)

    @pl.when(jnp.logical_not(has_right))
    def _():
        right_in[...] = jnp.zeros_like(right_in)

    def wide(value):
        return value.astype(jnp.float32)

    def row_copy(kind, chunk, source, target, to):
        return pltpu.make_async_remote_copy(
            src_ref=source,
            dst_ref=target,
            send_sem=send_sem.at[kind, chunk],
            recv_sem=recv_sem.at[kind, chunk],
            device_id={"row": to},
            device_id_type=pl.DeviceIdType.MESH,
        )

    pair, step_re, step_im, end_re, end_im = {}, {}, {}, {}, {}
    keep = {}
    for chunk in range(chunks):
        residue = chunk // halves
        rows = pl.ds(chunk % halves * depth, depth)
        pair[chunk] = row_copy(
            0, chunk, part_ref.at[:, residue, :, :, 1 - core, rows], mate_in.at[chunk], mate
        )
        pair[chunk].start()
        keep[chunk] = pltpu.make_async_copy(
            part_ref.at[:, residue, :, :, core, rows], own_part.at[chunk], own_sem.at[chunk]
        )
        keep[chunk].start()

    def place(chunk, source):
        residue = chunk // halves
        first = residue + chunk % halves * depth * RADIX
        rows = pl.ds(first, depth, stride=RADIX)
        for part in range(2):
            for block in range(plane.shape[1]):
                plane[part, block, rows, :] = wide(
                    source[chunk, part, :, block * LANES : (block + 1) * LANES]
                )

    def add_pair(chunk):
        keep[chunk].wait()
        pair[chunk].wait_recv()
        total = wide(own_part[chunk]) + wide(mate_in[chunk])
        chip_sum[chunk] = total.astype(chip_sum.dtype)
        step_re[chunk] = row_copy(
            1, chunk, chip_sum.at[chunk, 0, :, 1 - x], first_re_in.at[chunk], across_x
        )
        step_im[chunk] = row_copy(
            2, chunk, chip_sum.at[chunk, 1, 1 - y], first_im_in.at[chunk], across_y
        )
        step_re[chunk].start()
        step_im[chunk].start()

    def add_first(chunk):
        step_re[chunk].wait_recv()
        total = wide(chip_sum[chunk, 0, :, x]) + wide(first_re_in[chunk])
        first_re[chunk] = total.astype(first_re.dtype)
        end_re[chunk] = row_copy(
            3, chunk, first_re.at[chunk, 1 - y], last_re_in.at[chunk], across_y
        )
        end_re[chunk].start()
        step_im[chunk].wait_recv()
        total = wide(chip_sum[chunk, 1, y]) + wide(first_im_in[chunk])
        first_im[chunk] = total.astype(first_im.dtype)
        end_im[chunk] = row_copy(
            4, chunk, first_im.at[chunk, 1 - x], last_im_in.at[chunk], across_x
        )
        end_im[chunk].start()

    def src_copy(source, target, sent, received, to):
        return pltpu.make_async_remote_copy(
            src_ref=source,
            dst_ref=target,
            send_sem=sent,
            recv_sem=received,
            device_id={"src": to},
            device_id_type=pl.DeviceIdType.MESH,
        )

    after = jnp.minimum(own + 1, sources - 1)
    before = jnp.maximum(own - 1, 0)

    def to_right(chunk):
        return src_copy(
            chain.at[chunk], left_in.at[chunk], up_send.at[chunk], left_recv.at[chunk], after
        )

    def to_left(chunk):
        return src_copy(
            chain.at[chunk], right_in.at[chunk], up_send.at[chunk], right_recv.at[chunk], before
        )

    def down_left(chunk, source):
        return src_copy(
            source.at[chunk],
            final_in.at[chunk],
            down_send.at[0, chunk],
            down_recv.at[chunk],
            before,
        )

    def down_right(chunk, source):
        return src_copy(
            source.at[chunk],
            final_in.at[chunk],
            down_send.at[1, chunk],
            down_recv.at[chunk],
            after,
        )

    def add_last(chunk):
        end_re[chunk].wait_recv()
        end_im[chunk].wait_recv()

        @pl.when(has_left)
        def _():
            to_right(chunk).wait_recv()

        @pl.when(has_right)
        def _():
            to_left(chunk).wait_recv()

        real = wide(first_re[chunk, y]) + wide(last_re_in[chunk])
        imag = wide(first_im[chunk, x]) + wide(last_im_in[chunk])
        for part, total in enumerate((real, imag)):
            total = total + wide(left_in[chunk, part]) + wide(right_in[chunk, part])
            chain[chunk, part] = total.astype(chain.dtype)

        @pl.when(own < root)
        def _():
            to_right(chunk).start()

        @pl.when(own > root)
        def _():
            to_left(chunk).start()

        @pl.when(own == root)
        def _():
            if root > 0:
                down_left(chunk, chain).start()
            if root < sources - 1:
                down_right(chunk, chain).start()
            place(chunk, chain)

    def pass_final(chunk):
        @pl.when(jnp.logical_and(own < root, own > 0))
        def _():
            down_left(chunk, final_in).wait_recv()
            down_left(chunk, final_in).start()
            place(chunk, final_in)

        @pl.when(jnp.logical_and(own > root, own < sources - 1))
        def _():
            down_right(chunk, final_in).wait_recv()
            down_right(chunk, final_in).start()
            place(chunk, final_in)

    stages = ((add_pair, 0), (add_first, 1), (add_last, 2), (pass_final, 5))
    for time in range(chunks + 5):
        for stage, lag in stages:
            if 0 <= time - lag < chunks:
                stage(time - lag)
    for chunk in range(chunks):

        @pl.when(jnp.logical_and(leaf, own != root))
        def _():
            down_left(chunk, final_in).wait_recv()
            place(chunk, final_in)

    for part, out_ref in enumerate((out_re_ref, out_im_ref)):
        for block in range(plane.shape[1]):
            out_ref[:, block * LANES : (block + 1) * LANES] = plane[part, block]

    for chunk in range(chunks):
        for group in (pair, step_re, step_im, end_re, end_im):
            group[chunk].wait_send()

        @pl.when(own < root)
        def _():
            to_right(chunk).wait_send()

            @pl.when(own > 0)
            def _():
                down_left(chunk, final_in).wait_send()

        @pl.when(own > root)
        def _():
            to_left(chunk).wait_send()

            @pl.when(own < sources - 1)
            def _():
                down_right(chunk, final_in).wait_send()

        @pl.when(own == root)
        def _():
            if root > 0:
                down_left(chunk, chain).wait_send()
            if root < sources - 1:
                down_right(chunk, chain).wait_send()


def gather_all(spec_re, spec_im, cent_row, cent_col, weights, sources, kernels):
    rows_dev, band = spec_re.shape
    points_dev = weights.shape[0]
    if not kernels:
        pad = ((0, 6), (0, LANES - points_dev))
        cents = jnp.pad(jnp.stack([cent_row, cent_col], axis=0), pad)
        weights = jnp.pad(jnp.stack([weights, weights], axis=0), pad)
        spectrum = lax.all_gather(jnp.stack([spec_re, spec_im]), "row", axis=1, tiled=True)
        return spectrum, lax.all_gather(cents, "src"), lax.all_gather(weights, "src")
    tile = (8, LANES)
    hbm = pl.BlockSpec(memory_space=pl.ANY)
    vmem = pl.BlockSpec(memory_space=pltpu.VMEM)
    dma = pltpu.SemaphoreType.DMA
    return pl.pallas_call(
        functools.partial(gather_kernel, sources),
        out_shape=(
            jax.ShapeDtypeStruct((2, rows_dev * lax.axis_size("row"), band), spec_re.dtype),
            jax.ShapeDtypeStruct((sources,) + tile, cent_row.dtype),
            jax.ShapeDtypeStruct((sources,) + tile, weights.dtype),
        ),
        in_specs=[hbm, hbm, vmem, vmem, vmem],
        out_specs=(hbm, vmem, vmem),
        scratch_shapes=[
            pltpu.VMEM(tile, cent_row.dtype),
            pltpu.VMEM(tile, weights.dtype),
            dma((4,)),
            dma((26,)),
            dma((26,)),
            dma((2, max(sources - 1, 1))),
            dma((2, max(sources - 1, 1))),
        ],
        compiler_params=pltpu.CompilerParams(collective_id=0, has_side_effects=True),
    )(spec_re, spec_im, cent_row[None], cent_col[None], weights[None])


def reduce_all(partial, sources, kernels):
    _, residues, quarter, band = partial.shape
    own = quarter // lax.axis_size("row")
    rows_dev = own * residues
    if not kernels:
        summed = lax.psum_scatter(partial, "row", scatter_dimension=2, tiled=True)
        summed = lax.psum(summed, "src").astype(jnp.float32)
        summed = summed.transpose(0, 2, 1, 3).reshape(2, rows_dev, band)
        return summed[0], summed[1]
    halves = 2
    chunks = residues * halves
    partial = partial.reshape(2, residues, 2, 2, 2, own, band)
    vmem = pl.BlockSpec(memory_space=pltpu.VMEM)
    dma = pltpu.SemaphoreType.DMA

    def buffer(*lead):
        return pltpu.VMEM((chunks,) + lead + (own // halves, band), partial.dtype)

    result = jax.ShapeDtypeStruct((rows_dev, band), jnp.float32)
    return pl.pallas_call(
        functools.partial(reduce_kernel, sources),
        out_shape=(result, result),
        in_specs=[pl.BlockSpec(memory_space=pl.ANY)],
        out_specs=(vmem, vmem),
        scratch_shapes=[
            pltpu.VMEM((2, band // LANES, rows_dev, LANES), jnp.float32),
            buffer(2, 2, 2),
            dma((chunks,)),
            buffer(2, 2, 2),
            buffer(2, 2, 2),
            buffer(2),
            buffer(2),
            buffer(2),
            buffer(2),
            buffer(),
            buffer(),
            buffer(2),
            buffer(2),
            buffer(2),
            buffer(2),
            dma((5, chunks)),
            dma((5, chunks)),
            dma((chunks,)),
            dma((chunks,)),
            dma((chunks,)),
            dma((2, chunks)),
            dma((chunks,)),
        ],
        compiler_params=pltpu.CompilerParams(
            collective_id=1, has_side_effects=True, vmem_limit_bytes=61 * 1024 * 1024
        ),
    )(partial)


def local(spec_re, spec_im, target, weights, cent_row, cent_col):
    rows_dev, band = spec_re.shape
    groups_src = lax.axis_size("src")
    points_dev = weights.shape[0]
    total_points = points_dev * groups_src
    own_rows = target.shape[0] // groups_src
    slots = LANES // own_rows
    groups = total_points // slots
    quarter = band // RADIX
    cosine, sine = host_tables(band)

    kernels = lax.axis_size("row") == 8 and groups_src % 2 == 0 and rows_dev % LANES == 0
    spectrum, cents_all, weights_all = gather_all(
        spec_re, spec_im, cent_row, cent_col, weights, groups_src, kernels
    )

    cos_own, sin_own, target_own = jnp.asarray(cosine), jnp.asarray(sine), target
    if own_rows % 16:
        first_own = lax.axis_index("src") * own_rows
        first_row = lax.axis_index("row") * target.shape[0] + first_own
        cos_own = lax.dynamic_slice_in_dim(cos_own, first_row, own_rows, 0)
        sin_own = lax.dynamic_slice_in_dim(sin_own, first_row, own_rows, 0)
        cos_own = jnp.tile(cos_own, (slots, 1))
        sin_own = jnp.tile(sin_own, (slots, 1))
        target_own = lax.dynamic_slice_in_dim(target, first_own, own_rows, 0)
        target_own = jnp.tile(target_own, (slots, 1)).T
    cos_split = cosine[:quarter].reshape(quarter, quarter, RADIX).transpose(2, 0, 1)
    sin_split = sine[:quarter].reshape(quarter, quarter, RADIX).transpose(2, 0, 1)
    wide = jnp.asarray(np.concatenate([cos_split, sin_split], axis=2))
    back = jnp.asarray(
        np.concatenate([cos_split.transpose(0, 2, 1), sin_split.transpose(0, 2, 1)], axis=2)
    )

    vmem = pl.BlockSpec(memory_space=pltpu.VMEM)
    hbm = pl.BlockSpec(memory_space=pl.ANY)
    table = vmem if own_rows % 16 else hbm
    smem = pl.BlockSpec(memory_space=pltpu.SMEM)
    lanes_all = 2 * own_rows * total_points
    partial = pl.pallas_call(
        functools.partial(main_kernel, total_points, own_rows),
        out_shape=jax.ShapeDtypeStruct((2, RADIX, quarter, band), jnp.bfloat16),
        in_specs=[smem, smem, hbm, table, table, hbm, hbm, vmem],
        out_specs=hbm,
        scratch_shapes=[
            pltpu.VMEM(spectrum.shape, spectrum.dtype),
            pltpu.VMEM(wide.shape, wide.dtype),
            pltpu.VMEM(back.shape, back.dtype),
            pltpu.VMEM((2, RADIX, quarter, band), jnp.bfloat16),
            pltpu.SemaphoreType.DMA((3,)),
            pltpu.SemaphoreType.DMA((2, RADIX)),
            pltpu.VMEM((RADIX, 2 * quarter, lanes_all), jnp.bfloat16),
            pltpu.VMEM((RADIX, quarter, lanes_all), jnp.float32),
            pltpu.VMEM((RADIX, quarter, lanes_all), jnp.bfloat16),
            pltpu.VMEM((RADIX, quarter, LANES), jnp.float32),
            pltpu.VMEM((2, RADIX, quarter, band), jnp.float32),
            pltpu.VMEM((4, 2, RADIX * WIN_Q, LANES), jnp.float32),
            pltpu.VMEM((groups, 1, LANES), jnp.float32),
            pltpu.VMEM((2, 2 * LANES, band), jnp.bfloat16),
            pltpu.VMEM((RADIX, quarter, LANES), jnp.float32),
            pltpu.VMEM((2, max(own_rows, 16), band), jnp.bfloat16),
            pltpu.SemaphoreType.DMA((2,)),
        ],
        compiler_params=pltpu.CompilerParams(vmem_limit_bytes=56 * 1024 * 1024),
    )(cents_all, weights_all, spectrum, cos_own, sin_own, wide, back, target_own)

    return reduce_all(partial, groups_src, kernels)


def solution(mesh):
    return jax.shard_map(
        local,
        mesh=mesh,
        in_specs=(P("row", None), P("row", None), P("row", None), P("src"), P("src"), P("src")),
        out_specs=(P("row", None), P("row", None)),
        check_vma=False,
    )
```

```python
import functools
import math

import jax
import jax.numpy as jnp
import numpy as np
from jax import lax
from jax.experimental import pallas as pl
from jax.experimental.pallas import tpu as pltpu
from jax.sharding import PartitionSpec as P

RAD = 128
LANES = 128
RADIX = 4
WIN_Q = 80
WIN_L = 384


def host_tables(band):
    position = np.arange(band, dtype=np.int64)
    phase = position[:, None] * position[None, :] % band
    angle = phase.astype(np.float32) * np.float32(2.0 * math.pi / band)
    factor = np.float32(1.0 / math.sqrt(band))
    return (
        (np.cos(angle) * factor).astype(jnp.bfloat16),
        (np.sin(angle) * factor).astype(jnp.bfloat16),
    )


def times_i(value):
    return -value[1], value[0]


def add(a, b):
    return a[0] + b[0], a[1] + b[1]


def sub(a, b):
    return a[0] - b[0], a[1] - b[1]


def main_kernel(
    total_points,
    own_rows,
    cent_ref,
    weight_ref,
    spec_hbm,
    cos_ref,
    sin_ref,
    wide_hbm,
    back_hbm,
    target_ref,
    out_hbm,
    spec_ref,
    wide_ref,
    back_ref,
    out_ref,
    in_sem,
    out_sem,
    band_ref,
    field_ref,
    adj_ref,
    power_ref,
    grad_ref,
    product_ref,
    scale_ref,
    narrow_ref,
    tall_ref,
    aim_ref,
    own_ref,
    own_sem,
):
    slots = LANES // own_rows
    quarter = spec_ref.shape[1] // RADIX
    points_dev = total_points // cent_ref.shape[0]
    groups = total_points // slots
    wide_rows = RADIX * WIN_Q

    def window(point, split):
        centre_row = cent_ref[point // points_dev, 0, point % points_dev]
        centre_col = cent_ref[point // points_dev, 1, point % points_dev]
        first_q = pl.multiple_of((centre_row - RAD) // (RADIX * 16) * 16, 16)
        first_l = pl.multiple_of((centre_col - RAD) // LANES * LANES, LANES)
        if split:
            shape = (RADIX, WIN_Q, LANES)
            offset = lax.broadcasted_iota(jnp.int32, shape, 1) * RADIX
            offset = offset + lax.broadcasted_iota(jnp.int32, shape, 0)
        else:
            shape = (wide_rows, LANES)
            offset = lax.broadcasted_iota(jnp.int32, shape, 0)
        row_gap = (offset + (first_q * RADIX - centre_row)).astype(jnp.float32)
        room = float(RAD * RAD) - row_gap * row_gap
        flat = (1,) * (len(shape) - 1) + (LANES,)
        lane = lax.broadcasted_iota(jnp.int32, flat, len(shape) - 1)
        masks = []
        for block in range(WIN_L // LANES):
            gap = (lane + (first_l + block * LANES - centre_col)).astype(jnp.float32)
            masks.append(gap * gap <= room)
        return first_q, first_l, masks

    def slot_lanes(slot):
        lane = lax.broadcasted_iota(jnp.int32, (1, LANES), 1)
        return (lane // own_rows == slot).astype(jnp.float32)

    incoming = [
        pltpu.make_async_copy(source, target, in_sem.at[index])
        for index, (source, target) in enumerate(
            ((spec_hbm, spec_ref), (wide_hbm, wide_ref), (back_hbm, back_ref))
        )
    ]
    for copy in incoming:
        copy.start()
    scale_ref[...] = jnp.zeros_like(scale_ref)

    def place_weight(point, carry):
        weight = weight_ref[point // points_dev, 0, point % points_dev]
        scale_ref[point // slots] += weight * slot_lanes(point % slots)
        return carry

    lax.fori_loop(0, total_points, place_weight, 0)

    if own_rows % 16 == 0:
        first_own = pl.multiple_of(lax.axis_index("src") * own_rows, own_rows)
        first_row = lax.axis_index("row") * target_ref.shape[0] + first_own
        own = pl.ds(pl.multiple_of(first_row, own_rows), own_rows)
        copies = [
            pltpu.make_async_copy(table.at[own, :], own_ref.at[part], own_sem.at[part])
            for part, table in enumerate((cos_ref, sin_ref))
        ]
        for copy in copies:
            copy.start()
        aim = jnp.concatenate([target_ref[pl.ds(first_own, own_rows), :]] * slots, axis=0).T
        for copy in copies:
            copy.wait()
        for slot in range(slots):
            low = pl.ds(slot * own_rows, own_rows)
            high = pl.ds(LANES + slot * own_rows, own_rows)
            narrow_ref[0, low, :] = own_ref[0]
            narrow_ref[0, high, :] = own_ref[1]
            narrow_ref[1, low, :] = -own_ref[1]
            narrow_ref[1, high, :] = own_ref[0]
    else:
        aim = target_ref[...]
        narrow_ref[0, :LANES, :] = cos_ref[...]
        narrow_ref[0, LANES:, :] = sin_ref[...]
        narrow_ref[1, :LANES, :] = -sin_ref[...]
        narrow_ref[1, LANES:, :] = cos_ref[...]
    aim_ref[...] = aim.reshape(aim_ref.shape)
    for part in range(2):
        tall_ref[part] = narrow_ref[part].astype(jnp.float32).T.astype(tall_ref.dtype)

    band_ref[...] = jnp.zeros_like(band_ref)
    grad_ref[...] = jnp.zeros_like(grad_ref)

    incoming[0].wait()
    buffers = product_ref.shape[0]

    def spread(step, carry):
        places = []
        for buffer in range(buffers):
            point = step * buffers + buffer
            first_q, first_l, masks = window(point, False)
            inside = jnp.concatenate(
                [mask.astype(jnp.float32).astype(jnp.bfloat16) for mask in masks], axis=-1
            )
            rows_all = pl.ds(pl.multiple_of(first_q * RADIX, 16 * RADIX), wide_rows)
            cols = pl.ds(first_l, WIN_L)
            masked = jnp.concatenate(
                [spec_ref[part, rows_all, cols] * inside for part in range(2)], axis=1
            )
            table = jnp.concatenate([tall_ref[0, cols, :], tall_ref[1, cols, :]], axis=0)
            product = jnp.dot(masked, table, preferred_element_type=jnp.float32)
            product_ref[buffer, 0] = product[:, :LANES]
            product_ref[buffer, 1] = product[:, LANES:]
            places.append((point, first_q))
        for buffer, (point, first_q) in enumerate(places):
            chosen = slot_lanes(point % slots)
            base = pl.multiple_of(point // slots * (2 * LANES), 2 * LANES)
            low = pl.ds(base, LANES)
            high = pl.ds(base + LANES, LANES)
            rows = pl.ds(first_q, WIN_Q)
            rows_i = pl.ds(quarter + first_q, WIN_Q)
            for residue in range(RADIX):
                picked = pl.ds(residue, WIN_Q, stride=RADIX)
                real = (product_ref[buffer, 0, picked, :] * chosen).astype(jnp.bfloat16)
                imag = (product_ref[buffer, 1, picked, :] * chosen).astype(jnp.bfloat16)
                band_ref[residue, rows, low] += real
                band_ref[residue, rows, high] += imag
                band_ref[residue, rows_i, low] -= imag
                band_ref[residue, rows_i, high] += real
        return carry

    lax.fori_loop(0, total_points // buffers, spread, 0)
    incoming[1].wait()

    power_ref[...] = jnp.zeros_like(power_ref)

    def forward(group, carry):
        base = pl.multiple_of(group * (2 * LANES), 2 * LANES)
        cols = pl.ds(base, 2 * LANES)
        parts = []
        for residue in range(RADIX):
            product = jnp.dot(
                wide_ref[residue], band_ref[residue, :, cols], preferred_element_type=jnp.float32
            )
            parts.append((product[:, :LANES], product[:, LANES:]))
        even, odd = add(parts[0], parts[2]), add(parts[1], parts[3])
        even_gap, odd_gap = sub(parts[0], parts[2]), times_i(sub(parts[1], parts[3]))
        fields = [add(even, odd), add(even_gap, odd_gap), sub(even, odd), sub(even_gap, odd_gap)]
        weight = scale_ref[group]
        for index, (real, imag) in enumerate(fields):
            field_ref[index, :, pl.ds(base, LANES)] = real
            field_ref[index, :, pl.ds(base + LANES, LANES)] = imag
            power_ref[index] += weight * (real * real + imag * imag)
        return carry

    lax.fori_loop(0, groups, forward, 0, unroll=2)

    for index in range(RADIX):
        power = power_ref[index]
        shift = own_rows
        while shift < LANES:
            power = power + pltpu.roll(power, shift, 1)
            shift *= 2
        power_ref[index] = power * (2.0 / total_points) - 2.0 * aim_ref[index]

    incoming[2].wait()

    def backward(group, carry):
        base = pl.multiple_of(group * (2 * LANES), 2 * LANES)
        weight = scale_ref[group]
        grads = []
        for index in range(RADIX):
            scale = weight * power_ref[index]
            grads.append(
                (
                    scale * field_ref[index, :, pl.ds(base, LANES)],
                    scale * field_ref[index, :, pl.ds(base + LANES, LANES)],
                )
            )
        even, odd = add(grads[0], grads[2]), add(grads[1], grads[3])
        even_gap, odd_gap = sub(grads[0], grads[2]), times_i(sub(grads[1], grads[3]))
        folded = [add(even, odd), sub(even_gap, odd_gap), sub(even, odd), add(even_gap, odd_gap)]
        for residue, (real, imag) in enumerate(folded):
            real = real.astype(jnp.bfloat16)
            imag = imag.astype(jnp.bfloat16)
            operand = jnp.concatenate(
                [jnp.concatenate([real, imag], axis=1), jnp.concatenate([imag, -real], axis=1)],
                axis=0,
            )
            adj_ref[residue, :, pl.ds(base, 2 * LANES)] = jnp.dot(
                back_ref[residue], operand, preferred_element_type=jnp.float32
            ).astype(jnp.bfloat16)
        return carry

    lax.fori_loop(0, groups, backward, 0, unroll=2)

    def collect(point, carry):
        first_q, first_l, masks = window(point, True)
        rows = pl.ds(first_q, WIN_Q)
        cols = pl.ds(first_l, WIN_L)
        base = pl.multiple_of(point // slots * (2 * LANES), 2 * LANES)
        chosen = slot_lanes(point % slots).astype(jnp.bfloat16)
        adjoint = adj_ref[:, rows, pl.ds(base, 2 * LANES)]
        adjoint = adjoint * jnp.concatenate([chosen, chosen], axis=-1)[None]
        adjoint = adjoint.reshape(wide_rows, 2 * LANES)
        for part in range(2):
            term = jnp.dot(
                adjoint, narrow_ref[part, :, cols], preferred_element_type=jnp.float32
            ).reshape(RADIX, WIN_Q, WIN_L)
            for block, mask in enumerate(masks):
                where = (part, slice(None), rows, pl.ds(first_l + block * LANES, LANES))
                piece = term[:, :, block * LANES : (block + 1) * LANES]
                grad_ref[where] += jnp.where(mask, piece, 0.0)
        return carry

    lax.fori_loop(0, total_points, collect, 0, unroll=4)
    leaving = []
    for part in range(2):
        for residue in range(RADIX):
            out_ref[part, residue] = grad_ref[part, residue].astype(out_ref.dtype)
            copy = pltpu.make_async_copy(
                out_ref.at[part, residue], out_hbm.at[part, residue], out_sem.at[part, residue]
            )
            copy.start()
            leaving.append(copy)
    for copy in leaving:
        copy.wait()


def row_place():
    row = lax.axis_index("row")
    core, x, y = row % 2, row // 2 % 2, row // 4
    mate = row + 1 - 2 * core
    across_x = row + 2 - 4 * x
    across_y = row + 4 - 8 * y
    return row, core, x, y, mate, across_x, across_y


def enter(rows, sources):
    barrier = pltpu.get_barrier_semaphore()
    for row in rows:
        pl.semaphore_signal(
            barrier, inc=1, device_id={"row": row}, device_id_type=pl.DeviceIdType.MESH
        )
    for source in sources:
        pl.semaphore_signal(
            barrier, inc=1, device_id={"src": source}, device_id_type=pl.DeviceIdType.MESH
        )
    pl.semaphore_wait(barrier, len(rows) + len(sources))


def gather_kernel(
    sources,
    re_ref,
    im_ref,
    cent_row_ref,
    cent_col_ref,
    weight_row_ref,
    spec_ref,
    cents_ref,
    weights_ref,
    cent_ref,
    weight_ref,
    local_sem,
    send_sem,
    recv_sem,
    point_send_sem,
    point_recv_sem,
):
    row, core, x, y, mate, across_x, across_y = row_place()
    corner = across_x + across_y - row
    mate_step = mate - row
    rows_dev = re_ref.shape[0]
    own = lax.axis_index("src")
    peers = [(own + step) % sources for step in range(1, sources)]
    points_dev = weight_row_ref.shape[1]
    cent_ref[...] = jnp.zeros_like(cent_ref)
    weight_ref[...] = jnp.zeros_like(weight_ref)
    cent_ref[0:1, 0:points_dev] = cent_row_ref[...]
    cent_ref[1:2, 0:points_dev] = cent_col_ref[...]
    weight_ref[0:1, 0:points_dev] = weight_row_ref[...]
    enter([mate, across_x, across_y], peers)

    parity = own % 2
    partner = own + 1 - 2 * parity
    few = rows_dev * 3 // 8
    most = rows_dev - few
    fetched = (few * parity, most)
    passed = (most * parity, few)
    missing = (most * (1 - parity), few)
    whole = (0, rows_dev)

    def rows_of(device, piece=whole):
        return pl.ds(pl.multiple_of(device * rows_dev + piece[0], 16), piece[1])

    keep = [
        pltpu.make_async_copy(re_ref, spec_ref.at[0, rows_of(row), :], local_sem.at[0]),
        pltpu.make_async_copy(im_ref, spec_ref.at[1, rows_of(row), :], local_sem.at[1]),
        pltpu.make_async_copy(cent_ref, cents_ref.at[own], local_sem.at[2]),
        pltpu.make_async_copy(weight_ref, weights_ref.at[own], local_sem.at[3]),
    ]
    for copy in keep:
        copy.start()
    small = []
    for index, peer in enumerate(peers):
        for kind, (source, target) in enumerate(
            [(cent_ref, cents_ref.at[own]), (weight_ref, weights_ref.at[own])]
        ):
            small.append(
                pltpu.make_async_remote_copy(
                    src_ref=source,
                    dst_ref=target,
                    send_sem=point_send_sem.at[kind, index],
                    recv_sem=point_recv_sem.at[kind, index],
                    device_id={"src": peer},
                    device_id_type=pl.DeviceIdType.MESH,
                )
            )
    sent = []

    def send(part, holder, piece, axis, to):
        target = spec_ref.at[part, rows_of(row if holder is None else holder, piece), :]
        source = target
        if holder is None:
            first = pl.multiple_of(piece[0], 16)
            source = (re_ref, im_ref)[part].at[pl.ds(first, piece[1]), :]
        index = len(sent)
        copy = pltpu.make_async_remote_copy(
            src_ref=source,
            dst_ref=target,
            send_sem=send_sem.at[index],
            recv_sem=recv_sem.at[index],
            device_id={axis: to},
            device_id_type=pl.DeviceIdType.MESH,
        )
        copy.start()
        sent.append(copy)
        return copy

    re_x = send(0, None, fetched, "row", across_x)
    im_y = send(1, None, fetched, "row", across_y)
    im_x = send(1, None, fetched, "row", across_x)
    re_y = send(0, None, fetched, "row", across_y)
    for copy in small:
        copy.start()
    late = [send(part, None, whole, "row", mate) for part in range(2)]
    partner_copies = []

    def pass_on(part, holder):
        partner_copies.append((send(part, holder, passed, "src", partner), part, holder))
        late.append(send(part, holder, fetched, "row", mate))

    re_x.wait_recv()
    re_corner = send(0, across_x, fetched, "row", across_y)
    pass_on(0, across_x)
    im_y.wait_recv()
    im_corner = send(1, across_y, fetched, "row", across_x)
    pass_on(1, across_y)
    im_x.wait_recv()
    pass_on(1, across_x)
    re_y.wait_recv()
    pass_on(0, across_y)
    re_corner.wait_recv()
    pass_on(0, corner)
    im_corner.wait_recv()
    pass_on(1, corner)
    for copy, part, holder in partner_copies:
        copy.wait_recv()
        late.append(send(part, holder, missing, "row", mate))
    for copy in late:
        copy.wait_recv()
    for copy in sent:
        copy.wait_send()
    for copy in small:
        copy.wait()
    for copy in keep:
        copy.wait()


def reduce_kernel(
    sources,
    part_ref,
    out_ref,
    plane,
    own_part,
    own_sem,
    mate_in,
    chip_sum,
    first_re_in,
    first_im_in,
    first_re,
    first_im,
    last_re_in,
    last_im_in,
    left_in,
    right_in,
    chain,
    final_in,
    send_sem,
    recv_sem,
    up_send,
    left_recv,
    right_recv,
    down_send,
    down_recv,
):
    row, core, x, y, mate, across_x, across_y = row_place()
    chunks = mate_in.shape[0]
    depth = mate_in.shape[-2]
    halves = chunks // part_ref.shape[1]
    own = lax.axis_index("src")
    root = sources // 2
    leaf = jnp.logical_or(own == 0, own == sources - 1)
    has_left = jnp.logical_and(own > 0, own <= root)
    has_right = jnp.logical_and(own >= root, own < sources - 1)
    peers = [(own + step) % sources for step in range(1, sources)]
    enter([mate, across_x, across_y], peers)

    @pl.when(jnp.logical_not(has_left))
    def _():
        left_in[...] = jnp.zeros_like(left_in)

    @pl.when(jnp.logical_not(has_right))
    def _():
        right_in[...] = jnp.zeros_like(right_in)

    def wide(value):
        return value.astype(jnp.float32)

    def row_copy(kind, chunk, source, target, to):
        return pltpu.make_async_remote_copy(
            src_ref=source,
            dst_ref=target,
            send_sem=send_sem.at[kind, chunk],
            recv_sem=recv_sem.at[kind, chunk],
            device_id={"row": to},
            device_id_type=pl.DeviceIdType.MESH,
        )

    pair, step_re, step_im, end_re, end_im = {}, {}, {}, {}, {}
    keep = {}
    for chunk in range(chunks):
        residue = chunk // halves
        rows = pl.ds(chunk % halves * depth, depth)
        pair[chunk] = row_copy(
            0, chunk, part_ref.at[:, residue, :, :, 1 - core, rows], mate_in.at[chunk], mate
        )
        keep[chunk] = pltpu.make_async_copy(
            part_ref.at[:, residue, :, :, core, rows], own_part.at[chunk], own_sem.at[chunk]
        )
    ahead = 2
    for chunk in range(ahead):
        pair[chunk].start()
        keep[chunk].start()

    def place(chunk, source):
        residue = chunk // halves
        first = residue + chunk % halves * depth * RADIX
        rows = pl.ds(first, depth, stride=RADIX)
        for part in range(2):
            for block in range(plane.shape[1]):
                plane[part, block, rows, :] = wide(
                    source[chunk, part, :, block * LANES : (block + 1) * LANES]
                )

    def add_pair(chunk):
        keep[chunk].wait()
        pair[chunk].wait_recv()
        if chunk + ahead < chunks:
            pair[chunk + ahead].start()
            keep[chunk + ahead].start()
        total = wide(own_part[chunk]) + wide(mate_in[chunk])
        chip_sum[chunk] = total.astype(chip_sum.dtype)
        step_re[chunk] = row_copy(
            1, chunk, chip_sum.at[chunk, 0, :, 1 - x], first_re_in.at[chunk], across_x
        )
        step_im[chunk] = row_copy(
            2, chunk, chip_sum.at[chunk, 1, 1 - y], first_im_in.at[chunk], across_y
        )
        step_re[chunk].start()
        step_im[chunk].start()

    def add_first(chunk):
        step_re[chunk].wait_recv()
        total = wide(chip_sum[chunk, 0, :, x]) + wide(first_re_in[chunk])
        first_re[chunk] = total.astype(first_re.dtype)
        end_re[chunk] = row_copy(
            3, chunk, first_re.at[chunk, 1 - y], last_re_in.at[chunk], across_y
        )
        end_re[chunk].start()
        step_im[chunk].wait_recv()
        total = wide(chip_sum[chunk, 1, y]) + wide(first_im_in[chunk])
        first_im[chunk] = total.astype(first_im.dtype)
        end_im[chunk] = row_copy(
            4, chunk, first_im.at[chunk, 1 - x], last_im_in.at[chunk], across_x
        )
        end_im[chunk].start()

    def src_copy(source, target, sent, received, to):
        return pltpu.make_async_remote_copy(
            src_ref=source,
            dst_ref=target,
            send_sem=sent,
            recv_sem=received,
            device_id={"src": to},
            device_id_type=pl.DeviceIdType.MESH,
        )

    after = jnp.minimum(own + 1, sources - 1)
    before = jnp.maximum(own - 1, 0)

    def to_right(chunk):
        return src_copy(
            chain.at[chunk], left_in.at[chunk], up_send.at[chunk], left_recv.at[chunk], after
        )

    def to_left(chunk):
        return src_copy(
            chain.at[chunk], right_in.at[chunk], up_send.at[chunk], right_recv.at[chunk], before
        )

    def down_left(chunk, source):
        return src_copy(
            source.at[chunk],
            final_in.at[chunk],
            down_send.at[0, chunk],
            down_recv.at[chunk],
            before,
        )

    def down_right(chunk, source):
        return src_copy(
            source.at[chunk],
            final_in.at[chunk],
            down_send.at[1, chunk],
            down_recv.at[chunk],
            after,
        )

    def add_last(chunk):
        end_re[chunk].wait_recv()
        end_im[chunk].wait_recv()

        @pl.when(has_left)
        def _():
            to_right(chunk).wait_recv()

        @pl.when(has_right)
        def _():
            to_left(chunk).wait_recv()

        real = wide(first_re[chunk, y]) + wide(last_re_in[chunk])
        imag = wide(first_im[chunk, x]) + wide(last_im_in[chunk])
        for part, total in enumerate((real, imag)):
            total = total + wide(left_in[chunk, part]) + wide(right_in[chunk, part])
            chain[chunk, part] = total.astype(chain.dtype)

        @pl.when(own < root)
        def _():
            to_right(chunk).start()

        @pl.when(own > root)
        def _():
            to_left(chunk).start()

        @pl.when(own == root)
        def _():
            if root > 0:
                down_left(chunk, chain).start()
            if root < sources - 1:
                down_right(chunk, chain).start()
            place(chunk, chain)

    def pass_final(chunk):
        @pl.when(jnp.logical_and(own < root, own > 0))
        def _():
            down_left(chunk, final_in).wait_recv()
            down_left(chunk, final_in).start()
            place(chunk, final_in)

        @pl.when(jnp.logical_and(own > root, own < sources - 1))
        def _():
            down_right(chunk, final_in).wait_recv()
            down_right(chunk, final_in).start()
            place(chunk, final_in)

    stages = ((add_pair, 0), (add_first, 1), (add_last, 2), (pass_final, 5))
    for time in range(chunks + 5):
        for stage, lag in stages:
            if 0 <= time - lag < chunks:
                stage(time - lag)
    for chunk in range(chunks):

        @pl.when(jnp.logical_and(leaf, own != root))
        def _():
            down_left(chunk, final_in).wait_recv()
            place(chunk, final_in)

    for part in range(2):
        for block in range(plane.shape[1]):
            cols = slice(block * LANES, (block + 1) * LANES)
            out_ref[part, :, cols] = plane[part, block].astype(out_ref.dtype)

    for chunk in range(chunks):
        for group in (pair, step_re, step_im, end_re, end_im):
            group[chunk].wait_send()

        @pl.when(own < root)
        def _():
            to_right(chunk).wait_send()

            @pl.when(own > 0)
            def _():
                down_left(chunk, final_in).wait_send()

        @pl.when(own > root)
        def _():
            to_left(chunk).wait_send()

            @pl.when(own < sources - 1)
            def _():
                down_right(chunk, final_in).wait_send()

        @pl.when(own == root)
        def _():
            if root > 0:
                down_left(chunk, chain).wait_send()
            if root < sources - 1:
                down_right(chunk, chain).wait_send()


def gather_all(spec_re, spec_im, cent_row, cent_col, weights, sources, kernels):
    rows_dev, band = spec_re.shape
    points_dev = weights.shape[0]
    if not kernels:
        pad = ((0, 6), (0, LANES - points_dev))
        cents = jnp.pad(jnp.stack([cent_row, cent_col], axis=0), pad)
        weights = jnp.pad(jnp.stack([weights, weights], axis=0), pad)
        spectrum = lax.all_gather(jnp.stack([spec_re, spec_im]), "row", axis=1, tiled=True)
        return spectrum, lax.all_gather(cents, "src"), lax.all_gather(weights, "src")
    tile = (8, LANES)
    hbm = pl.BlockSpec(memory_space=pl.ANY)
    vmem = pl.BlockSpec(memory_space=pltpu.VMEM)
    dma = pltpu.SemaphoreType.DMA
    return pl.pallas_call(
        functools.partial(gather_kernel, sources),
        out_shape=(
            jax.ShapeDtypeStruct((2, rows_dev * lax.axis_size("row"), band), spec_re.dtype),
            jax.ShapeDtypeStruct((sources,) + tile, cent_row.dtype),
            jax.ShapeDtypeStruct((sources,) + tile, weights.dtype),
        ),
        in_specs=[hbm, hbm, vmem, vmem, vmem],
        out_specs=(hbm, vmem, vmem),
        scratch_shapes=[
            pltpu.VMEM(tile, cent_row.dtype),
            pltpu.VMEM(tile, weights.dtype),
            dma((4,)),
            dma((26,)),
            dma((26,)),
            dma((2, max(sources - 1, 1))),
            dma((2, max(sources - 1, 1))),
        ],
        compiler_params=pltpu.CompilerParams(collective_id=0, has_side_effects=True),
    )(spec_re, spec_im, cent_row[None], cent_col[None], weights[None])


def reduce_all(partial, sources, kernels):
    _, residues, quarter, band = partial.shape
    own = quarter // lax.axis_size("row")
    rows_dev = own * residues
    if not kernels:
        summed = lax.psum_scatter(partial, "row", scatter_dimension=2, tiled=True)
        summed = lax.psum(summed, "src").astype(jnp.float32)
        summed = summed.transpose(0, 2, 1, 3).reshape(2, rows_dev, band)
        return summed[0], summed[1]
    halves = 2
    chunks = residues * halves
    partial = partial.reshape(2, residues, 2, 2, 2, own, band)
    vmem = pl.BlockSpec(memory_space=pltpu.VMEM)
    dma = pltpu.SemaphoreType.DMA

    def buffer(*lead):
        return pltpu.VMEM((chunks,) + lead + (own // halves, band), partial.dtype)

    summed = pl.pallas_call(
        functools.partial(reduce_kernel, sources),
        out_shape=jax.ShapeDtypeStruct((2, rows_dev, band), partial.dtype),
        in_specs=[pl.BlockSpec(memory_space=pl.ANY)],
        out_specs=vmem,
        scratch_shapes=[
            pltpu.VMEM((2, band // LANES, rows_dev, LANES), jnp.float32),
            buffer(2, 2, 2),
            dma((chunks,)),
            buffer(2, 2, 2),
            buffer(2, 2, 2),
            buffer(2),
            buffer(2),
            buffer(2),
            buffer(2),
            buffer(),
            buffer(),
            buffer(2),
            buffer(2),
            buffer(2),
            buffer(2),
            dma((5, chunks)),
            dma((5, chunks)),
            dma((chunks,)),
            dma((chunks,)),
            dma((chunks,)),
            dma((2, chunks)),
            dma((chunks,)),
        ],
        compiler_params=pltpu.CompilerParams(
            collective_id=1, has_side_effects=True, vmem_limit_bytes=61 * 1024 * 1024
        ),
    )(partial)
    return summed[0].astype(jnp.float32), summed[1].astype(jnp.float32)


def local(spec_re, spec_im, target, weights, cent_row, cent_col):
    rows_dev, band = spec_re.shape
    groups_src = lax.axis_size("src")
    points_dev = weights.shape[0]
    total_points = points_dev * groups_src
    own_rows = target.shape[0] // groups_src
    slots = LANES // own_rows
    groups = total_points // slots
    quarter = band // RADIX
    cosine, sine = host_tables(band)

    kernels = lax.axis_size("row") == 8 and groups_src % 2 == 0 and rows_dev % LANES == 0
    spectrum, cents_all, weights_all = gather_all(
        spec_re, spec_im, cent_row, cent_col, weights, groups_src, kernels
    )

    cos_own, sin_own, target_own = jnp.asarray(cosine), jnp.asarray(sine), target
    if own_rows % 16:
        first_own = lax.axis_index("src") * own_rows
        first_row = lax.axis_index("row") * target.shape[0] + first_own
        cos_own = lax.dynamic_slice_in_dim(cos_own, first_row, own_rows, 0)
        sin_own = lax.dynamic_slice_in_dim(sin_own, first_row, own_rows, 0)
        cos_own = jnp.tile(cos_own, (slots, 1))
        sin_own = jnp.tile(sin_own, (slots, 1))
        target_own = lax.dynamic_slice_in_dim(target, first_own, own_rows, 0)
        target_own = jnp.tile(target_own, (slots, 1)).T
    cos_split = cosine[:quarter].reshape(quarter, quarter, RADIX).transpose(2, 0, 1)
    sin_split = sine[:quarter].reshape(quarter, quarter, RADIX).transpose(2, 0, 1)
    wide = jnp.asarray(np.concatenate([cos_split, sin_split], axis=2))
    back = jnp.asarray(
        np.concatenate([cos_split.transpose(0, 2, 1), sin_split.transpose(0, 2, 1)], axis=2)
    )

    vmem = pl.BlockSpec(memory_space=pltpu.VMEM)
    hbm = pl.BlockSpec(memory_space=pl.ANY)
    table = vmem if own_rows % 16 else hbm
    smem = pl.BlockSpec(memory_space=pltpu.SMEM)
    lanes_all = 2 * own_rows * total_points
    partial = pl.pallas_call(
        functools.partial(main_kernel, total_points, own_rows),
        out_shape=jax.ShapeDtypeStruct((2, RADIX, quarter, band), jnp.bfloat16),
        in_specs=[smem, smem, hbm, table, table, hbm, hbm, vmem],
        out_specs=hbm,
        scratch_shapes=[
            pltpu.VMEM(spectrum.shape, spectrum.dtype),
            pltpu.VMEM(wide.shape, wide.dtype),
            pltpu.VMEM(back.shape, back.dtype),
            pltpu.VMEM((2, RADIX, quarter, band), jnp.bfloat16),
            pltpu.SemaphoreType.DMA((3,)),
            pltpu.SemaphoreType.DMA((2, RADIX)),
            pltpu.VMEM((RADIX, 2 * quarter, lanes_all), jnp.bfloat16),
            pltpu.VMEM((RADIX, quarter, lanes_all), jnp.float32),
            pltpu.VMEM((RADIX, quarter, lanes_all), jnp.bfloat16),
            pltpu.VMEM((RADIX, quarter, LANES), jnp.float32),
            pltpu.VMEM((2, RADIX, quarter, band), jnp.float32),
            pltpu.VMEM((4, 2, RADIX * WIN_Q, LANES), jnp.float32),
            pltpu.VMEM((groups, 1, LANES), jnp.float32),
            pltpu.VMEM((2, 2 * LANES, band), jnp.bfloat16),
            pltpu.VMEM((2, band, 2 * LANES), jnp.bfloat16),
            pltpu.VMEM((RADIX, quarter, LANES), jnp.float32),
            pltpu.VMEM((2, max(own_rows, 16), band), jnp.bfloat16),
            pltpu.SemaphoreType.DMA((2,)),
        ],
        compiler_params=pltpu.CompilerParams(vmem_limit_bytes=56 * 1024 * 1024),
    )(cents_all, weights_all, spectrum, cos_own, sin_own, wide, back, target_own)

    return reduce_all(partial, groups_src, kernels)


def solution(mesh):
    return jax.shard_map(
        local,
        mesh=mesh,
        in_specs=(P("row", None), P("row", None), P("row", None), P("src"), P("src"), P("src")),
        out_specs=(P("row", None), P("row", None)),
        check_vma=False,
    )
```

```python
import functools
import math

import jax
import jax.numpy as jnp
import numpy as np
from jax import lax
from jax.experimental import pallas as pl
from jax.experimental.pallas import tpu as pltpu
from jax.sharding import PartitionSpec as P

RAD = 128
LANES = 128
RADIX = 4
WIN_Q = 80
WIN_L = 384


def host_tables(band):
    position = np.arange(band, dtype=np.int64)
    phase = position[:, None] * position[None, :] % band
    angle = phase.astype(np.float32) * np.float32(2.0 * math.pi / band)
    factor = np.float32(1.0 / math.sqrt(band))
    return (
        (np.cos(angle) * factor).astype(jnp.bfloat16),
        (np.sin(angle) * factor).astype(jnp.bfloat16),
    )


def times_i(value):
    return -value[1], value[0]


def add(a, b):
    return a[0] + b[0], a[1] + b[1]


def sub(a, b):
    return a[0] - b[0], a[1] - b[1]


def main_kernel(
    total_points,
    own_rows,
    cent_ref,
    weight_ref,
    spec_hbm,
    cos_ref,
    sin_ref,
    wide_hbm,
    back_hbm,
    target_ref,
    out_hbm,
    spec_ref,
    wide_ref,
    back_ref,
    out_ref,
    in_sem,
    out_sem,
    band_ref,
    field_ref,
    adj_ref,
    power_ref,
    grad_ref,
    product_ref,
    scale_ref,
    narrow_ref,
    tall_ref,
    aim_ref,
    own_ref,
    own_sem,
):
    slots = LANES // own_rows
    quarter = spec_ref.shape[1] // RADIX
    points_dev = total_points // cent_ref.shape[0]
    groups = total_points // slots
    wide_rows = RADIX * WIN_Q

    def window(point, split):
        centre_row = cent_ref[point // points_dev, 0, point % points_dev]
        centre_col = cent_ref[point // points_dev, 1, point % points_dev]
        first_q = pl.multiple_of((centre_row - RAD) // (RADIX * 16) * 16, 16)
        first_l = pl.multiple_of((centre_col - RAD) // LANES * LANES, LANES)
        if split:
            shape = (RADIX, WIN_Q, LANES)
            offset = lax.broadcasted_iota(jnp.int32, shape, 1) * RADIX
            offset = offset + lax.broadcasted_iota(jnp.int32, shape, 0)
        else:
            shape = (wide_rows, LANES)
            offset = lax.broadcasted_iota(jnp.int32, shape, 0)
        row_gap = (offset + (first_q * RADIX - centre_row)).astype(jnp.float32)
        room = float(RAD * RAD) - row_gap * row_gap
        flat = (1,) * (len(shape) - 1) + (LANES,)
        lane = lax.broadcasted_iota(jnp.int32, flat, len(shape) - 1)
        masks = []
        for block in range(WIN_L // LANES):
            gap = (lane + (first_l + block * LANES - centre_col)).astype(jnp.float32)
            masks.append(gap * gap <= room)
        return first_q, first_l, masks

    def slot_lanes(slot):
        lane = lax.broadcasted_iota(jnp.int32, (1, LANES), 1)
        return (lane // own_rows == slot).astype(jnp.float32)

    incoming = [
        pltpu.make_async_copy(source, target, in_sem.at[index])
        for index, (source, target) in enumerate(
            ((spec_hbm, spec_ref), (wide_hbm, wide_ref), (back_hbm, back_ref))
        )
    ]
    for copy in incoming:
        copy.start()
    scale_ref[...] = jnp.zeros_like(scale_ref)

    def place_weight(point, carry):
        weight = weight_ref[point // points_dev, 0, point % points_dev]
        scale_ref[point // slots] += weight * slot_lanes(point % slots)
        return carry

    lax.fori_loop(0, total_points, place_weight, 0, unroll=16)

    if own_rows % 16 == 0:
        first_own = pl.multiple_of(lax.axis_index("src") * own_rows, own_rows)
        first_row = lax.axis_index("row") * target_ref.shape[0] + first_own
        own = pl.ds(pl.multiple_of(first_row, own_rows), own_rows)
        copies = [
            pltpu.make_async_copy(table.at[own, :], own_ref.at[part], own_sem.at[part])
            for part, table in enumerate((cos_ref, sin_ref))
        ]
        for copy in copies:
            copy.start()
        aim = jnp.concatenate([target_ref[pl.ds(first_own, own_rows), :]] * slots, axis=0).T
        for copy in copies:
            copy.wait()
        for slot in range(slots):
            low = pl.ds(slot * own_rows, own_rows)
            high = pl.ds(LANES + slot * own_rows, own_rows)
            narrow_ref[0, low, :] = own_ref[0]
            narrow_ref[0, high, :] = own_ref[1]
            narrow_ref[1, low, :] = -own_ref[1]
            narrow_ref[1, high, :] = own_ref[0]
    else:
        aim = target_ref[...]
        narrow_ref[0, :LANES, :] = cos_ref[...]
        narrow_ref[0, LANES:, :] = sin_ref[...]
        narrow_ref[1, :LANES, :] = -sin_ref[...]
        narrow_ref[1, LANES:, :] = cos_ref[...]
    aim_ref[...] = aim.reshape(aim_ref.shape)
    for block in range(2):
        lanes = pl.ds(block * LANES, LANES)
        turned = narrow_ref[0, lanes, :].astype(jnp.float32).T.astype(tall_ref.dtype)
        tall_ref[0, :, lanes] = turned
        tall_ref[1, :, pl.ds((1 - block) * LANES, LANES)] = -turned if block else turned

    band_ref[...] = jnp.zeros_like(band_ref)
    grad_ref[...] = jnp.zeros_like(grad_ref)

    incoming[0].wait()
    buffers = product_ref.shape[0]

    def spread(step, carry):
        places = []
        for buffer in range(buffers):
            point = step * buffers + buffer
            first_q, first_l, masks = window(point, False)
            inside = jnp.concatenate(
                [mask.astype(jnp.float32).astype(jnp.bfloat16) for mask in masks], axis=-1
            )
            rows_all = pl.ds(pl.multiple_of(first_q * RADIX, 16 * RADIX), wide_rows)
            cols = pl.ds(first_l, WIN_L)
            masked = jnp.concatenate(
                [spec_ref[part, rows_all, cols] * inside for part in range(2)], axis=1
            )
            table = jnp.concatenate([tall_ref[0, cols, :], tall_ref[1, cols, :]], axis=0)
            product = jnp.dot(masked, table, preferred_element_type=jnp.float32)
            product_ref[buffer, 0] = product[:, :LANES]
            product_ref[buffer, 1] = product[:, LANES:]
            places.append((point, first_q))
        for buffer, (point, first_q) in enumerate(places):
            chosen = slot_lanes(point % slots)
            base = pl.multiple_of(point // slots * (2 * LANES), 2 * LANES)
            low = pl.ds(base, LANES)
            high = pl.ds(base + LANES, LANES)
            rows = pl.ds(first_q, WIN_Q)
            for residue in range(RADIX):
                picked = pl.ds(residue, WIN_Q, stride=RADIX)
                real = (product_ref[buffer, 0, picked, :] * chosen).astype(jnp.bfloat16)
                imag = (product_ref[buffer, 1, picked, :] * chosen).astype(jnp.bfloat16)
                band_ref[residue, rows, low] += real
                band_ref[residue, rows, high] += imag
        return carry

    lax.fori_loop(0, total_points // buffers, spread, 0)
    incoming[1].wait()

    power_ref[...] = jnp.zeros_like(power_ref)

    def forward(group, carry):
        base = pl.multiple_of(group * (2 * LANES), 2 * LANES)
        parts = []
        for residue in range(RADIX):
            real = band_ref[residue, :, pl.ds(base, LANES)]
            imag = band_ref[residue, :, pl.ds(base + LANES, LANES)]
            operand = jnp.concatenate(
                [jnp.concatenate([real, imag], axis=1), jnp.concatenate([-imag, real], axis=1)],
                axis=0,
            )
            product = jnp.dot(wide_ref[residue], operand, preferred_element_type=jnp.float32)
            parts.append((product[:, :LANES], product[:, LANES:]))
        even, odd = add(parts[0], parts[2]), add(parts[1], parts[3])
        even_gap, odd_gap = sub(parts[0], parts[2]), times_i(sub(parts[1], parts[3]))
        fields = [add(even, odd), add(even_gap, odd_gap), sub(even, odd), sub(even_gap, odd_gap)]
        weight = scale_ref[group]
        for index, (real, imag) in enumerate(fields):
            field_ref[index, :, pl.ds(base, LANES)] = real
            field_ref[index, :, pl.ds(base + LANES, LANES)] = imag
            power_ref[index] += weight * (real * real + imag * imag)
        return carry

    lax.fori_loop(0, groups, forward, 0, unroll=min(groups, 4))

    for index in range(RADIX):
        power = power_ref[index]
        shift = own_rows
        while shift < LANES:
            power = power + pltpu.roll(power, shift, 1)
            shift *= 2
        power_ref[index] = power * (2.0 / total_points) - 2.0 * aim_ref[index]

    incoming[2].wait()

    def backward(group, carry):
        base = pl.multiple_of(group * (2 * LANES), 2 * LANES)
        weight = scale_ref[group]
        grads = []
        for index in range(RADIX):
            scale = weight * power_ref[index]
            grads.append(
                (
                    scale * field_ref[index, :, pl.ds(base, LANES)],
                    scale * field_ref[index, :, pl.ds(base + LANES, LANES)],
                )
            )
        even, odd = add(grads[0], grads[2]), add(grads[1], grads[3])
        even_gap, odd_gap = sub(grads[0], grads[2]), times_i(sub(grads[1], grads[3]))
        folded = [add(even, odd), sub(even_gap, odd_gap), sub(even, odd), add(even_gap, odd_gap)]
        for residue, (real, imag) in enumerate(folded):
            real = real.astype(jnp.bfloat16)
            imag = imag.astype(jnp.bfloat16)
            operand = jnp.concatenate(
                [jnp.concatenate([real, imag], axis=1), jnp.concatenate([imag, -real], axis=1)],
                axis=0,
            )
            adj_ref[residue, :, pl.ds(base, 2 * LANES)] = jnp.dot(
                back_ref[residue], operand, preferred_element_type=jnp.float32
            ).astype(jnp.bfloat16)
        return carry

    lax.fori_loop(0, groups, backward, 0, unroll=min(groups, 4))

    def collect(point, carry):
        first_q, first_l, masks = window(point, True)
        rows = pl.ds(first_q, WIN_Q)
        cols = pl.ds(first_l, WIN_L)
        base = pl.multiple_of(point // slots * (2 * LANES), 2 * LANES)
        chosen = slot_lanes(point % slots).astype(jnp.bfloat16)
        adjoint = adj_ref[:, rows, pl.ds(base, 2 * LANES)]
        adjoint = adjoint * jnp.concatenate([chosen, chosen], axis=-1)[None]
        adjoint = adjoint.reshape(wide_rows, 2 * LANES)
        for part in range(2):
            term = jnp.dot(
                adjoint, narrow_ref[part, :, cols], preferred_element_type=jnp.float32
            ).reshape(RADIX, WIN_Q, WIN_L)
            for block, mask in enumerate(masks):
                where = (part, slice(None), rows, pl.ds(first_l + block * LANES, LANES))
                piece = term[:, :, block * LANES : (block + 1) * LANES]
                grad_ref[where] += jnp.where(mask, piece, 0.0)
        return carry

    lax.fori_loop(0, total_points, collect, 0, unroll=4)
    leaving = []
    for part in range(2):
        for residue in range(RADIX):
            out_ref[part, residue] = grad_ref[part, residue].astype(out_ref.dtype)
            copy = pltpu.make_async_copy(
                out_ref.at[part, residue], out_hbm.at[part, residue], out_sem.at[part, residue]
            )
            copy.start()
            leaving.append(copy)
    for copy in leaving:
        copy.wait()


def row_place():
    row = lax.axis_index("row")
    core, x, y = row % 2, row // 2 % 2, row // 4
    mate = row + 1 - 2 * core
    across_x = row + 2 - 4 * x
    across_y = row + 4 - 8 * y
    return row, core, x, y, mate, across_x, across_y


def enter(rows, sources):
    barrier = pltpu.get_barrier_semaphore()
    for row in rows:
        pl.semaphore_signal(
            barrier, inc=1, device_id={"row": row}, device_id_type=pl.DeviceIdType.MESH
        )
    for source in sources:
        pl.semaphore_signal(
            barrier, inc=1, device_id={"src": source}, device_id_type=pl.DeviceIdType.MESH
        )
    pl.semaphore_wait(barrier, len(rows) + len(sources))


def gather_kernel(
    sources,
    re_ref,
    im_ref,
    cent_row_ref,
    cent_col_ref,
    weight_row_ref,
    spec_ref,
    cents_ref,
    weights_ref,
    cent_ref,
    weight_ref,
    local_sem,
    send_sem,
    recv_sem,
    point_send_sem,
    point_recv_sem,
):
    row, core, x, y, mate, across_x, across_y = row_place()
    corner = across_x + across_y - row
    mate_step = mate - row
    rows_dev = re_ref.shape[0]
    own = lax.axis_index("src")
    peers = [(own + step) % sources for step in range(1, sources)]
    points_dev = weight_row_ref.shape[1]
    cent_ref[...] = jnp.zeros_like(cent_ref)
    weight_ref[...] = jnp.zeros_like(weight_ref)
    cent_ref[0:1, 0:points_dev] = cent_row_ref[...]
    cent_ref[1:2, 0:points_dev] = cent_col_ref[...]
    weight_ref[0:1, 0:points_dev] = weight_row_ref[...]
    enter([mate, across_x, across_y], peers)

    parity = own % 2
    partner = own + 1 - 2 * parity
    few = rows_dev * 3 // 8
    most = rows_dev - few
    fetched = (few * parity, most)
    passed = (most * parity, few)
    missing = (most * (1 - parity), few)
    whole = (0, rows_dev)

    def rows_of(device, piece=whole):
        return pl.ds(pl.multiple_of(device * rows_dev + piece[0], 16), piece[1])

    keep = [
        pltpu.make_async_copy(re_ref, spec_ref.at[0, rows_of(row), :], local_sem.at[0]),
        pltpu.make_async_copy(im_ref, spec_ref.at[1, rows_of(row), :], local_sem.at[1]),
        pltpu.make_async_copy(cent_ref, cents_ref.at[own], local_sem.at[2]),
        pltpu.make_async_copy(weight_ref, weights_ref.at[own], local_sem.at[3]),
    ]
    for copy in keep:
        copy.start()
    small = []
    for index, peer in enumerate(peers):
        for kind, (source, target) in enumerate(
            [(cent_ref, cents_ref.at[own]), (weight_ref, weights_ref.at[own])]
        ):
            small.append(
                pltpu.make_async_remote_copy(
                    src_ref=source,
                    dst_ref=target,
                    send_sem=point_send_sem.at[kind, index],
                    recv_sem=point_recv_sem.at[kind, index],
                    device_id={"src": peer},
                    device_id_type=pl.DeviceIdType.MESH,
                )
            )
    sent = []

    def send(part, holder, piece, axis, to):
        target = spec_ref.at[part, rows_of(row if holder is None else holder, piece), :]
        source = target
        if holder is None:
            first = pl.multiple_of(piece[0], 16)
            source = (re_ref, im_ref)[part].at[pl.ds(first, piece[1]), :]
        index = len(sent)
        copy = pltpu.make_async_remote_copy(
            src_ref=source,
            dst_ref=target,
            send_sem=send_sem.at[index],
            recv_sem=recv_sem.at[index],
            device_id={axis: to},
            device_id_type=pl.DeviceIdType.MESH,
        )
        copy.start()
        sent.append(copy)
        return copy

    re_x = send(0, None, fetched, "row", across_x)
    im_y = send(1, None, fetched, "row", across_y)
    im_x = send(1, None, fetched, "row", across_x)
    re_y = send(0, None, fetched, "row", across_y)
    for copy in small:
        copy.start()
    late = [send(part, None, whole, "row", mate) for part in range(2)]
    partner_copies = []

    def pass_on(part, holder):
        partner_copies.append((send(part, holder, passed, "src", partner), part, holder))
        late.append(send(part, holder, fetched, "row", mate))

    re_x.wait_recv()
    re_corner = send(0, across_x, fetched, "row", across_y)
    pass_on(0, across_x)
    im_y.wait_recv()
    im_corner = send(1, across_y, fetched, "row", across_x)
    pass_on(1, across_y)
    im_x.wait_recv()
    pass_on(1, across_x)
    re_y.wait_recv()
    pass_on(0, across_y)
    re_corner.wait_recv()
    pass_on(0, corner)
    im_corner.wait_recv()
    pass_on(1, corner)
    for copy, part, holder in partner_copies:
        copy.wait_recv()
        late.append(send(part, holder, missing, "row", mate))
    for copy in late:
        copy.wait_recv()
    for copy in sent:
        copy.wait_send()
    for copy in small:
        copy.wait()
    for copy in keep:
        copy.wait()


def reduce_kernel(
    sources,
    part_ref,
    out_ref,
    plane,
    own_part,
    own_sem,
    mate_in,
    chip_sum,
    first_re_in,
    first_im_in,
    first_re,
    first_im,
    last_re_in,
    last_im_in,
    left_in,
    right_in,
    chain,
    final_in,
    send_sem,
    recv_sem,
    up_send,
    left_recv,
    right_recv,
    down_send,
    down_recv,
):
    row, core, x, y, mate, across_x, across_y = row_place()
    chunks = mate_in.shape[0]
    depth = mate_in.shape[-2]
    halves = chunks // part_ref.shape[1]
    own = lax.axis_index("src")
    root = sources // 2
    leaf = jnp.logical_or(own == 0, own == sources - 1)
    has_left = jnp.logical_and(own > 0, own <= root)
    has_right = jnp.logical_and(own >= root, own < sources - 1)
    peers = [(own + step) % sources for step in range(1, sources)]
    enter([mate, across_x, across_y], peers)

    @pl.when(jnp.logical_not(has_left))
    def _():
        left_in[...] = jnp.zeros_like(left_in)

    @pl.when(jnp.logical_not(has_right))
    def _():
        right_in[...] = jnp.zeros_like(right_in)

    def wide(value):
        return value.astype(jnp.float32)

    def row_copy(kind, chunk, source, target, to):
        return pltpu.make_async_remote_copy(
            src_ref=source,
            dst_ref=target,
            send_sem=send_sem.at[kind, chunk],
            recv_sem=recv_sem.at[kind, chunk],
            device_id={"row": to},
            device_id_type=pl.DeviceIdType.MESH,
        )

    pair, step_re, step_im, end_re, end_im = {}, {}, {}, {}, {}
    keep = {}
    for chunk in range(chunks):
        residue = chunk // halves
        rows = pl.ds(chunk % halves * depth, depth)
        pair[chunk] = row_copy(
            0, chunk, part_ref.at[:, residue, :, :, 1 - core, rows], mate_in.at[chunk], mate
        )
        keep[chunk] = pltpu.make_async_copy(
            part_ref.at[:, residue, :, :, core, rows], own_part.at[chunk], own_sem.at[chunk]
        )
    ahead = 2
    for chunk in range(ahead):
        pair[chunk].start()
        keep[chunk].start()

    def place(chunk, source):
        residue = chunk // halves
        first = residue + chunk % halves * depth * RADIX
        rows = pl.ds(first, depth, stride=RADIX)
        for part in range(2):
            for block in range(plane.shape[1]):
                plane[part, block, rows, :] = wide(
                    source[chunk, part, :, block * LANES : (block + 1) * LANES]
                )

    def add_pair(chunk):
        keep[chunk].wait()
        pair[chunk].wait_recv()
        if chunk + ahead < chunks:
            pair[chunk + ahead].start()
            keep[chunk + ahead].start()
        total = wide(own_part[chunk]) + wide(mate_in[chunk])
        chip_sum[chunk] = total.astype(chip_sum.dtype)
        step_re[chunk] = row_copy(
            1, chunk, chip_sum.at[chunk, 0, :, 1 - x], first_re_in.at[chunk], across_x
        )
        step_im[chunk] = row_copy(
            2, chunk, chip_sum.at[chunk, 1, 1 - y], first_im_in.at[chunk], across_y
        )
        step_re[chunk].start()
        step_im[chunk].start()

    def add_first(chunk):
        step_re[chunk].wait_recv()
        total = wide(chip_sum[chunk, 0, :, x]) + wide(first_re_in[chunk])
        first_re[chunk] = total.astype(first_re.dtype)
        end_re[chunk] = row_copy(
            3, chunk, first_re.at[chunk, 1 - y], last_re_in.at[chunk], across_y
        )
        end_re[chunk].start()
        step_im[chunk].wait_recv()
        total = wide(chip_sum[chunk, 1, y]) + wide(first_im_in[chunk])
        first_im[chunk] = total.astype(first_im.dtype)
        end_im[chunk] = row_copy(
            4, chunk, first_im.at[chunk, 1 - x], last_im_in.at[chunk], across_x
        )
        end_im[chunk].start()

    def src_copy(source, target, sent, received, to):
        return pltpu.make_async_remote_copy(
            src_ref=source,
            dst_ref=target,
            send_sem=sent,
            recv_sem=received,
            device_id={"src": to},
            device_id_type=pl.DeviceIdType.MESH,
        )

    after = jnp.minimum(own + 1, sources - 1)
    before = jnp.maximum(own - 1, 0)

    def to_right(chunk):
        return src_copy(
            chain.at[chunk], left_in.at[chunk], up_send.at[chunk], left_recv.at[chunk], after
        )

    def to_left(chunk):
        return src_copy(
            chain.at[chunk], right_in.at[chunk], up_send.at[chunk], right_recv.at[chunk], before
        )

    def down_left(chunk, source):
        return src_copy(
            source.at[chunk],
            final_in.at[chunk],
            down_send.at[0, chunk],
            down_recv.at[chunk],
            before,
        )

    def down_right(chunk, source):
        return src_copy(
            source.at[chunk],
            final_in.at[chunk],
            down_send.at[1, chunk],
            down_recv.at[chunk],
            after,
        )

    def add_last(chunk):
        end_re[chunk].wait_recv()
        end_im[chunk].wait_recv()

        @pl.when(has_left)
        def _():
            to_right(chunk).wait_recv()

        @pl.when(has_right)
        def _():
            to_left(chunk).wait_recv()

        real = wide(first_re[chunk, y]) + wide(last_re_in[chunk])
        imag = wide(first_im[chunk, x]) + wide(last_im_in[chunk])
        for part, total in enumerate((real, imag)):
            total = total + wide(left_in[chunk, part]) + wide(right_in[chunk, part])
            chain[chunk, part] = total.astype(chain.dtype)

        @pl.when(own < root)
        def _():
            to_right(chunk).start()

        @pl.when(own > root)
        def _():
            to_left(chunk).start()

        @pl.when(own == root)
        def _():
            if root > 0:
                down_left(chunk, chain).start()
            if root < sources - 1:
                down_right(chunk, chain).start()
            place(chunk, chain)

    def pass_final(chunk):
        @pl.when(jnp.logical_and(own < root, own > 0))
        def _():
            down_left(chunk, final_in).wait_recv()
            down_left(chunk, final_in).start()
            place(chunk, final_in)

        @pl.when(jnp.logical_and(own > root, own < sources - 1))
        def _():
            down_right(chunk, final_in).wait_recv()
            down_right(chunk, final_in).start()
            place(chunk, final_in)

    stages = ((add_pair, 0), (add_first, 1), (add_last, 2), (pass_final, 5))
    for time in range(chunks + 5):
        for stage, lag in stages:
            if 0 <= time - lag < chunks:
                stage(time - lag)
    for chunk in range(chunks):

        @pl.when(jnp.logical_and(leaf, own != root))
        def _():
            down_left(chunk, final_in).wait_recv()
            place(chunk, final_in)

    for part in range(2):
        for block in range(plane.shape[1]):
            cols = slice(block * LANES, (block + 1) * LANES)
            out_ref[part, :, cols] = plane[part, block].astype(out_ref.dtype)

    for chunk in range(chunks):
        for group in (pair, step_re, step_im, end_re, end_im):
            group[chunk].wait_send()

        @pl.when(own < root)
        def _():
            to_right(chunk).wait_send()

            @pl.when(own > 0)
            def _():
                down_left(chunk, final_in).wait_send()

        @pl.when(own > root)
        def _():
            to_left(chunk).wait_send()

            @pl.when(own < sources - 1)
            def _():
                down_right(chunk, final_in).wait_send()

        @pl.when(own == root)
        def _():
            if root > 0:
                down_left(chunk, chain).wait_send()
            if root < sources - 1:
                down_right(chunk, chain).wait_send()


def gather_all(spec_re, spec_im, cent_row, cent_col, weights, sources, kernels):
    rows_dev, band = spec_re.shape
    points_dev = weights.shape[0]
    if not kernels:
        pad = ((0, 6), (0, LANES - points_dev))
        cents = jnp.pad(jnp.stack([cent_row, cent_col], axis=0), pad)
        weights = jnp.pad(jnp.stack([weights, weights], axis=0), pad)
        spectrum = lax.all_gather(jnp.stack([spec_re, spec_im]), "row", axis=1, tiled=True)
        return spectrum, lax.all_gather(cents, "src"), lax.all_gather(weights, "src")
    tile = (8, LANES)
    hbm = pl.BlockSpec(memory_space=pl.ANY)
    vmem = pl.BlockSpec(memory_space=pltpu.VMEM)
    dma = pltpu.SemaphoreType.DMA
    return pl.pallas_call(
        functools.partial(gather_kernel, sources),
        out_shape=(
            jax.ShapeDtypeStruct((2, rows_dev * lax.axis_size("row"), band), spec_re.dtype),
            jax.ShapeDtypeStruct((sources,) + tile, cent_row.dtype),
            jax.ShapeDtypeStruct((sources,) + tile, weights.dtype),
        ),
        in_specs=[hbm, hbm, vmem, vmem, vmem],
        out_specs=(hbm, vmem, vmem),
        scratch_shapes=[
            pltpu.VMEM(tile, cent_row.dtype),
            pltpu.VMEM(tile, weights.dtype),
            dma((4,)),
            dma((26,)),
            dma((26,)),
            dma((2, max(sources - 1, 1))),
            dma((2, max(sources - 1, 1))),
        ],
        compiler_params=pltpu.CompilerParams(collective_id=0, has_side_effects=True),
    )(spec_re, spec_im, cent_row[None], cent_col[None], weights[None])


def reduce_all(partial, sources, kernels):
    _, residues, quarter, band = partial.shape
    own = quarter // lax.axis_size("row")
    rows_dev = own * residues
    if not kernels:
        summed = lax.psum_scatter(partial, "row", scatter_dimension=2, tiled=True)
        summed = lax.psum(summed, "src").astype(jnp.float32)
        summed = summed.transpose(0, 2, 1, 3).reshape(2, rows_dev, band)
        return summed[0], summed[1]
    halves = 2
    chunks = residues * halves
    partial = partial.reshape(2, residues, 2, 2, 2, own, band)
    vmem = pl.BlockSpec(memory_space=pltpu.VMEM)
    dma = pltpu.SemaphoreType.DMA

    def buffer(*lead):
        return pltpu.VMEM((chunks,) + lead + (own // halves, band), partial.dtype)

    summed = pl.pallas_call(
        functools.partial(reduce_kernel, sources),
        out_shape=jax.ShapeDtypeStruct((2, rows_dev, band), partial.dtype),
        in_specs=[pl.BlockSpec(memory_space=pl.ANY)],
        out_specs=vmem,
        scratch_shapes=[
            pltpu.VMEM((2, band // LANES, rows_dev, LANES), jnp.float32),
            buffer(2, 2, 2),
            dma((chunks,)),
            buffer(2, 2, 2),
            buffer(2, 2, 2),
            buffer(2),
            buffer(2),
            buffer(2),
            buffer(2),
            buffer(),
            buffer(),
            buffer(2),
            buffer(2),
            buffer(2),
            buffer(2),
            dma((5, chunks)),
            dma((5, chunks)),
            dma((chunks,)),
            dma((chunks,)),
            dma((chunks,)),
            dma((2, chunks)),
            dma((chunks,)),
        ],
        compiler_params=pltpu.CompilerParams(
            collective_id=1, has_side_effects=True, vmem_limit_bytes=61 * 1024 * 1024
        ),
    )(partial)
    return summed[0].astype(jnp.float32), summed[1].astype(jnp.float32)


def local(spec_re, spec_im, target, weights, cent_row, cent_col):
    rows_dev, band = spec_re.shape
    groups_src = lax.axis_size("src")
    points_dev = weights.shape[0]
    total_points = points_dev * groups_src
    own_rows = target.shape[0] // groups_src
    slots = LANES // own_rows
    groups = total_points // slots
    quarter = band // RADIX
    cosine, sine = host_tables(band)

    kernels = lax.axis_size("row") == 8 and groups_src % 2 == 0 and rows_dev % LANES == 0
    spectrum, cents_all, weights_all = gather_all(
        spec_re, spec_im, cent_row, cent_col, weights, groups_src, kernels
    )

    cos_own, sin_own, target_own = jnp.asarray(cosine), jnp.asarray(sine), target
    if own_rows % 16:
        first_own = lax.axis_index("src") * own_rows
        first_row = lax.axis_index("row") * target.shape[0] + first_own
        cos_own = lax.dynamic_slice_in_dim(cos_own, first_row, own_rows, 0)
        sin_own = lax.dynamic_slice_in_dim(sin_own, first_row, own_rows, 0)
        cos_own = jnp.tile(cos_own, (slots, 1))
        sin_own = jnp.tile(sin_own, (slots, 1))
        target_own = lax.dynamic_slice_in_dim(target, first_own, own_rows, 0)
        target_own = jnp.tile(target_own, (slots, 1)).T
    cos_split = cosine[:quarter].reshape(quarter, quarter, RADIX).transpose(2, 0, 1)
    sin_split = sine[:quarter].reshape(quarter, quarter, RADIX).transpose(2, 0, 1)
    wide = jnp.asarray(np.concatenate([cos_split, sin_split], axis=2))
    back = jnp.asarray(
        np.concatenate([cos_split.transpose(0, 2, 1), sin_split.transpose(0, 2, 1)], axis=2)
    )

    vmem = pl.BlockSpec(memory_space=pltpu.VMEM)
    hbm = pl.BlockSpec(memory_space=pl.ANY)
    table = vmem if own_rows % 16 else hbm
    smem = pl.BlockSpec(memory_space=pltpu.SMEM)
    lanes_all = 2 * own_rows * total_points
    partial = pl.pallas_call(
        functools.partial(main_kernel, total_points, own_rows),
        out_shape=jax.ShapeDtypeStruct((2, RADIX, quarter, band), jnp.bfloat16),
        in_specs=[smem, smem, hbm, table, table, hbm, hbm, vmem],
        out_specs=hbm,
        scratch_shapes=[
            pltpu.VMEM(spectrum.shape, spectrum.dtype),
            pltpu.VMEM(wide.shape, wide.dtype),
            pltpu.VMEM(back.shape, back.dtype),
            pltpu.VMEM((2, RADIX, quarter, band), jnp.bfloat16),
            pltpu.SemaphoreType.DMA((3,)),
            pltpu.SemaphoreType.DMA((2, RADIX)),
            pltpu.VMEM((RADIX, quarter, lanes_all), jnp.bfloat16),
            pltpu.VMEM((RADIX, quarter, lanes_all), jnp.float32),
            pltpu.VMEM((RADIX, quarter, lanes_all), jnp.bfloat16),
            pltpu.VMEM((RADIX, quarter, LANES), jnp.float32),
            pltpu.VMEM((2, RADIX, quarter, band), jnp.float32),
            pltpu.VMEM((4, 2, RADIX * WIN_Q, LANES), jnp.float32),
            pltpu.VMEM((groups, 1, LANES), jnp.float32),
            pltpu.VMEM((2, 2 * LANES, band), jnp.bfloat16),
            pltpu.VMEM((2, band, 2 * LANES), jnp.bfloat16),
            pltpu.VMEM((RADIX, quarter, LANES), jnp.float32),
            pltpu.VMEM((2, max(own_rows, 16), band), jnp.bfloat16),
            pltpu.SemaphoreType.DMA((2,)),
        ],
        compiler_params=pltpu.CompilerParams(vmem_limit_bytes=56 * 1024 * 1024),
    )(cents_all, weights_all, spectrum, cos_own, sin_own, wide, back, target_own)

    return reduce_all(partial, groups_src, kernels)


def solution(mesh):
    return jax.shard_map(
        local,
        mesh=mesh,
        in_specs=(P("row", None), P("row", None), P("row", None), P("src"), P("src"), P("src")),
        out_specs=(P("row", None), P("row", None)),
        check_vma=False,
    )
```

```python
import functools
import math

import jax
import jax.numpy as jnp
import numpy as np
from jax import lax
from jax.experimental import pallas as pl
from jax.experimental.pallas import tpu as pltpu
from jax.sharding import PartitionSpec as P

RAD = 128
LANES = 128
RADIX = 4
WIN_Q = 80
WIN_L = 384


def host_tables(band):
    position = np.arange(band, dtype=np.int64)
    phase = position[:, None] * position[None, :] % band
    angle = phase.astype(np.float32) * np.float32(2.0 * math.pi / band)
    factor = np.float32(1.0 / math.sqrt(band))
    return (
        (np.cos(angle) * factor).astype(jnp.bfloat16),
        (np.sin(angle) * factor).astype(jnp.bfloat16),
    )


def times_i(value):
    return -value[1], value[0]


def add(a, b):
    return a[0] + b[0], a[1] + b[1]


def sub(a, b):
    return a[0] - b[0], a[1] - b[1]


def main_kernel(
    total_points,
    own_rows,
    cent_ref,
    weight_ref,
    spec_hbm,
    cos_ref,
    sin_ref,
    wide_hbm,
    back_hbm,
    target_ref,
    out_hbm,
    spec_ref,
    wide_ref,
    back_ref,
    out_ref,
    in_sem,
    out_sem,
    band_ref,
    field_ref,
    adj_ref,
    power_ref,
    grad_ref,
    product_ref,
    scale_ref,
    narrow_ref,
    tall_ref,
    aim_ref,
    own_ref,
    own_sem,
):
    slots = LANES // own_rows
    quarter = spec_ref.shape[1] // RADIX
    points_dev = total_points // cent_ref.shape[0]
    groups = total_points // slots
    wide_rows = RADIX * WIN_Q

    def window(point, split):
        centre_row = cent_ref[point // points_dev, 0, point % points_dev]
        centre_col = cent_ref[point // points_dev, 1, point % points_dev]
        first_q = pl.multiple_of((centre_row - RAD) // (RADIX * 16) * 16, 16)
        first_l = pl.multiple_of((centre_col - RAD) // LANES * LANES, LANES)
        if split:
            shape = (RADIX, WIN_Q, LANES)
            offset = lax.broadcasted_iota(jnp.int32, shape, 1) * RADIX
            offset = offset + lax.broadcasted_iota(jnp.int32, shape, 0)
        else:
            shape = (wide_rows, LANES)
            offset = lax.broadcasted_iota(jnp.int32, shape, 0)
        row_gap = (offset + (first_q * RADIX - centre_row)).astype(jnp.float32)
        room = float(RAD * RAD) - row_gap * row_gap
        flat = (1,) * (len(shape) - 1) + (LANES,)
        lane = lax.broadcasted_iota(jnp.int32, flat, len(shape) - 1)
        masks = []
        for block in range(WIN_L // LANES):
            gap = (lane + (first_l + block * LANES - centre_col)).astype(jnp.float32)
            masks.append(gap * gap <= room)
        return first_q, first_l, masks

    def slot_lanes(slot):
        lane = lax.broadcasted_iota(jnp.int32, (1, LANES), 1)
        return (lane // own_rows == slot).astype(jnp.float32)

    incoming = [
        pltpu.make_async_copy(source, target, in_sem.at[index])
        for index, (source, target) in enumerate(
            ((spec_hbm, spec_ref), (wide_hbm, wide_ref), (back_hbm, back_ref))
        )
    ]
    for copy in incoming:
        copy.start()
    scale_ref[...] = jnp.zeros_like(scale_ref)

    def place_weight(point, carry):
        weight = weight_ref[point // points_dev, 0, point % points_dev]
        scale_ref[point // slots] += weight * slot_lanes(point % slots)
        return carry

    lax.fori_loop(0, total_points, place_weight, 0, unroll=16)

    if own_rows % 16 == 0:
        first_own = pl.multiple_of(lax.axis_index("src") * own_rows, own_rows)
        first_row = lax.axis_index("row") * target_ref.shape[0] + first_own
        own = pl.ds(pl.multiple_of(first_row, own_rows), own_rows)
        copies = [
            pltpu.make_async_copy(table.at[own, :], own_ref.at[part], own_sem.at[part])
            for part, table in enumerate((cos_ref, sin_ref))
        ]
        for copy in copies:
            copy.start()
        aim = jnp.concatenate([target_ref[pl.ds(first_own, own_rows), :]] * slots, axis=0).T
        for copy in copies:
            copy.wait()
        for slot in range(slots):
            low = pl.ds(slot * own_rows, own_rows)
            high = pl.ds(LANES + slot * own_rows, own_rows)
            narrow_ref[0, low, :] = own_ref[0]
            narrow_ref[0, high, :] = own_ref[1]
            narrow_ref[1, low, :] = -own_ref[1]
            narrow_ref[1, high, :] = own_ref[0]
    else:
        aim = target_ref[...]
        narrow_ref[0, :LANES, :] = cos_ref[...]
        narrow_ref[0, LANES:, :] = sin_ref[...]
        narrow_ref[1, :LANES, :] = -sin_ref[...]
        narrow_ref[1, LANES:, :] = cos_ref[...]
    aim_ref[...] = aim.reshape(aim_ref.shape)
    for block in range(2):
        lanes = pl.ds(block * LANES, LANES)
        turned = narrow_ref[0, lanes, :].astype(jnp.float32).T.astype(tall_ref.dtype)
        tall_ref[0, :, lanes] = turned
        tall_ref[1, :, pl.ds((1 - block) * LANES, LANES)] = -turned if block else turned

    band_ref[...] = jnp.zeros_like(band_ref)
    grad_ref[...] = jnp.zeros_like(grad_ref)

    incoming[0].wait()
    buffers = product_ref.shape[0]

    def spread(step, carry):
        places = []
        for buffer in range(buffers):
            point = step * buffers + buffer
            first_q, first_l, masks = window(point, False)
            inside = jnp.concatenate(
                [mask.astype(jnp.float32).astype(jnp.bfloat16) for mask in masks], axis=-1
            )
            rows_all = pl.ds(pl.multiple_of(first_q * RADIX, 16 * RADIX), wide_rows)
            cols = pl.ds(first_l, WIN_L)
            masked = jnp.concatenate(
                [spec_ref[part, rows_all, cols] * inside for part in range(2)], axis=1
            )
            table = jnp.concatenate([tall_ref[0, cols, :], tall_ref[1, cols, :]], axis=0)
            product = jnp.dot(masked, table, preferred_element_type=jnp.float32)
            product_ref[buffer, 0] = product[:, :LANES]
            product_ref[buffer, 1] = product[:, LANES:]
            places.append((point, first_q))
        for buffer, (point, first_q) in enumerate(places):
            chosen = slot_lanes(point % slots)
            base = pl.multiple_of(point // slots * (2 * LANES), 2 * LANES)
            low = pl.ds(base, LANES)
            high = pl.ds(base + LANES, LANES)
            rows = pl.ds(first_q, WIN_Q)
            for residue in range(RADIX):
                picked = pl.ds(residue, WIN_Q, stride=RADIX)
                real = (product_ref[buffer, 0, picked, :] * chosen).astype(jnp.bfloat16)
                imag = (product_ref[buffer, 1, picked, :] * chosen).astype(jnp.bfloat16)
                band_ref[residue, rows, low] += real
                band_ref[residue, rows, high] += imag
        return carry

    lax.fori_loop(0, total_points // buffers, spread, 0)
    incoming[1].wait()

    power_ref[...] = jnp.zeros_like(power_ref)

    def forward(group, carry):
        base = pl.multiple_of(group * (2 * LANES), 2 * LANES)
        parts = []
        for residue in range(RADIX):
            real = band_ref[residue, :, pl.ds(base, LANES)]
            imag = band_ref[residue, :, pl.ds(base + LANES, LANES)]
            operand = jnp.concatenate(
                [jnp.concatenate([real, imag], axis=1), jnp.concatenate([-imag, real], axis=1)],
                axis=0,
            )
            product = jnp.dot(wide_ref[residue], operand, preferred_element_type=jnp.float32)
            parts.append((product[:, :LANES], product[:, LANES:]))
        even, odd = add(parts[0], parts[2]), add(parts[1], parts[3])
        even_gap, odd_gap = sub(parts[0], parts[2]), times_i(sub(parts[1], parts[3]))
        fields = [add(even, odd), add(even_gap, odd_gap), sub(even, odd), sub(even_gap, odd_gap)]
        weight = scale_ref[group]
        for index, (real, imag) in enumerate(fields):
            field_ref[index, :, pl.ds(base, LANES)] = real
            field_ref[index, :, pl.ds(base + LANES, LANES)] = imag
            power_ref[index] += weight * (real * real + imag * imag)
        return carry

    lax.fori_loop(0, groups, forward, 0, unroll=min(groups, 4))

    for index in range(RADIX):
        power = power_ref[index]
        shift = own_rows
        while shift < LANES:
            power = power + pltpu.roll(power, shift, 1)
            shift *= 2
        power_ref[index] = power * (2.0 / total_points) - 2.0 * aim_ref[index]

    incoming[2].wait()

    def backward(group, carry):
        base = pl.multiple_of(group * (2 * LANES), 2 * LANES)
        weight = scale_ref[group]
        grads = []
        for index in range(RADIX):
            scale = weight * power_ref[index]
            grads.append(
                (
                    scale * field_ref[index, :, pl.ds(base, LANES)],
                    scale * field_ref[index, :, pl.ds(base + LANES, LANES)],
                )
            )
        even, odd = add(grads[0], grads[2]), add(grads[1], grads[3])
        even_gap, odd_gap = sub(grads[0], grads[2]), times_i(sub(grads[1], grads[3]))
        folded = [add(even, odd), sub(even_gap, odd_gap), sub(even, odd), add(even_gap, odd_gap)]
        for residue, (real, imag) in enumerate(folded):
            real = real.astype(jnp.bfloat16)
            imag = imag.astype(jnp.bfloat16)
            operand = jnp.concatenate(
                [jnp.concatenate([real, imag], axis=1), jnp.concatenate([imag, -real], axis=1)],
                axis=0,
            )
            adj_ref[residue, :, pl.ds(base, 2 * LANES)] = jnp.dot(
                back_ref[residue], operand, preferred_element_type=jnp.float32
            ).astype(jnp.bfloat16)
        return carry

    lax.fori_loop(0, groups, backward, 0, unroll=min(groups, 4))

    def collect(point, carry):
        first_q, first_l, masks = window(point, True)
        rows = pl.ds(first_q, WIN_Q)
        cols = pl.ds(first_l, WIN_L)
        base = pl.multiple_of(point // slots * (2 * LANES), 2 * LANES)
        chosen = slot_lanes(point % slots).astype(jnp.bfloat16)
        adjoint = adj_ref[:, rows, pl.ds(base, 2 * LANES)]
        adjoint = adjoint * jnp.concatenate([chosen, chosen], axis=-1)[None]
        adjoint = adjoint.reshape(wide_rows, 2 * LANES)
        for part in range(2):
            term = jnp.dot(
                adjoint, narrow_ref[part, :, cols], preferred_element_type=jnp.float32
            ).reshape(RADIX, WIN_Q, WIN_L)
            for block, mask in enumerate(masks):
                where = (part, slice(None), rows, pl.ds(first_l + block * LANES, LANES))
                piece = term[:, :, block * LANES : (block + 1) * LANES]
                grad_ref[where] += jnp.where(mask, piece, 0.0)
        return carry

    lax.fori_loop(0, total_points, collect, 0, unroll=4)
    leaving = []
    for part in range(2):
        for residue in range(RADIX):
            out_ref[part, residue] = grad_ref[part, residue].astype(out_ref.dtype)
            copy = pltpu.make_async_copy(
                out_ref.at[part, residue], out_hbm.at[part, residue], out_sem.at[part, residue]
            )
            copy.start()
            leaving.append(copy)
    for copy in leaving:
        copy.wait()


def row_place():
    row = lax.axis_index("row")
    core, x, y = row % 2, row // 2 % 2, row // 4
    mate = row + 1 - 2 * core
    across_x = row + 2 - 4 * x
    across_y = row + 4 - 8 * y
    return row, core, x, y, mate, across_x, across_y


def enter(rows, sources):
    barrier = pltpu.get_barrier_semaphore()
    for row in rows:
        pl.semaphore_signal(
            barrier, inc=1, device_id={"row": row}, device_id_type=pl.DeviceIdType.MESH
        )
    for source in sources:
        pl.semaphore_signal(
            barrier, inc=1, device_id={"src": source}, device_id_type=pl.DeviceIdType.MESH
        )
    pl.semaphore_wait(barrier, len(rows) + len(sources))


def gather_kernel(
    sources,
    re_ref,
    im_ref,
    cent_row_ref,
    cent_col_ref,
    weight_row_ref,
    spec_ref,
    cents_ref,
    weights_ref,
    cent_ref,
    weight_ref,
    local_sem,
    send_sem,
    recv_sem,
    point_send_sem,
    point_recv_sem,
):
    row, core, x, y, mate, across_x, across_y = row_place()
    corner = across_x + across_y - row
    mate_step = mate - row
    rows_dev = re_ref.shape[0]
    own = lax.axis_index("src")
    peers = [(own + step) % sources for step in range(1, sources)]
    points_dev = weight_row_ref.shape[1]
    cent_ref[...] = jnp.zeros_like(cent_ref)
    weight_ref[...] = jnp.zeros_like(weight_ref)
    cent_ref[0:1, 0:points_dev] = cent_row_ref[...]
    cent_ref[1:2, 0:points_dev] = cent_col_ref[...]
    weight_ref[0:1, 0:points_dev] = weight_row_ref[...]
    enter([mate, across_x, across_y], peers)

    parity = own % 2
    partner = own + 1 - 2 * parity
    few = rows_dev * 3 // 8
    most = rows_dev - few
    fetched = (few * parity, most)
    passed = (most * parity, few)
    missing = (most * (1 - parity), few)
    whole = (0, rows_dev)

    def rows_of(device, piece=whole):
        return pl.ds(pl.multiple_of(device * rows_dev + piece[0], 16), piece[1])

    keep = [
        pltpu.make_async_copy(re_ref, spec_ref.at[0, rows_of(row), :], local_sem.at[0]),
        pltpu.make_async_copy(im_ref, spec_ref.at[1, rows_of(row), :], local_sem.at[1]),
        pltpu.make_async_copy(cent_ref, cents_ref.at[own], local_sem.at[2]),
        pltpu.make_async_copy(weight_ref, weights_ref.at[own], local_sem.at[3]),
    ]
    for copy in keep:
        copy.start()
    small = []
    for index, peer in enumerate(peers):
        for kind, (source, target) in enumerate(
            [(cent_ref, cents_ref.at[own]), (weight_ref, weights_ref.at[own])]
        ):
            small.append(
                pltpu.make_async_remote_copy(
                    src_ref=source,
                    dst_ref=target,
                    send_sem=point_send_sem.at[kind, index],
                    recv_sem=point_recv_sem.at[kind, index],
                    device_id={"src": peer},
                    device_id_type=pl.DeviceIdType.MESH,
                )
            )
    sent = []

    def send(part, holder, piece, axis, to):
        target = spec_ref.at[part, rows_of(row if holder is None else holder, piece), :]
        source = target
        if holder is None:
            first = pl.multiple_of(piece[0], 16)
            source = (re_ref, im_ref)[part].at[pl.ds(first, piece[1]), :]
        index = len(sent)
        copy = pltpu.make_async_remote_copy(
            src_ref=source,
            dst_ref=target,
            send_sem=send_sem.at[index],
            recv_sem=recv_sem.at[index],
            device_id={axis: to},
            device_id_type=pl.DeviceIdType.MESH,
        )
        copy.start()
        sent.append(copy)
        return copy

    re_x = send(0, None, fetched, "row", across_x)
    im_y = send(1, None, fetched, "row", across_y)
    im_x = send(1, None, fetched, "row", across_x)
    re_y = send(0, None, fetched, "row", across_y)
    for copy in small:
        copy.start()
    late = [send(part, None, whole, "row", mate) for part in range(2)]
    partner_copies = []

    def pass_on(part, holder):
        partner_copies.append((send(part, holder, passed, "src", partner), part, holder))
        late.append(send(part, holder, fetched, "row", mate))

    re_x.wait_recv()
    re_corner = send(0, across_x, fetched, "row", across_y)
    pass_on(0, across_x)
    im_y.wait_recv()
    im_corner = send(1, across_y, fetched, "row", across_x)
    pass_on(1, across_y)
    im_x.wait_recv()
    pass_on(1, across_x)
    re_y.wait_recv()
    pass_on(0, across_y)
    re_corner.wait_recv()
    pass_on(0, corner)
    im_corner.wait_recv()
    pass_on(1, corner)
    for copy, part, holder in partner_copies:
        copy.wait_recv()
        late.append(send(part, holder, missing, "row", mate))
    for copy in late:
        copy.wait_recv()
    for copy in sent:
        copy.wait_send()
    for copy in small:
        copy.wait()
    for copy in keep:
        copy.wait()


def reduce_kernel(
    sources,
    part_ref,
    out_ref,
    plane,
    own_part,
    own_sem,
    mate_in,
    chip_sum,
    first_re_in,
    first_im_in,
    first_re,
    first_im,
    last_re_in,
    last_im_in,
    left_in,
    right_in,
    chain,
    final_in,
    send_sem,
    recv_sem,
    up_send,
    left_recv,
    right_recv,
    down_send,
    down_recv,
):
    row, core, x, y, mate, across_x, across_y = row_place()
    chunks = mate_in.shape[0]
    depth = mate_in.shape[-2]
    halves = chunks // part_ref.shape[1]
    own = lax.axis_index("src")
    root = sources // 2
    leaf = jnp.logical_or(own == 0, own == sources - 1)
    has_left = jnp.logical_and(own > 0, own <= root)
    has_right = jnp.logical_and(own >= root, own < sources - 1)
    peers = [(own + step) % sources for step in range(1, sources)]
    enter([mate, across_x, across_y], peers)

    @pl.when(jnp.logical_not(has_left))
    def _():
        left_in[...] = jnp.zeros_like(left_in)

    @pl.when(jnp.logical_not(has_right))
    def _():
        right_in[...] = jnp.zeros_like(right_in)

    def wide(value):
        return value.astype(jnp.float32)

    def row_copy(kind, chunk, source, target, to):
        return pltpu.make_async_remote_copy(
            src_ref=source,
            dst_ref=target,
            send_sem=send_sem.at[kind, chunk],
            recv_sem=recv_sem.at[kind, chunk],
            device_id={"row": to},
            device_id_type=pl.DeviceIdType.MESH,
        )

    pair, step_re, step_im, end_re, end_im = {}, {}, {}, {}, {}
    keep = {}
    for chunk in range(chunks):
        residue = chunk // halves
        rows = pl.ds(chunk % halves * depth, depth)
        pair[chunk] = row_copy(
            0, chunk, part_ref.at[:, residue, :, :, 1 - core, rows], mate_in.at[chunk], mate
        )
        keep[chunk] = pltpu.make_async_copy(
            part_ref.at[:, residue, :, :, core, rows], own_part.at[chunk], own_sem.at[chunk]
        )
    ahead = 3
    for chunk in range(ahead):
        pair[chunk].start()
        keep[chunk].start()

    def place(chunk, source):
        residue = chunk // halves
        first = residue + chunk % halves * depth * RADIX
        rows = pl.ds(first, depth, stride=RADIX)
        for part in range(2):
            for block in range(plane.shape[1]):
                plane[part, block, rows, :] = wide(
                    source[chunk, part, :, block * LANES : (block + 1) * LANES]
                )

    def add_pair(chunk):
        keep[chunk].wait()
        pair[chunk].wait_recv()
        if chunk + ahead < chunks:
            pair[chunk + ahead].start()
            keep[chunk + ahead].start()
        total = wide(own_part[chunk]) + wide(mate_in[chunk])
        chip_sum[chunk] = total.astype(chip_sum.dtype)
        step_re[chunk] = row_copy(
            1, chunk, chip_sum.at[chunk, 0, :, 1 - x], first_re_in.at[chunk], across_x
        )
        step_im[chunk] = row_copy(
            2, chunk, chip_sum.at[chunk, 1, 1 - y], first_im_in.at[chunk], across_y
        )
        step_re[chunk].start()
        step_im[chunk].start()

    def add_first(chunk):
        step_re[chunk].wait_recv()
        total = wide(chip_sum[chunk, 0, :, x]) + wide(first_re_in[chunk])
        first_re[chunk] = total.astype(first_re.dtype)
        end_re[chunk] = row_copy(
            3, chunk, first_re.at[chunk, 1 - y], last_re_in.at[chunk], across_y
        )
        end_re[chunk].start()
        step_im[chunk].wait_recv()
        total = wide(chip_sum[chunk, 1, y]) + wide(first_im_in[chunk])
        first_im[chunk] = total.astype(first_im.dtype)
        end_im[chunk] = row_copy(
            4, chunk, first_im.at[chunk, 1 - x], last_im_in.at[chunk], across_x
        )
        end_im[chunk].start()

    def src_copy(source, target, sent, received, to):
        return pltpu.make_async_remote_copy(
            src_ref=source,
            dst_ref=target,
            send_sem=sent,
            recv_sem=received,
            device_id={"src": to},
            device_id_type=pl.DeviceIdType.MESH,
        )

    after = jnp.minimum(own + 1, sources - 1)
    before = jnp.maximum(own - 1, 0)

    def to_right(chunk):
        return src_copy(
            chain.at[chunk], left_in.at[chunk], up_send.at[chunk], left_recv.at[chunk], after
        )

    def to_left(chunk):
        return src_copy(
            chain.at[chunk], right_in.at[chunk], up_send.at[chunk], right_recv.at[chunk], before
        )

    def down_left(chunk, source):
        return src_copy(
            source.at[chunk],
            final_in.at[chunk],
            down_send.at[0, chunk],
            down_recv.at[chunk],
            before,
        )

    def down_right(chunk, source):
        return src_copy(
            source.at[chunk],
            final_in.at[chunk],
            down_send.at[1, chunk],
            down_recv.at[chunk],
            after,
        )

    def add_last(chunk):
        end_re[chunk].wait_recv()
        end_im[chunk].wait_recv()

        @pl.when(has_left)
        def _():
            to_right(chunk).wait_recv()

        @pl.when(has_right)
        def _():
            to_left(chunk).wait_recv()

        real = wide(first_re[chunk, y]) + wide(last_re_in[chunk])
        imag = wide(first_im[chunk, x]) + wide(last_im_in[chunk])
        for part, total in enumerate((real, imag)):
            total = total + wide(left_in[chunk, part]) + wide(right_in[chunk, part])
            chain[chunk, part] = total.astype(chain.dtype)

        @pl.when(own < root)
        def _():
            to_right(chunk).start()

        @pl.when(own > root)
        def _():
            to_left(chunk).start()

        @pl.when(own == root)
        def _():
            if root > 0:
                down_left(chunk, chain).start()
            if root < sources - 1:
                down_right(chunk, chain).start()
            place(chunk, chain)

    def pass_final(chunk):
        @pl.when(jnp.logical_and(own < root, own > 0))
        def _():
            down_left(chunk, final_in).wait_recv()
            down_left(chunk, final_in).start()
            place(chunk, final_in)

        @pl.when(jnp.logical_and(own > root, own < sources - 1))
        def _():
            down_right(chunk, final_in).wait_recv()
            down_right(chunk, final_in).start()
            place(chunk, final_in)

    stages = ((add_pair, 0), (add_first, 2), (add_last, 4), (pass_final, 7))
    for time in range(chunks + 7):
        for stage, lag in stages:
            if 0 <= time - lag < chunks:
                stage(time - lag)
    for chunk in range(chunks):

        @pl.when(jnp.logical_and(leaf, own != root))
        def _():
            down_left(chunk, final_in).wait_recv()
            place(chunk, final_in)

    for part in range(2):
        for block in range(plane.shape[1]):
            cols = slice(block * LANES, (block + 1) * LANES)
            out_ref[part, :, cols] = plane[part, block].astype(out_ref.dtype)

    for chunk in range(chunks):
        for group in (pair, step_re, step_im, end_re, end_im):
            group[chunk].wait_send()

        @pl.when(own < root)
        def _():
            to_right(chunk).wait_send()

            @pl.when(own > 0)
            def _():
                down_left(chunk, final_in).wait_send()

        @pl.when(own > root)
        def _():
            to_left(chunk).wait_send()

            @pl.when(own < sources - 1)
            def _():
                down_right(chunk, final_in).wait_send()

        @pl.when(own == root)
        def _():
            if root > 0:
                down_left(chunk, chain).wait_send()
            if root < sources - 1:
                down_right(chunk, chain).wait_send()


def gather_all(spec_re, spec_im, cent_row, cent_col, weights, sources, kernels):
    rows_dev, band = spec_re.shape
    points_dev = weights.shape[0]
    if not kernels:
        pad = ((0, 6), (0, LANES - points_dev))
        cents = jnp.pad(jnp.stack([cent_row, cent_col], axis=0), pad)
        weights = jnp.pad(jnp.stack([weights, weights], axis=0), pad)
        spectrum = lax.all_gather(jnp.stack([spec_re, spec_im]), "row", axis=1, tiled=True)
        return spectrum, lax.all_gather(cents, "src"), lax.all_gather(weights, "src")
    tile = (8, LANES)
    hbm = pl.BlockSpec(memory_space=pl.ANY)
    vmem = pl.BlockSpec(memory_space=pltpu.VMEM)
    dma = pltpu.SemaphoreType.DMA
    return pl.pallas_call(
        functools.partial(gather_kernel, sources),
        out_shape=(
            jax.ShapeDtypeStruct((2, rows_dev * lax.axis_size("row"), band), spec_re.dtype),
            jax.ShapeDtypeStruct((sources,) + tile, cent_row.dtype),
            jax.ShapeDtypeStruct((sources,) + tile, weights.dtype),
        ),
        in_specs=[hbm, hbm, vmem, vmem, vmem],
        out_specs=(hbm, vmem, vmem),
        scratch_shapes=[
            pltpu.VMEM(tile, cent_row.dtype),
            pltpu.VMEM(tile, weights.dtype),
            dma((4,)),
            dma((26,)),
            dma((26,)),
            dma((2, max(sources - 1, 1))),
            dma((2, max(sources - 1, 1))),
        ],
        compiler_params=pltpu.CompilerParams(collective_id=0, has_side_effects=True),
    )(spec_re, spec_im, cent_row[None], cent_col[None], weights[None])


def reduce_all(partial, sources, kernels):
    _, residues, quarter, band = partial.shape
    own = quarter // lax.axis_size("row")
    rows_dev = own * residues
    if not kernels:
        summed = lax.psum_scatter(partial, "row", scatter_dimension=2, tiled=True)
        summed = lax.psum(summed, "src").astype(jnp.float32)
        summed = summed.transpose(0, 2, 1, 3).reshape(2, rows_dev, band)
        return summed[0], summed[1]
    halves = 2
    chunks = residues * halves
    partial = partial.reshape(2, residues, 2, 2, 2, own, band)
    vmem = pl.BlockSpec(memory_space=pltpu.VMEM)
    dma = pltpu.SemaphoreType.DMA

    def buffer(*lead):
        return pltpu.VMEM((chunks,) + lead + (own // halves, band), partial.dtype)

    summed = pl.pallas_call(
        functools.partial(reduce_kernel, sources),
        out_shape=jax.ShapeDtypeStruct((2, rows_dev, band), partial.dtype),
        in_specs=[pl.BlockSpec(memory_space=pl.ANY)],
        out_specs=vmem,
        scratch_shapes=[
            pltpu.VMEM((2, band // LANES, rows_dev, LANES), jnp.float32),
            buffer(2, 2, 2),
            dma((chunks,)),
            buffer(2, 2, 2),
            buffer(2, 2, 2),
            buffer(2),
            buffer(2),
            buffer(2),
            buffer(2),
            buffer(),
            buffer(),
            buffer(2),
            buffer(2),
            buffer(2),
            buffer(2),
            dma((5, chunks)),
            dma((5, chunks)),
            dma((chunks,)),
            dma((chunks,)),
            dma((chunks,)),
            dma((2, chunks)),
            dma((chunks,)),
        ],
        compiler_params=pltpu.CompilerParams(
            collective_id=1, has_side_effects=True, vmem_limit_bytes=61 * 1024 * 1024
        ),
    )(partial)
    return summed[0].astype(jnp.float32), summed[1].astype(jnp.float32)


def local(spec_re, spec_im, target, weights, cent_row, cent_col):
    rows_dev, band = spec_re.shape
    groups_src = lax.axis_size("src")
    points_dev = weights.shape[0]
    total_points = points_dev * groups_src
    own_rows = target.shape[0] // groups_src
    slots = LANES // own_rows
    groups = total_points // slots
    quarter = band // RADIX
    cosine, sine = host_tables(band)

    kernels = lax.axis_size("row") == 8 and groups_src % 2 == 0 and rows_dev % LANES == 0
    spectrum, cents_all, weights_all = gather_all(
        spec_re, spec_im, cent_row, cent_col, weights, groups_src, kernels
    )

    cos_own, sin_own, target_own = jnp.asarray(cosine), jnp.asarray(sine), target
    if own_rows % 16:
        first_own = lax.axis_index("src") * own_rows
        first_row = lax.axis_index("row") * target.shape[0] + first_own
        cos_own = lax.dynamic_slice_in_dim(cos_own, first_row, own_rows, 0)
        sin_own = lax.dynamic_slice_in_dim(sin_own, first_row, own_rows, 0)
        cos_own = jnp.tile(cos_own, (slots, 1))
        sin_own = jnp.tile(sin_own, (slots, 1))
        target_own = lax.dynamic_slice_in_dim(target, first_own, own_rows, 0)
        target_own = jnp.tile(target_own, (slots, 1)).T
    cos_split = cosine[:quarter].reshape(quarter, quarter, RADIX).transpose(2, 0, 1)
    sin_split = sine[:quarter].reshape(quarter, quarter, RADIX).transpose(2, 0, 1)
    wide = jnp.asarray(np.concatenate([cos_split, sin_split], axis=2))
    back = jnp.asarray(
        np.concatenate([cos_split.transpose(0, 2, 1), sin_split.transpose(0, 2, 1)], axis=2)
    )

    vmem = pl.BlockSpec(memory_space=pltpu.VMEM)
    hbm = pl.BlockSpec(memory_space=pl.ANY)
    table = vmem if own_rows % 16 else hbm
    smem = pl.BlockSpec(memory_space=pltpu.SMEM)
    lanes_all = 2 * own_rows * total_points
    partial = pl.pallas_call(
        functools.partial(main_kernel, total_points, own_rows),
        out_shape=jax.ShapeDtypeStruct((2, RADIX, quarter, band), jnp.bfloat16),
        in_specs=[smem, smem, hbm, table, table, hbm, hbm, vmem],
        out_specs=hbm,
        scratch_shapes=[
            pltpu.VMEM(spectrum.shape, spectrum.dtype),
            pltpu.VMEM(wide.shape, wide.dtype),
            pltpu.VMEM(back.shape, back.dtype),
            pltpu.VMEM((2, RADIX, quarter, band), jnp.bfloat16),
            pltpu.SemaphoreType.DMA((3,)),
            pltpu.SemaphoreType.DMA((2, RADIX)),
            pltpu.VMEM((RADIX, quarter, lanes_all), jnp.bfloat16),
            pltpu.VMEM((RADIX, quarter, lanes_all), jnp.float32),
            pltpu.VMEM((RADIX, quarter, lanes_all), jnp.bfloat16),
            pltpu.VMEM((RADIX, quarter, LANES), jnp.float32),
            pltpu.VMEM((2, RADIX, quarter, band), jnp.float32),
            pltpu.VMEM((4, 2, RADIX * WIN_Q, LANES), jnp.float32),
            pltpu.VMEM((groups, 1, LANES), jnp.float32),
            pltpu.VMEM((2, 2 * LANES, band), jnp.bfloat16),
            pltpu.VMEM((2, band, 2 * LANES), jnp.bfloat16),
            pltpu.VMEM((RADIX, quarter, LANES), jnp.float32),
            pltpu.VMEM((2, max(own_rows, 16), band), jnp.bfloat16),
            pltpu.SemaphoreType.DMA((2,)),
        ],
        compiler_params=pltpu.CompilerParams(vmem_limit_bytes=56 * 1024 * 1024),
    )(cents_all, weights_all, spectrum, cos_own, sin_own, wide, back, target_own)

    return reduce_all(partial, groups_src, kernels)


def solution(mesh):
    return jax.shard_map(
        local,
        mesh=mesh,
        in_specs=(P("row", None), P("row", None), P("row", None), P("src"), P("src"), P("src")),
        out_specs=(P("row", None), P("row", None)),
        check_vma=False,
    )
```
